32 devices in a mesh: section: 2 (over x), rows: 16 (over z, y, core).
Axes of the slice: x: 2, y: 2, z: 4, core: 2. Of those that a mesh axis runs over, the one named last changes fastest.
Arguments:
- section_input: bfloat16 [2, 2, 2048, 512], P('section', None, 'rows'), may hold values from -6 to 6
- segments: int32 [2, 2, 16, 128], P(None, None, 'rows'), may hold values from 0 to 7, never falling along the last dimension, each value on 1 to 32 neighbouring positions
- cotangent: bfloat16 [2, 2048, 512], P(None, 'rows'), may hold values from -6 to 6
- encoder_inward: bfloat16 [512, 1536], replicated, may hold values from -0.25 to 0.25
- encoder_outward: bfloat16 [512, 512], replicated, may hold values from -0.75 to 0.75
- encoder_widen: bfloat16 [512, 2048], replicated, may hold values from -0.25 to 0.25
- encoder_narrow: bfloat16 [2048, 512], replicated, may hold values from -0.125 to 0.125
- encoder_gain: float32 [2, 512], replicated, may hold values from 0.25 to 1.75
- encoder_shift: float32 [2, 512], replicated, may hold values from -3 to 3
- decoder_inward: bfloat16 [512, 1536], replicated, may hold values from -0.25 to 0.25
- decoder_outward: bfloat16 [512, 512], replicated, may hold values from -0.75 to 0.75
- decoder_cross_query: bfloat16 [512, 512], replicated, may hold values from -0.25 to 0.25
- decoder_cross_memory: bfloat16 [512, 1024], replicated, may hold values from -0.25 to 0.25
- decoder_cross_outward: bfloat16 [512, 512], replicated, may hold values from -0.75 to 0.75
- decoder_widen: bfloat16 [512, 2048], replicated, may hold values from -0.25 to 0.25
- decoder_narrow: bfloat16 [2048, 512], replicated, may hold values from -0.125 to 0.125
- decoder_gain: float32 [3, 512], replicated, may hold values from 0.25 to 1.75
- decoder_shift: float32 [3, 512], replicated, may hold values from -3 to 3
Outputs:
- section_output: bfloat16 [2, 2, 2048, 512], P('section', None, 'rows')
- input_delta: bfloat16 [2, 2, 2048, 512], P('section', None, 'rows')
- encoder_inward_delta: float32 [512, 1536], P('rows', 'section')
- encoder_outward_delta: float32 [512, 512], P('rows', 'section')
- encoder_widen_delta: float32 [512, 2048], P('rows', 'section')
- encoder_narrow_delta: float32 [2048, 512], P('rows', 'section')
- encoder_gain_delta: float32 [2, 512], P(None, 'rows')
- encoder_shift_delta: float32 [2, 512], P(None, 'rows')
- decoder_inward_delta: float32 [512, 1536], P('rows', 'section')
- decoder_outward_delta: float32 [512, 512], P('rows', 'section')
- decoder_cross_query_delta: float32 [512, 512], P('rows', 'section')
- decoder_cross_memory_delta: float32 [512, 1024], P('rows', 'section')
- decoder_cross_outward_delta: float32 [512, 512], P('rows', 'section')
- decoder_widen_delta: float32 [512, 2048], P('rows', 'section')
- decoder_narrow_delta: float32 [2048, 512], P('rows', 'section')
- decoder_gain_delta: float32 [3, 512], P(None, 'rows')
- decoder_shift_delta: float32 [3, 512], P(None, 'rows')
The draws below stay inside these ranges and needn't reach their ends.
Inputs may be any that keep to these rules, and one draw needn't show every extreme that they name: `segments`: in every row of 128 tokens the ids never fall, each id of 0 to 7 appears, and each covers at most 32 positions, one exactly that many.
All inputs are finite; a program needn't handle non-finite values.
Results may differ from the reference program's by a relative error of at most 0.02.
Values may be sent and summed in bfloat16 or wider, within the bound.
No kernel may reach another device: no remote copies, remote signals or barrier semaphores. Data moves between devices by JAX's collectives and lax.ppermute only.
A program may use at most 320 MiB of HBM per device.

```python
import math
import jax
import jax.numpy as jnp
import numpy as np
from jax import lax

D = 512
FF = 2048
HEADS = 8
HEAD_DIM = 64
LEN = 128
MB = 2
SEGS = 8
BATCH = 16
TOKENS = 2048


def with_spikes(entries, key, source, target, blocks, factor):
    def block_of(axis_at):
        return (jnp.arange(entries.shape[axis_at]) // (entries.shape[axis_at] // blocks)).reshape((-1,) + (1,) * (entries.ndim - 1 - axis_at))

    near = jax.random.permutation(key, blocks)[block_of(target)]
    second = (block_of(target) + blocks // 2) % blocks
    return jnp.where((block_of(source) == near) | (block_of(source) == second), factor * entries, entries)


def level_of(rng, shape, cuts, least, high):
    level = 1.0
    for axis_at, shards_of in cuts:
        steps = jax.random.uniform(jax.random.fold_in(jax.random.fold_in(rng, 6), axis_at), (shards_of,), jnp.float32, least / len(cuts), high / len(cuts))
        level = level * jnp.repeat(jnp.exp(steps), shape[axis_at] // shards_of).reshape((-1,) + (1,) * (len(shape) - 1 - axis_at))
    return level


def length_profile(number_of, total, reach, slope):
    loads = [(1 << 20) // math.isqrt(grade ** slope) + 1 for grade in range(2, number_of + 1)]
    surplus, holding = total - reach - (number_of - 1), [1] * (number_of - 1)
    while surplus > 0:
        candidates = [i for i in range(number_of - 1) if holding[i] < reach]
        whole, remaining = sum([loads[i] for i in candidates]), surplus
        for i in candidates:
            extra = min(reach - holding[i], max(1, remaining * loads[i] // whole), surplus)
            holding[i] = holding[i] + extra
            surplus = surplus - extra
    return np.array([reach] + holding)


def uneven_parts(rng, count, total, most, skew):
    if count == 2:
        one = jax.random.randint(rng, (), max(1, total - most), min(most, total - 1) + 1)
        return jnp.stack([one, total - one])
    sizes = jnp.asarray(length_profile(count, total, most, skew), jnp.int32)
    twos = (count - 1) // 2
    giver, receiver = sizes[1:1 + 2 * twos:2], sizes[2:2 + 2 * twos:2]
    slack = jnp.minimum(giver - 1, most - receiver)
    moved = jax.random.randint(jax.random.fold_in(rng, 1), (twos,), 0, 1 << 20) % (slack + 1)
    sizes = sizes.at[1:1 + 2 * twos:2].set(giver - moved).at[2:2 + 2 * twos:2].set(receiver + moved)
    return sizes[jax.random.permutation(jax.random.fold_in(rng, 2), count)]


def scatter_about(stream_key, extent, deviation, bound, shards=(), held_as=jnp.bfloat16):
    values = deviation * jax.random.normal(stream_key, extent, jnp.float32)
    if shards:
        values = values * level_of(stream_key, extent, shards, -0.22, 0.18)
    return jnp.clip(values, -bound, bound).astype(held_as)


def bell_draw_with(stream_key, extent, scale, most, shards, heavy, dtype=jnp.bfloat16):
    entries = scale * jax.random.normal(stream_key, extent, jnp.float32)
    if shards:
        entries = entries * level_of(stream_key, extent, shards, -0.22, 0.18)
    return jnp.clip(with_spikes(entries, jax.random.fold_in(stream_key, 3), *heavy), -most, most).astype(dtype)


def setup_inputs(seed: int = 0) -> dict:
    key_of = jax.random.split(jax.random.key(seed), 19)
    return {
        "section_input": scatter_about(key_of[0], (2, MB, TOKENS, D), 1.0, 6.0, ((0, 2), (2, 16))),
        "segments": jax.vmap(lambda own: jnp.searchsorted(jnp.cumsum(uneven_parts(own, SEGS, LEN, LEN // 4, 1)), jnp.arange(LEN), side="right"))(jax.random.split(key_of[1], 2 * MB * BATCH)).reshape((2, MB, BATCH, LEN)).astype(jnp.int32),
        "cotangent": bell_draw_with(key_of[2], (MB, TOKENS, D), 1.0, 6.0, ((1, 16),), (1, 2, 16, 2.0)),
        "encoder_inward": scatter_about(key_of[3], (D, 3 * D), D ** -0.5, 0.25),
        "encoder_outward": scatter_about(key_of[4], (D, D), (D // 8) ** -0.5, 0.75),
        "encoder_widen": scatter_about(key_of[5], (D, FF), D ** -0.5, 0.25),
        "encoder_narrow": scatter_about(key_of[6], (FF, D), FF ** -0.5, 0.125),
        "encoder_gain": jnp.clip(1.0 + 0.15 * jax.random.normal(key_of[7], (2, D), jnp.float32), 0.25, 1.75),
        "encoder_shift": scatter_about(key_of[8], (2, D), 0.3, 3.0, (), jnp.float32),
        "decoder_inward": scatter_about(key_of[9], (D, 3 * D), D ** -0.5, 0.25),
        "decoder_outward": scatter_about(key_of[10], (D, D), (D // 8) ** -0.5, 0.75),
        "decoder_cross_query": scatter_about(key_of[11], (D, D), D ** -0.5, 0.25),
        "decoder_cross_memory": scatter_about(key_of[12], (D, 2 * D), D ** -0.5, 0.25),
        "decoder_cross_outward": scatter_about(key_of[13], (D, D), (D // 8) ** -0.5, 0.75),
        "decoder_widen": scatter_about(key_of[14], (D, FF), D ** -0.5, 0.25),
        "decoder_narrow": scatter_about(key_of[15], (FF, D), FF ** -0.5, 0.125),
        "decoder_gain": jnp.clip(1.0 + 0.15 * jax.random.normal(key_of[16], (3, D), jnp.float32), 0.25, 1.75),
        "decoder_shift": scatter_about(key_of[17], (3, D), 0.3, 3.0, (), jnp.float32),
    }


@jax.custom_vjp
def low(v):
    return lax.optimization_barrier(v.astype(jnp.bfloat16)).astype(jnp.float32)

@jax.custom_vjp
def low_back(v):
    return v

def low_keep(v):
    return (low(v), None)

def low_pass(kept, grad):
    return (grad,)

def back_keep(v):
    return (v, None)

def back_low(kept, grad):
    return (low(grad),)
low.defvjp(low_keep, low_pass)
low_back.defvjp(back_keep, back_low)
NEG = -1e+30
EPS = 1e-05
EXACT = lax.Precision.HIGHEST

def product(left, right):
    return jnp.dot(left, right, precision=EXACT)

def layer_norm(summed, gain, shift):
    center = lax.optimization_barrier(jnp.mean(summed, -1, keepdims=True))
    centered = summed - center
    spread = lax.optimization_barrier(jnp.mean(centered * centered, -1, keepdims=True))
    return centered * lax.rsqrt(spread + EPS) * gain + shift

def split_heads(array):
    return array.reshape(array.shape[0], HEADS, HEAD_DIM)

def attend(query, keys, values, allowed):
    factor = 1.0 / math.sqrt(HEAD_DIM)
    raw_scores = jnp.einsum('qhd,khd->hqk', split_heads(query), split_heads(keys), precision=EXACT) * factor
    scores = low_back(jnp.where(allowed[None], raw_scores, NEG))
    peak = lax.optimization_barrier(jnp.max(scores, -1, keepdims=True))
    weights = jnp.exp(scores - peak)
    chances = low(weights / lax.optimization_barrier(jnp.sum(weights, -1, keepdims=True)))
    mixed = jnp.einsum('hqk,khd->qhd', chances, split_heads(values), precision=EXACT)
    return low_back(low(mixed.reshape(query.shape[0], -1)))

def self_attention(inputs, allowed, inward, outward):
    width = outward.shape[0]
    projected = low_back(low(product(inputs, inward)))
    mixed = attend(projected[:, :width], projected[:, width:2 * width], projected[:, 2 * width:], allowed)
    return inputs + low_back(product(mixed, outward))

def feed_forward(normed, widen, narrow):
    hidden = low(jax.nn.gelu(low_back(product(low(normed), widen)), approximate=True))
    return normed + low_back(product(hidden, narrow))

def encoder_layer(weights, source, source_ids):
    inward, outward, widen, narrow, gains, shifts = weights[:6]
    allowed = source_ids[:, None] == source_ids[None, :]
    normed = layer_norm(self_attention(source, allowed, inward, outward), gains[0], shifts[0])
    return low_back(low(layer_norm(feed_forward(normed, widen, narrow), gains[1], shifts[1])))

def decoder_layer(weights, target, memory, source_ids, target_ids):
    inward, outward, cross_query, cross_memory, cross_outward, widen, narrow, gains, shifts = weights[6:]
    places = jnp.arange(target.shape[0])
    causal = (target_ids[:, None] == target_ids[None, :]) & (places[:, None] >= places[None, :])
    across = target_ids[:, None] == source_ids[None, :]
    normed = layer_norm(self_attention(target, causal, inward, outward), gains[0], shifts[0])
    width = cross_outward.shape[0]
    query = low_back(low(product(low(normed), cross_query)))
    paired = low_back(low(product(memory, cross_memory)))
    mixed = attend(query, paired[:, :width], paired[:, width:], across)
    normed = layer_norm(normed + low_back(product(mixed, cross_outward)), gains[1], shifts[1])
    return layer_norm(feed_forward(normed, widen, narrow), gains[2], shifts[2])

def row_pass(weights, source, target, source_ids, target_ids):
    memory = encoder_layer(weights, source, source_ids)
    return (memory, decoder_layer(weights, target, memory, source_ids, target_ids))

def reference(section_input, segments, cotangent, encoder_inward, encoder_outward, encoder_widen, encoder_narrow, encoder_gain, encoder_shift, decoder_inward, decoder_outward, decoder_cross_query, decoder_cross_memory, decoder_cross_outward, decoder_widen, decoder_narrow, decoder_gain, decoder_shift):
    weights = tuple((item.astype(jnp.float32) for item in (encoder_inward, encoder_outward, encoder_widen, encoder_narrow, encoder_gain, encoder_shift, decoder_inward, decoder_outward, decoder_cross_query, decoder_cross_memory, decoder_cross_outward, decoder_widen, decoder_narrow, decoder_gain, decoder_shift)))
    rows_all = MB * BATCH
    group = math.gcd(rows_all, max(1, 4096 // LEN))
    steps = rows_all // group
    source = section_input[0].astype(jnp.float32).reshape(steps, group, LEN, D)
    target = section_input[1].astype(jnp.float32).reshape(steps, group, LEN, D)
    source_ids = segments[0].reshape(steps, group, LEN)
    target_ids = segments[1].reshape(steps, group, LEN)
    grad_out = cotangent.astype(jnp.float32).reshape(steps, group, LEN, D)

    def step(totals, block):
        block_source, block_target, block_source_ids, block_target_ids, block_grad = block

        def group_pass(weights_in, source_in, target_in):
            return jax.vmap(row_pass, in_axes=(None, 0, 0, 0, 0))(weights_in, source_in, target_in, block_source_ids, block_target_ids)
        (memory, output), backward = jax.vjp(group_pass, weights, block_source, block_target)
        weight_grads, source_grad, target_grad = backward((jnp.zeros_like(memory), block_grad))
        return (jax.tree.map(jnp.add, totals, weight_grads), (memory, output, source_grad, target_grad))
    totals, (memory, output, source_grad, target_grad) = lax.scan(step, jax.tree.map(jnp.zeros_like, weights), (source, target, source_ids, target_ids, grad_out))
    shape_out = (MB, BATCH * LEN, D)
    results = jnp.stack([memory.reshape(shape_out), output.reshape(shape_out)]).astype(jnp.bfloat16)
    gradients = jnp.stack([source_grad.reshape(shape_out), target_grad.reshape(shape_out)]).astype(jnp.bfloat16)
    return (results, gradients, totals[0], totals[1], totals[2], totals[3], totals[4], totals[5], totals[6], totals[7], totals[8], totals[9], totals[10], totals[11], totals[12], totals[13], totals[14])
```

```python
from functools import partial
import math

import jax
import jax.numpy as jnp
from jax import lax
from jax.experimental import pallas as pl
from jax.experimental.pallas import tpu as pltpu
from jax.sharding import PartitionSpec as P

HEADS = 8
HEAD_DIM = 64
NEG = -1e30
EPS = 1e-05
GROUPS = 16
SLAB = 256
LANES = 128
PER_SLAB = SLAB // HEAD_DIM
BF = jnp.bfloat16
F32 = jnp.float32
FACTOR = 1.0 / math.sqrt(HEAD_DIM)
VMEM_LIMIT = 56 * 1024 * 1024
ANY = pl.BlockSpec(memory_space=pl.ANY)


def matmul(left, right):
    return lax.dot_general(left, right, (((1,), (0,)), ((), ())), preferred_element_type=F32)


def matmul_back(grad, weight):
    return lax.dot_general(grad, weight, (((1,), (1,)), ((), ())), preferred_element_type=F32)


def matmul_across(left, grad):
    return lax.dot_general(left, grad, (((0,), (0,)), ((), ())), preferred_element_type=F32)


def norm(summed, gain, shift):
    center = jnp.mean(summed, -1, keepdims=True)
    centered = summed - center
    spread = jnp.mean(centered * centered, -1, keepdims=True)
    scale = lax.rsqrt(spread + EPS)
    unit = centered * scale
    return unit * gain + shift, unit, scale


def norm_back(grad, unit, scale, gain):
    grad_gain = jnp.sum(grad * unit, 0, keepdims=True)
    grad_shift = jnp.sum(grad, 0, keepdims=True)
    inner = grad * gain
    center = jnp.mean(inner, -1, keepdims=True)
    along = jnp.mean(inner * unit, -1, keepdims=True)
    return scale * (inner - center - unit * along), grad_gain, grad_shift


def gelu_both(before):
    root = math.sqrt(2.0 / math.pi)
    square = before * before
    bent = jnp.tanh(root * before * (1.0 + 0.044715 * square))
    half = 0.5 * (1.0 + bent)
    slope = half + 0.5 * before * (1.0 - bent * bent) * (root * (1.0 + 3 * 0.044715 * square))
    return before * half, slope


def head_marks(dtype):
    lane = lax.broadcasted_iota(jnp.int32, (1, SLAB), 1) // HEAD_DIM
    return [(lane == h).astype(F32).astype(dtype) for h in range(PER_SLAB)]


def spread_heads(slab, marks):
    return jnp.concatenate([slab * mark for mark in marks], 0)


def gather_heads(stacked, rows):
    lane = lax.broadcasted_iota(jnp.int32, (1, SLAB), 1) // HEAD_DIM
    total = stacked[:rows]
    for h in range(1, PER_SLAB):
        total = jnp.where(lane == h, stacked[h * rows : (h + 1) * rows], total)
    return total


def attend(query, keys, values, allowed, chances_ref):
    rows = query.shape[0]
    marks = head_marks(BF)
    wide = jnp.concatenate([allowed] * PER_SLAB, 0)
    mixed = []
    for slab in range(query.shape[1] // SLAB):
        at = slice(slab * SLAB, (slab + 1) * SLAB)
        scores = matmul_back(spread_heads(query[:, at], marks), keys[:, at]) * FACTOR
        scores = jnp.where(wide, scores, NEG)
        weights = jnp.exp(scores - jnp.max(scores, -1, keepdims=True))
        chances = weights * (1.0 / jnp.sum(weights, -1, keepdims=True))
        chances_ref[slab] = chances
        mixed.append(gather_heads(matmul(chances.astype(BF), values[:, at]), rows).astype(BF))
    return jnp.concatenate(mixed, 1)


def attend_back(query, keys, values, chances_ref, grad_mixed):
    rows = query.shape[0]
    marks = head_marks(BF)
    grad_query, grad_keys, grad_values = [], [], []
    for slab in range(query.shape[1] // SLAB):
        at = slice(slab * SLAB, (slab + 1) * SLAB)
        chances = chances_ref[slab]
        spread_grad = spread_heads(grad_mixed[:, at], marks)
        grad_chances = matmul_back(spread_grad, values[:, at])
        grad_values.append(matmul_across(chances.astype(BF), spread_grad).astype(BF))
        held = jnp.sum(chances * grad_chances, -1, keepdims=True)
        grad_scores = (chances * (grad_chances - held)).astype(BF)
        grad_query.append((gather_heads(matmul(grad_scores, keys[:, at]), rows) * FACTOR).astype(BF))
        spread_query = spread_heads(query[:, at], marks)
        grad_keys.append((matmul_across(grad_scores, spread_query) * FACTOR).astype(BF))
    return [jnp.concatenate(item, 1) for item in (grad_query, grad_keys, grad_values)]


def tiles_of(array):
    return [array[:, at : at + LANES] for at in range(0, array.shape[1], LANES)]


class Room:
    def __init__(self, sources, targets, held_in, held_out, sem_in, sem_out):
        self.sources, self.targets = sources, targets
        self.held_in, self.held_out = held_in, held_out
        self.sem_in, self.sem_out = sem_in, sem_out
        self.arrived, self.sent = set(), []
        self.names_in, self.names_out = list(sources), list(targets)

    def copy_in(self, name, source=None):
        place = self.names_in.index(name)
        source = self.sources[name] if source is None else source
        return pltpu.make_async_copy(source, self.held_in[name], self.sem_in.at[place])

    def fetch(self, names):
        for name in names:
            self.copy_in(name).start()

    def get(self, name):
        if name not in self.arrived:
            source = self.sources[name]
            if source.shape != self.held_in[name].shape:
                source = source.at[0]
            self.copy_in(name, source).wait()
            self.arrived.add(name)
        return self.held_in[name]

    def put(self, name, value=None):
        if value is not None:
            self.held_out[name][...] = value
        place = self.names_out.index(name)
        copy = pltpu.make_async_copy(
            self.held_out[name], self.targets[name], self.sem_out.at[place]
        )
        copy.start()
        self.sent.append(copy)

    def finish(self):
        for copy in self.sent:
            copy.wait()


class Packet:
    def __init__(self, weights, extra=0):
        self.weights = dict(weights)
        self.left_at, self.grad_at = {}, {}
        left = grad = 0
        for name, (depth, width) in self.weights.items():
            self.left_at[name], self.grad_at[name] = left, grad
            left, grad = left + depth // 2, grad + width
        self.left, self.extra_at, self.grad = left, grad, grad + extra
        self.rows = {}
        top = 0
        for name, (depth, width) in self.weights.items():
            self.rows[name] = top
            top += depth // GROUPS * width // (2 * SLAB)
        self.small_at = top
        self.height = top + (16 if extra else 0)

    def shapes(self):
        return {
            "keep": jax.ShapeDtypeStruct((self.left, LANES), BF),
            "send": jax.ShapeDtypeStruct((self.left + self.grad, LANES), BF),
        }

    def scratch(self):
        return {
            "left": jax.ShapeDtypeStruct((2, self.left, LANES), BF),
            "grad": jax.ShapeDtypeStruct((self.grad, LANES), BF),
        }

    def stash(self, refs, name, left, grad):
        depth, width = self.weights[name]
        block = depth // GROUPS
        across = left.T
        for group in range(GROUPS):
            top = self.left_at[name] + group // 2 * block
            refs["left"][group % 2, top : top + block] = across[group * block : (group + 1) * block]
        for place, tile in enumerate(tiles_of(grad)):
            top = self.grad_at[name] + place * LANES
            refs["grad"][top : top + LANES] = tile

    def ship(self, refs, targets, sems, core):
        copies = [
            pltpu.make_async_copy(refs["left"].at[core], targets["keep"], sems.at[0]),
            pltpu.make_async_copy(
                refs["left"].at[1 - core], targets["send"].at[pl.ds(0, self.left)], sems.at[1]
            ),
            pltpu.make_async_copy(
                refs["grad"], targets["send"].at[pl.ds(self.left, self.grad)], sems.at[2]
            ),
        ]
        for copy in copies:
            copy.start()
        return copies


def call(body, inputs, outputs, scalars, flops, packets=None, single=(), extra=None):
    packets, extra = packets or {}, extra or {}
    outputs = dict(outputs)
    names_in, names_out = list(inputs), list(outputs)
    ways = [(name, way) for name in packets for way in ("keep", "send")]
    shapes_out = [outputs[name] for name in names_out]
    shapes_out += [packets[name].shapes()[way] for name, way in ways]
    stashes = [(name, part) for name in packets for part in ("left", "grad")]

    def kernel(*refs):
        refs = list(refs)
        scalar_ref = refs.pop(0)
        sources = {name: refs.pop(0) for name in names_in}
        targets = {name: refs.pop(0) for name in names_out}
        leaving = {key: refs.pop(0) for key in ways}
        held_in = {name: refs.pop(0) for name in names_in}
        held_out = {name: refs.pop(0) for name in names_out}
        stashed = {key: refs.pop(0) for key in stashes}
        held_out.update({name: refs.pop(0) for name in extra})
        sem_in, sem_out, sem_packet = refs
        room = Room(sources, targets, held_in, held_out, sem_in, sem_out)

        def stash(packet, name, left, grad):
            refs_here = {part: stashed[packet, part] for part in ("left", "grad")}
            packets[packet].stash(refs_here, name, left, grad)

        def ship(packet):
            refs_here = {part: stashed[packet, part] for part in ("left", "grad")}
            targets_here = {way: leaving[packet, way] for way in ("keep", "send")}
            sems = sem_packet.at[list(packets).index(packet)]
            room.sent += packets[packet].ship(refs_here, targets_here, sems, scalar_ref[1])

        room.stash, room.ship, room.stashed = stash, ship, stashed
        body(room, scalar_ref)
        room.finish()

    moved = sum(item.size * item.dtype.itemsize for item in list(inputs.values()) + shapes_out)
    results = pl.pallas_call(
        kernel,
        out_shape=shapes_out,
        in_specs=[pl.BlockSpec(memory_space=pltpu.SMEM)] + [ANY] * len(names_in),
        out_specs=[ANY] * len(shapes_out),
        scratch_shapes=[
            pltpu.VMEM(inputs[name].shape[name in single :], inputs[name].dtype) for name in names_in
        ]
        + [pltpu.VMEM(outputs[name].shape, outputs[name].dtype) for name in names_out]
        + [
            pltpu.VMEM(packets[name].scratch()[part].shape, BF) for name, part in stashes
        ]
        + [pltpu.VMEM(item.shape, item.dtype) for item in extra.values()]
        + [
            pltpu.SemaphoreType.DMA((len(names_in),)),
            pltpu.SemaphoreType.DMA((max(1, len(names_out)),)),
            pltpu.SemaphoreType.DMA((max(1, len(packets)), 3)),
        ],
        compiler_params=pltpu.CompilerParams(vmem_limit_bytes=VMEM_LIMIT),
        cost_estimate=pl.CostEstimate(flops=flops, bytes_accessed=moved, transcendentals=0),
    )(scalars, *inputs.values())
    rest = dict(zip(ways, results[len(names_out) :]))
    return dict(zip(names_out, results)), {
        name: (rest[name, "keep"], rest[name, "send"]) for name in packets
    }


def weight_grads(packet, names, keep, send, came, scalars, small=False):
    tops, height = {}, 0
    for name in names:
        depth, width = packet.weights[name]
        tops[name] = height
        height += depth // GROUPS * width // (2 * SLAB)
    small_at = height
    height += 16 if small else 0
    half = jax.ShapeDtypeStruct((GROUPS // 2, height, SLAB), BF)

    def kernel(scalar, keep_in, send_in, came_in, kept_out, sent_out, keep_ref, grad_ref, came_ref, packed, sems, sems_out):
        first = pltpu.make_async_copy(keep_in, keep_ref, sems.at[0])
        second = pltpu.make_async_copy(
            send_in.at[pl.ds(packet.left, packet.grad)], grad_ref, sems.at[1]
        )
        third = pltpu.make_async_copy(came_in, came_ref, sems.at[2])
        for copy in (first, second, third):
            copy.start()
        for copy in (first, second, third):
            copy.wait()
        core, mine = scalar[1], scalar[2]

        def place(side, block):
            spot = side * scalar[3]
            for bit in range(3):
                spot = spot + (block >> bit & 1) * scalar[4 + bit]
            return spot

        sent = []

        def ship(top, rows, which):
            for way, target in ((mine, kept_out), (1 - mine, sent_out)):
                copy = pltpu.make_async_copy(
                    packed.at[pl.ds(way * (GROUPS // 2), GROUPS // 2), pl.ds(top, rows)],
                    target.at[:, pl.ds(top, rows)],
                    sems_out.at[which, len(sent) % 2],
                )
                copy.start()
                sent.append(copy)

        for which, name in enumerate(names):
            depth, width = packet.weights[name]
            block, half_pieces = depth // GROUPS, width // (2 * SLAB)
            left_at, grad_at = packet.left_at[name], packet.grad_at[name]
            left = jnp.concatenate(
                [ref[left_at : left_at + depth // 2] for ref in (keep_ref, came_ref)], 1
            )
            for piece in range(width // SLAB):
                at = grad_at + piece * SLAB
                right = jnp.concatenate(
                    [
                        jnp.concatenate(
                            [ref[base + at + i * LANES : base + at + (i + 1) * LANES] for i in (0, 1)], 1
                        )
                        for ref, base in ((grad_ref, 0), (came_ref, packet.left))
                    ],
                    0,
                )
                tile = matmul(left, right).astype(BF)
                side, offset = divmod(piece, half_pieces)
                top = tops[name] + offset * block
                for number in range(GROUPS // 2):
                    packed[place(side, number), top : top + block] = tile[
                        number * block : (number + 1) * block
                    ]
            ship(tops[name], block * half_pieces, which)
        if small:
            at = packet.extra_at
            total = sum(
                jnp.concatenate(
                    [ref[base + at + 16 * i : base + at + 16 * (i + 1)].astype(F32) for i in range(4)], 1
                )
                for ref, base in ((grad_ref, 0), (came_ref, packet.left))
            )
            share = total.shape[1] // GROUPS
            for number in range(GROUPS // 2):
                turned = [
                    pltpu.roll(total, (total.shape[1] - (2 * number + i) * share) % total.shape[1], 1)
                    for i in (0, 1)
                ]
                part = jnp.where(core == 0, turned[0], turned[1])[:, :SLAB].astype(BF)
                for side in (0, 1):
                    packed[place(side, number), small_at : small_at + 16] = part
            ship(small_at, 16, len(names))
        for copy in sent:
            copy.wait()

    flops = sum(2 * 2 * LANES * packet.weights[name][0] * packet.weights[name][1] // 2 for name in names)
    return pl.pallas_call(
        kernel,
        out_shape=[half, half],
        in_specs=[pl.BlockSpec(memory_space=pltpu.SMEM)] + [ANY] * 3,
        out_specs=[ANY] * 2,
        scratch_shapes=[
            pltpu.VMEM(keep.shape, BF),
            pltpu.VMEM((packet.grad, LANES), BF),
            pltpu.VMEM(came.shape, BF),
            pltpu.VMEM((GROUPS, height, SLAB), BF),
            pltpu.SemaphoreType.DMA((3,)),
            pltpu.SemaphoreType.DMA((len(names) + 1, 2)),
        ],
        compiler_params=pltpu.CompilerParams(vmem_limit_bytes=VMEM_LIMIT),
        cost_estimate=pl.CostEstimate(
            flops=flops, bytes_accessed=4 * half.size + 6 * came.size, transcendentals=0
        ),
    )(scalars, keep, send, came)


def equal_ids(row_ids, column_ids):
    length = row_ids.shape[1]
    down = jnp.broadcast_to(row_ids.astype(F32), (length, length)).T
    return down == jnp.broadcast_to(column_ids.astype(F32), (length, length))


def scale_out(scale):
    return jnp.broadcast_to(scale, (scale.shape[0], 128))


def make_forward(width):
    def body(room, scalar):
        section = scalar[0]
        get, put, held = room.get, room.put, room.held_out
        start_forward(room, section)
        source_ids = get("segments")[0, pl.ds(section, 1), 0, :]
        target_ids = room.held_in["segments"][1, pl.ds(section, 1), 0, :]

        source = get("source")[...]
        gains, shifts = get("encoder_gain"), get("encoder_shift")
        put("e_projected", matmul(source, get("encoder_inward")[...]).astype(BF))
        projected = held["e_projected"]
        mixed = attend(
            projected[:, :width],
            projected[:, width : 2 * width],
            projected[:, 2 * width :],
            equal_ids(source_ids, source_ids),
            held["e_chances"],
        )
        put("e_chances")
        put("e_mixed", mixed)
        summed = source.astype(F32) + matmul(mixed, get("encoder_outward")[...])
        first, unit, scale = norm(summed, gains[0:1], shifts[0:1])
        put("e_unit0", unit)
        put("e_scale0", scale_out(scale))
        low = first.astype(BF)
        put("e_low", low)
        widen_forward(low, get("encoder_widen"), held["e_hidden"], held["e_slope"])
        put("e_hidden")
        put("e_slope")
        summed = first + matmul(held["e_hidden"][...], get("encoder_narrow")[...])
        result, unit, scale = norm(summed, gains[1:2], shifts[1:2])
        put("e_unit1", unit)
        put("e_scale1", scale_out(scale))
        memory = result.astype(BF)
        put("memory", memory)

        target = get("target")[...]
        gains, shifts = get("decoder_gain"), get("decoder_shift")
        put("d_projected", matmul(target, get("decoder_inward")[...]).astype(BF))
        projected = held["d_projected"]
        length = target.shape[0]
        rows = lax.broadcasted_iota(jnp.int32, (length, length), 0)
        columns = lax.broadcasted_iota(jnp.int32, (length, length), 1)
        mixed = attend(
            projected[:, :width],
            projected[:, width : 2 * width],
            projected[:, 2 * width :],
            equal_ids(target_ids, target_ids) & (rows >= columns),
            held["d_chances"],
        )
        put("d_chances")
        put("d_mixed", mixed)
        summed = target.astype(F32) + matmul(mixed, get("decoder_outward")[...])
        first, unit, scale = norm(summed, gains[0:1], shifts[0:1])
        put("d_unit0", unit)
        put("d_scale0", scale_out(scale))
        low = first.astype(BF)
        put("d_low", low)

        query = matmul(low, get("decoder_cross_query")[...]).astype(BF)
        put("c_query", query)
        put("c_paired", matmul(memory, get("decoder_cross_memory")[...]).astype(BF))
        paired = held["c_paired"]
        mixed = attend(
            query,
            paired[:, :width],
            paired[:, width:],
            equal_ids(target_ids, source_ids),
            held["c_chances"],
        )
        put("c_chances")
        put("c_mixed", mixed)
        summed = first + matmul(mixed, get("decoder_cross_outward")[...])
        second, unit1, scale1 = norm(summed, gains[1:2], shifts[1:2])
        put("d_unit1", unit1)
        put("d_scale1", scale_out(scale1))

        low = second.astype(BF)
        hidden_ref, slope_ref = room.held_out["d_hidden"], room.held_out["d_slope"]
        widen_forward(low, get("decoder_widen"), hidden_ref, slope_ref)
        summed = second + matmul(hidden_ref[...], get("decoder_narrow")[...])
        result, unit, scale = norm(summed, gains[2:3], shifts[2:3])
        put("output", result.astype(BF))

        grad_sum, grad_gain, grad_shift = norm_back(
            get("cotangent")[...].astype(F32), unit, scale, gains[2:3]
        )
        grad_low = grad_sum.astype(BF)
        room.stash("d_wide", "decoder_narrow", hidden_ref[...], grad_low)
        grad_before = widen_backward(grad_low, room.held_in["decoder_narrow"], slope_ref)
        room.stash("d_wide", "decoder_widen", low, grad_before)
        room.ship("d_wide")
        put("d_grad", grad_sum + matmul_back(grad_before, room.held_in["decoder_widen"][...]))
        put("d_small2", jnp.concatenate([grad_gain, grad_shift], 0))

    return body


def start_forward(room, section):
    room.copy_in("segments").start()

    @pl.when(section == 0)
    def _():
        room.copy_in("source", room.sources["source"].at[0]).start()
        room.copy_in("target").start()

    @pl.when(section != 0)
    def _():
        room.copy_in("source", room.sources["target"]).start()
        room.copy_in("target", room.sources["source"].at[1]).start()

    room.copy_in("cotangent", room.sources["cotangent"].at[section]).start()
    room.fetch(
        name
        for name in room.names_in
        if name not in ("segments", "source", "target", "cotangent")
    )


def widen_forward(low, widen_ref, hidden_ref, slope_ref):
    step = 512
    for at in range(0, widen_ref.shape[1], step):
        hidden, slope = gelu_both(matmul(low, widen_ref[:, at : at + step]))
        hidden_ref[:, at : at + step] = hidden.astype(BF)
        slope_ref[:, at : at + step] = slope


def widen_backward(grad_low, narrow_ref, slope_ref):
    step = 512
    parts = []
    for at in range(0, narrow_ref.shape[0], step):
        grad_hidden = matmul_back(grad_low, narrow_ref[at : at + step])
        parts.append((grad_hidden * slope_ref[:, at : at + step]).astype(BF))
    return jnp.concatenate(parts, 1)


def make_decoder_back(width):
    def body(room, scalar):
        get, put = room.get, room.put
        room.fetch(room.names_in)
        gains = get("decoder_gain")
        grad_sum, gain1, shift1 = norm_back(
            get("d_grad")[...], get("d_unit1")[...], get("d_scale1")[:, :1], gains[1:2]
        )
        grad_low = grad_sum.astype(BF)
        grad_mixed = matmul_back(grad_low, get("decoder_cross_outward")[...]).astype(BF)
        paired = get("c_paired")
        grad_query, grad_keys, grad_values = attend_back(
            get("c_query")[...], paired[:, :width], paired[:, width:], get("c_chances"), grad_mixed
        )
        grad_paired = jnp.concatenate([grad_keys, grad_values], 1)
        put(
            "grad_memory", matmul_back(grad_paired, get("decoder_cross_memory")[...]).astype(BF)
        )
        room.stash("d_rest", "decoder_cross_query", get("d_low")[...], grad_query)
        room.stash("d_rest", "decoder_cross_memory", get("memory")[...], grad_paired)
        room.stash("d_rest", "decoder_cross_outward", get("c_mixed")[...], grad_low)
        grad_normed = grad_sum + matmul_back(grad_query, get("decoder_cross_query")[...])
        grad_sum, gain0, shift0 = norm_back(
            grad_normed, get("d_unit0")[...], get("d_scale0")[:, :1], gains[0:1]
        )
        put("d_small01", jnp.concatenate([gain0, gain1, shift0, shift1], 0))
        grad_inputs = self_backward(room, "d", "decoder", "target", "d_rest", grad_sum, width)
        room.ship("d_rest")
        put("grad_inputs", grad_inputs.astype(BF))

    return body


def self_backward(room, short, layer, inputs, packet, grad_sum, width):
    get = room.get
    grad_low = grad_sum.astype(BF)
    grad_mixed = matmul_back(grad_low, get(layer + "_outward")[...]).astype(BF)
    projected = get(short + "_projected")
    grad_projected = jnp.concatenate(
        attend_back(
            projected[:, :width],
            projected[:, width : 2 * width],
            projected[:, 2 * width :],
            get(short + "_chances"),
            grad_mixed,
        ),
        1,
    )
    room.stash(packet, layer + "_inward", get(inputs)[...], grad_projected)
    room.stash(packet, layer + "_outward", get(short + "_mixed")[...], grad_low)
    return grad_sum + matmul_back(grad_projected, get(layer + "_inward")[...])


def make_encoder_back(width, packet):
    def body(room, scalar):
        get, put = room.get, room.put
        room.fetch(room.names_in)
        gains = get("encoder_gain")
        grad_sum, gain1, shift1 = norm_back(
            get("grad_memory")[...].astype(F32),
            get("e_unit1")[...],
            get("e_scale1")[:, :1],
            gains[1:2],
        )
        grad_low = grad_sum.astype(BF)
        room.stash("e_all", "encoder_narrow", get("e_hidden")[...], grad_low)
        grad_before = widen_backward(grad_low, get("encoder_narrow"), get("e_slope"))
        room.stash("e_all", "encoder_widen", get("e_low")[...], grad_before)
        grad_normed = grad_sum + matmul_back(grad_before, get("encoder_widen")[...])
        grad_sum, gain0, shift0 = norm_back(
            grad_normed, get("e_unit0")[...], get("e_scale0")[:, :1], gains[0:1]
        )
        inner, outer = get("d_small01")[...], get("d_small2")[...]
        small = jnp.concatenate(
            [gain0, gain1, shift0, shift1, inner[0:2], outer[0:1], inner[2:4], outer[1:2]]
            + [jnp.zeros((6, width), F32)],
            0,
        )
        for place, tile in enumerate(tiles_of(small.astype(BF))):
            top = packet.extra_at + 16 * place
            room.stashed["e_all", "grad"][top : top + 16] = tile
        grad_inputs = self_backward(room, "e", "encoder", "source", "e_all", grad_sum, width)
        room.ship("e_all")
        put("grad_inputs", grad_inputs.astype(BF))

    return body


def pair_swap(value, axis, apart):
    count = lax.axis_size(axis)
    return lax.ppermute(value, axis, [(i, i ^ apart) for i in range(count)])


def bit_of(step, section, row):
    return section if step == "section" else (row >> step) & 1


def reduce_group(kept, sent, orders, section, row):
    pieces = lax.axis_size("rows")
    for turn, pair in enumerate(zip(*orders)):
        route = []
        for device in range(2 * pieces):
            step = pair[device & 1]
            route.append((device, device ^ (pieces if step == "section" else 1 << step)))
        came = lax.ppermute(sent, ("section", "rows"), route)
        if turn == len(orders[0]) - 1:
            return kept[0].astype(F32) + came[0].astype(F32)
        following = [order[turn + 1] for order in orders]
        mine = jnp.where(
            row & 1 == 0, bit_of(following[0], section, row), bit_of(following[1], section, row)
        )
        kept, sent = halve(kept, came, mine)


def halve(kept, came, mine):
    count = kept.shape[0] // 2

    def half(which):
        one = lax.dynamic_slice_in_dim(kept, which * count, count, 0).astype(F32)
        two = lax.dynamic_slice_in_dim(came, which * count, count, 0).astype(F32)
        return (one + two).astype(BF)

    return half(mine), half(1 - mine)


def place_scalars(orders, section, row):
    core = row & 1

    def pick(values):
        return jnp.where(core == 0, values[0], values[1])

    mine = pick([bit_of(order[0], section, row) for order in orders])
    spots = [pick([8 >> order.index(step) for order in orders]) for step in STEPS]
    return jnp.stack([section, core, mine] + spots).astype(jnp.int32)


def spread_out(halves, core, top, count, share):
    both = jnp.stack(halves)[:, :, top : top + count * share].astype(F32)
    both = both.reshape(2, 2, 2, 2, count, share, SLAB)
    both = both.transpose(0, 3, 2, 1, 5, 4, 6).reshape(2, GROUPS // 2, 1, share, count * SLAB)
    held = jnp.concatenate([both * (core == 0), both * (core == 1)], 2)
    return held.reshape(2, GROUPS, share, count * SLAB)


ENCODER = ("inward", "outward", "widen", "narrow")
DECODER = ("inward", "outward", "cross_query", "cross_memory", "cross_outward", "widen", "narrow")
STEPS = ("section", 1, 2, 3)
CROSSED = (("section", 1, 2, 3), (1, "section", 2, 3))
UPWARD = ((2, 3, "section", 1), (2, 3, 1, "section"))
TEAMS = {
    "d_wide": ("d_wide", ("decoder_narrow", "decoder_widen"), False, CROSSED),
    "d_cross": (
        "d_rest",
        ("decoder_cross_query", "decoder_cross_memory", "decoder_cross_outward"),
        False,
        CROSSED,
    ),
    "d_self": ("d_rest", ("decoder_inward", "decoder_outward"), False, CROSSED),
    "e_wide": ("e_all", ("encoder_narrow", "encoder_widen"), False, CROSSED),
    "e_self": ("e_all", ("encoder_inward", "encoder_outward"), True, UPWARD),
}
PACKETS = {
    "d_wide": ("decoder_narrow", "decoder_widen"),
    "d_rest": (
        "decoder_cross_query",
        "decoder_cross_memory",
        "decoder_cross_outward",
        "decoder_inward",
        "decoder_outward",
    ),
    "e_all": ("encoder_narrow", "encoder_widen", "encoder_inward", "encoder_outward"),
}


def per_device(*arguments):
    names = ["section_input", "segments", "cotangent"]
    for layer, matrices in (("encoder", ENCODER), ("decoder", DECODER)):
        names += [f"{layer}_{short}" for short in matrices + ("gain", "shift")]
    given = dict(zip(names, arguments))
    section = lax.axis_index("section")
    row = lax.axis_index("rows")
    pieces = lax.axis_size("rows")
    core = row & 1
    even = pieces == GROUPS
    orders = {name: team[3] if even else CROSSED[:1] * 2 for name, team in TEAMS.items()}
    spots = {
        pair: place_scalars(pair, section if even else 0 * section, row if even else core)
        for pair in set(orders.values())
    }
    scalars = jnp.stack([section, core]).astype(jnp.int32)
    own = given["section_input"][0]
    length, width = own.shape[1:]
    wide = given["encoder_widen"].shape[1]
    other = pair_swap(
        lax.dynamic_index_in_dim(own, 1 - section, 0, keepdims=False), "section", 1
    )

    def low(*shape):
        return jax.ShapeDtypeStruct(shape, BF)

    def full(*shape):
        return jax.ShapeDtypeStruct(shape, F32)

    chances = full(width // SLAB, PER_SLAB * length, length)
    slabs = low(length, width)
    units = full(length, width)
    scales = full(length, 128)
    product = 2 * length * width * width

    def weights(layer, *short):
        return {f"{layer}_{name}": given[f"{layer}_{name}"] for name in short}

    forward_in = {
        "segments": given["segments"],
        "source": own,
        "target": other,
        **weights("encoder", "gain", "shift", "inward", "outward", "widen", "narrow"),
        **weights("decoder", "gain", "shift", "inward", "outward"),
        **weights("decoder", "cross_query", "cross_memory", "cross_outward", "widen", "narrow"),
        "cotangent": given["cotangent"],
    }
    forward_out = {
        "memory": slabs,
        "output": slabs,
        "e_projected": low(length, 3 * width),
        "e_chances": chances,
        "e_mixed": slabs,
        "e_unit0": units,
        "e_scale0": scales,
        "e_low": slabs,
        "e_hidden": low(length, wide),
        "e_slope": full(length, wide),
        "e_unit1": units,
        "e_scale1": scales,
        "d_projected": low(length, 3 * width),
        "d_chances": chances,
        "d_mixed": slabs,
        "d_unit0": units,
        "d_scale0": scales,
        "d_low": slabs,
        "c_query": slabs,
        "c_paired": low(length, 2 * width),
        "c_chances": chances,
        "c_mixed": slabs,
        "d_unit1": units,
        "d_scale1": scales,
        "d_grad": units,
        "d_small2": full(2, width),
    }
    packets = {
        name: Packet([(item, given[item].shape) for item in items], 64 if name == "e_all" else 0)
        for name, items in PACKETS.items()
    }
    parcels = {}

    def send_parcels(made):
        for name, (keep, sent) in made.items():
            parcels[name] = (keep, sent, pair_swap(sent, "rows", 1))

    kept, made = call(
        make_forward(width),
        forward_in,
        forward_out,
        scalars,
        36 * product,
        {"d_wide": packets["d_wide"]},
        ("source", "cotangent"),
        {"d_hidden": low(length, wide), "d_slope": full(length, wide)},
    )
    send_parcels(made)

    def pick(*keys):
        return {key: kept[key] for key in keys}

    source = jnp.where(section == 0, own[0], other)
    target = jnp.where(section == 0, other, own[1])
    back_in = {
        **weights("decoder", "gain"),
        **pick("d_grad", "d_unit1", "d_scale1"),
        **weights("decoder", "cross_outward"),
        **pick("c_query", "c_paired", "c_chances"),
        **weights("decoder", "cross_memory"),
        **pick("d_low", "memory", "c_mixed"),
        **weights("decoder", "cross_query"),
        **pick("d_unit0", "d_scale0"),
        **weights("decoder", "outward"),
        **pick("d_projected", "d_chances"),
        "target": target,
        **pick("d_mixed"),
        **weights("decoder", "inward"),
    }
    back_out = {
        "grad_memory": slabs,
        "d_small01": full(4, width),
        "grad_inputs": slabs,
    }
    decoded, made = call(
        make_decoder_back(width),
        back_in,
        back_out,
        scalars,
        10 * product,
        {"d_rest": packets["d_rest"]},
    )
    send_parcels(made)

    back_in = {
        **weights("encoder", "gain"),
        "grad_memory": decoded["grad_memory"],
        **pick("e_unit1", "e_scale1", "e_hidden"),
        **weights("encoder", "narrow"),
        **pick("e_slope", "e_low"),
        **weights("encoder", "widen"),
        **pick("e_unit0", "e_scale0"),
        "d_small01": decoded["d_small01"],
        **pick("d_small2"),
        **weights("encoder", "outward"),
        **pick("e_projected", "e_chances"),
        "source": source,
        **pick("e_mixed"),
        **weights("encoder", "inward"),
    }
    ended, made = call(
        make_encoder_back(width, packets["e_all"]),
        back_in,
        {"grad_inputs": slabs},
        scalars,
        13 * product,
        {"e_all": packets["e_all"]},
    )
    send_parcels(made)

    halves = {}
    for name, (packet, items, small, unused) in TEAMS.items():
        halves[name] = weight_grads(
            packets[packet], items, *parcels[packet], spots[orders[name]], small
        )

    def sides(source_side, target_side):
        mine = jnp.where(section == 0, source_side, target_side)
        theirs = pair_swap(
            jnp.where(section == 0, target_side, source_side), "section", 1
        )
        return jnp.stack(
            [jnp.where(section == 0, mine, theirs), jnp.where(section == 0, theirs, mine)]
        )[None]

    results = sides(kept["memory"], kept["output"])
    gradients = sides(ended["grad_inputs"], decoded["grad_inputs"])

    deltas, small = {}, None
    for name, (packet, items, with_small, unused) in TEAMS.items():
        if even:
            block = reduce_group(*halves[name], orders[name], section, row)
        top = 0
        for item in items:
            depth, columns = given[item].shape
            count = columns // (2 * SLAB)
            share = depth // GROUPS
            if even:
                parts = [block[top + i * share : top + (i + 1) * share] for i in range(count)]
                deltas[item] = jnp.concatenate(parts, 1)
            else:
                whole = spread_out(halves[name], core, top, count, share)
                deltas[item] = whole.reshape(2, depth, columns // 2)
            top += count * share
        if with_small and even:
            small = block[top : top + 10, : width // pieces]
        elif with_small:
            small = spread_out(halves[name], core, top, 1, 16)[0, :, :10, : width // GROUPS]
            small = lax.psum(jnp.moveaxis(small, 1, 0).reshape(10, width), ("section", "rows"))
            small = lax.dynamic_slice_in_dim(small, row * (width // pieces), width // pieces, 1)
    if not even:
        for item, part in deltas.items():
            part = lax.psum_scatter(part, "rows", scatter_dimension=1, tiled=True)
            deltas[item] = lax.psum_scatter(part, "section", scatter_dimension=0, tiled=True)[0]

    return (
        results,
        gradients,
        deltas["encoder_inward"],
        deltas["encoder_outward"],
        deltas["encoder_widen"],
        deltas["encoder_narrow"],
        small[0:2],
        small[2:4],
        deltas["decoder_inward"],
        deltas["decoder_outward"],
        deltas["decoder_cross_query"],
        deltas["decoder_cross_memory"],
        deltas["decoder_cross_outward"],
        deltas["decoder_widen"],
        deltas["decoder_narrow"],
        small[4:7],
        small[7:10],
    )


def solution(mesh):
    weights = (P(),) * 15
    shares = P("rows", "section")
    small = P(None, "rows")
    sides = P("section", None, "rows", None)
    return jax.shard_map(
        per_device,
        mesh=mesh,
        in_specs=(sides, P(None, None, "rows", None), P(None, "rows", None)) + weights,
        out_specs=(sides, sides)
        + (shares,) * 4
        + (small,) * 2
        + (shares,) * 7
        + (small,) * 2,
        check_vma=False,
    )
```

```python
import math
from types import SimpleNamespace
from types import SimpleNamespace
from types import SimpleNamespace

import jax
import jax.numpy as jnp
from jax import lax
from jax.experimental import pallas as pl
from jax.experimental.pallas import tpu as pltpu
from jax.sharding import PartitionSpec as P

HEADS = 8
HEAD_DIM = 64
NEG = -1e30
EPS = 1e-05
GROUPS = 16
SLAB = 256
LANES = 128
PER_SLAB = SLAB // HEAD_DIM
BF = jnp.bfloat16
F32 = jnp.float32
def lasting(span):
    return pl.CostEstimate(flops=int(span * 8e9), bytes_accessed=1, transcendentals=0)


FACTOR = 1.0 / math.sqrt(HEAD_DIM)
HBM = pl.BlockSpec(memory_space=pltpu.HBM)
VMEM = pl.BlockSpec(memory_space=pltpu.VMEM)


def matmul(left, right):
    return lax.dot_general(left, right, (((1,), (0,)), ((), ())), preferred_element_type=F32)


def matmul_back(grad, weight):
    return lax.dot_general(grad, weight, (((1,), (1,)), ((), ())), preferred_element_type=F32)


def matmul_across(left, grad):
    return lax.dot_general(left, grad, (((0,), (0,)), ((), ())), preferred_element_type=F32)


def norm(summed, gain, shift):
    center = jnp.mean(summed, -1, keepdims=True)
    centered = summed - center
    spread = jnp.mean(centered * centered, -1, keepdims=True)
    scale = lax.rsqrt(spread + EPS)
    unit = centered * scale
    return unit * gain + shift, unit, scale


def norm_back(grad, unit, scale, gain):
    grad_gain = jnp.sum(grad * unit, 0, keepdims=True)
    grad_shift = jnp.sum(grad, 0, keepdims=True)
    inner = grad * gain
    center = jnp.mean(inner, -1, keepdims=True)
    along = jnp.mean(inner * unit, -1, keepdims=True)
    return scale * (inner - center - unit * along), grad_gain, grad_shift


def gelu_both(before):
    root = math.sqrt(2.0 / math.pi)
    square = before * before
    bent = jnp.tanh(root * before * (1.0 + 0.044715 * square))
    half = 0.5 * (1.0 + bent)
    slope = half + 0.5 * before * (1.0 - bent * bent) * (root * (1.0 + 3 * 0.044715 * square))
    return before * half, slope


def head_marks(dtype):
    lane = lax.broadcasted_iota(jnp.int32, (1, SLAB), 1) // HEAD_DIM
    return [(lane == h).astype(F32).astype(dtype) for h in range(PER_SLAB)]


def spread_heads(slab, marks):
    return jnp.concatenate([slab * mark for mark in marks], 0)


def gather_heads(stacked, rows):
    lane = lax.broadcasted_iota(jnp.int32, (1, SLAB), 1) // HEAD_DIM
    total = stacked[:rows]
    for h in range(1, PER_SLAB):
        total = jnp.where(lane == h, stacked[h * rows : (h + 1) * rows], total)
    return total


def attend(query, keys, values, allowed, chances_ref):
    rows = query.shape[0]
    marks = head_marks(BF)
    wide = jnp.concatenate([allowed] * PER_SLAB, 0)
    mixed = []
    for slab in range(query.shape[1] // SLAB):
        at = slice(slab * SLAB, (slab + 1) * SLAB)
        scores = matmul_back(spread_heads(query[:, at], marks), keys[:, at]) * FACTOR
        scores = jnp.where(wide, scores, NEG)
        weights = jnp.exp(scores - jnp.max(scores, -1, keepdims=True))
        chances = weights * (1.0 / jnp.sum(weights, -1, keepdims=True))
        chances_ref[slab] = chances
        mixed.append(gather_heads(matmul(chances.astype(BF), values[:, at]), rows).astype(BF))
    return jnp.concatenate(mixed, 1)


def attend_back(query, keys, values, chances_ref, grad_mixed):
    rows = query.shape[0]
    marks = head_marks(BF)
    grad_query, grad_keys, grad_values = [], [], []
    for slab in range(query.shape[1] // SLAB):
        at = slice(slab * SLAB, (slab + 1) * SLAB)
        chances = chances_ref[slab]
        spread_grad = spread_heads(grad_mixed[:, at], marks)
        grad_chances = matmul_back(spread_grad, values[:, at])
        grad_values.append(matmul_across(chances.astype(BF), spread_grad).astype(BF))
        held = jnp.sum(chances * grad_chances, -1, keepdims=True)
        grad_scores = (chances * (grad_chances - held)).astype(BF)
        grad_query.append((gather_heads(matmul(grad_scores, keys[:, at]), rows) * FACTOR).astype(BF))
        spread_query = spread_heads(query[:, at], marks)
        grad_keys.append((matmul_across(grad_scores, spread_query) * FACTOR).astype(BF))
    return [jnp.concatenate(item, 1) for item in (grad_query, grad_keys, grad_values)]


def tiles_of(array):
    return [array[:, at : at + LANES] for at in range(0, array.shape[1], LANES)]


class Entry:
    def __init__(self, array):
        self.arrays = (array,)
        self.shape, self.dtype = array.shape[1:], array.dtype

    def pieces(self, refs, section):
        return [(None, refs[0].at[section])]


class Either:
    def __init__(self, *pair):
        pair = [item if isinstance(item, tuple) else (item, None) for item in pair]
        self.arrays = tuple(array for array, unused in pair)
        self.entries = [entry for unused, entry in pair]
        first = self.arrays[0]
        self.shape = first.shape if self.entries[0] is None else first.shape[1:]
        self.dtype = first.dtype

    def pieces(self, refs, section):
        return [
            (here, ref if entry is None else ref.at[entry])
            for here, (ref, entry) in enumerate(zip(refs, self.entries))
        ]


class Whole:
    def __init__(self, array):
        self.arrays = (array,)
        self.shape, self.dtype = array.shape, array.dtype

    def pieces(self, refs, section):
        return [(None, refs[0])]


class Room:
    def __init__(self, inputs, sources, held, sems):
        self.inputs, self.sources, self.held, self.sems = inputs, sources, held, sems
        self.section = lax.axis_index("section")
        self.core = lax.axis_index("rows") & 1
        self.arrived = set()
        for place, name in enumerate(inputs):
            for here, source in inputs[name].pieces(sources[name], self.section):
                copy = pltpu.make_async_copy(source, held[name], sems.at[place])
                if here is None:
                    copy.start()
                else:
                    pl.when(self.section == here)(copy.start)

    def __getattr__(self, name):
        if name in self.inputs and name not in self.arrived:
            self.arrived.add(name)
            place = list(self.inputs).index(name)
            source = self.inputs[name].pieces(self.sources[name], self.section)[0][1]
            pltpu.make_async_copy(source, self.held[name], self.sems.at[place]).wait()
        return self.held[name]

    def finish(self):
        for name in self.inputs:
            getattr(self, name)

    def either(self, here, there):
        return jnp.where(self.section == 0, here[...], there[...])


class Packet:
    def __init__(self, extra=0, **weights):
        self.shapes = {name: array.shape for name, array in weights.items()}
        self.left_at, self.grad_at = {}, {}
        left = grad = 0
        for name, (depth, width) in self.shapes.items():
            self.left_at[name], self.grad_at[name] = left, grad
            left, grad = left + depth // 2, grad + width
        self.left, self.extra_at, self.grad = left, grad, grad + extra

    def leaving(self):
        return [
            pltpu.VMEM((self.left, LANES), BF),
            pltpu.VMEM((self.left + self.grad, LANES), BF),
        ]

    def bind(self, room, refs):
        self.room, (self.keep, self.send) = room, refs

    def stash(self, **operands):
        even = self.room.core == 0
        for name, (left, grad) in operands.items():
            depth, width = self.shapes[name]
            block = depth // GROUPS
            across = left.T
            for group in range(0, GROUPS, 2):
                first = across[group * block : (group + 1) * block]
                second = across[(group + 1) * block : (group + 2) * block]
                top = self.left_at[name] + group // 2 * block
                self.keep[top : top + block] = jnp.where(even, first, second)
                self.send[top : top + block] = jnp.where(even, second, first)
            for place, tile in enumerate(tiles_of(grad)):
                top = self.left + self.grad_at[name] + place * LANES
                self.send[top : top + LANES] = tile


def far_away(array):
    return pltpu.with_memory_space_constraint(array, pltpu.HBM)


def pinned(array):
    return pltpu.with_memory_space_constraint(array, pltpu.VMEM)


def call(body, inputs, near, outputs, loads, span, limit, packet=None, extra=None):
    extra = extra or {}
    inputs = {
        name: item if hasattr(item, "pieces") else Whole(item) for name, item in inputs.items()
    }
    inputs.update({name: Whole(item) for name, item in loads.items()})
    arrays = [array for item in inputs.values() for array in item.arrays]
    outputs = {
        **outputs,
        **{name: jax.ShapeDtypeStruct(item.shape, item.dtype) for name, item in loads.items()},
    }
    shapes_out = [pltpu.VMEM(item.shape, item.dtype) for item in outputs.values()]
    shapes_out += packet.leaving() if packet else []
    brought = [name for name in inputs if name not in loads]

    def kernel(*refs):
        refs = list(refs)

        def take(count):
            taken = refs[:count]
            del refs[:count]
            return taken

        sources = {name: take(len(item.arrays)) for name, item in inputs.items()}
        held = dict(zip(near, take(len(near))))
        held.update(zip(outputs, take(len(outputs))))
        leaving = take(2) if packet else None
        held.update(zip(brought, take(len(brought))))
        held.update(zip(extra, take(len(extra))))
        room = Room(inputs, sources, held, refs[0])
        if packet:
            packet.bind(room, leaving)
        body(room)
        room.finish()

    scratch = [inputs[name] for name in brought] + list(extra.values())
    results = pl.pallas_call(
        kernel,
        out_shape=shapes_out,
        in_specs=[HBM] * len(arrays) + [VMEM] * len(near),
        out_specs=[VMEM] * len(shapes_out),
        scratch_shapes=[pltpu.VMEM(item.shape, item.dtype) for item in scratch]
        + [pltpu.SemaphoreType.DMA((max(1, len(inputs)),))],
        compiler_params=pltpu.CompilerParams(vmem_limit_bytes=limit << 20),
        cost_estimate=lasting(span),
    )(*(far_away(item) for item in arrays), *(pinned(item) for item in near.values()))
    return SimpleNamespace(**dict(zip(outputs, results))), tuple(results[len(outputs) :])


def place_of(side, block, orders, core):
    spots = []
    for order in orders:
        spot = side * (8 >> order.index(SIDE))
        for bit in range(3):
            spot = spot + (block >> bit & 1) * (8 >> order.index(bit + 1))
        spots.append(spot)
    return jnp.where(core == 0, spots[0], spots[1])


def bit_of(step, section, row):
    return section if step == SIDE else (row >> step) & 1


def weight_grads(parcels, names, orders, even, small=False):
    parts = [
        (packet, which, name)
        for which, (packet, *unused) in enumerate(parcels)
        for name in packet.shapes
        if name in names
    ]
    height = sum(
        packet.shapes[name][0] // GROUPS * packet.shapes[name][1] // (2 * SLAB)
        for packet, unused, name in parts
    )
    small_at = height
    height += 16 if small else 0
    half = pltpu.VMEM((GROUPS // 2, height, SLAB), BF)

    def kernel(*refs):
        *operands, kept_out, sent_out, packed = refs
        row = lax.axis_index("rows")
        core = row & 1
        if even:
            first = [bit_of(order[0], lax.axis_index("section"), row) for order in orders]
            mine = jnp.where(core == 0, first[0], first[1])
        else:
            mine = 0

        base = 0
        for packet, which, name in parts:
            keep_ref, send_ref, came_ref = operands[3 * which : 3 * which + 3]
            depth, width = packet.shapes[name]
            block, half_pieces = depth // GROUPS, width // (2 * SLAB)
            left_at, grad_at = packet.left_at[name], packet.left + packet.grad_at[name]
            left = jnp.concatenate(
                [ref[left_at : left_at + depth // 2] for ref in (keep_ref, came_ref)], 1
            )
            for piece in range(width // SLAB):
                at = grad_at + piece * SLAB
                right = jnp.concatenate(
                    [
                        jnp.concatenate([ref[at : at + LANES], ref[at + LANES : at + 2 * LANES]], 1)
                        for ref in (send_ref, came_ref)
                    ],
                    0,
                )
                tile = matmul(left, right).astype(BF)
                side, offset = divmod(piece, half_pieces)
                top = base + offset * block
                for number in range(GROUPS // 2):
                    packed[place_of(side, number, orders, core), top : top + block] = tile[
                        number * block : (number + 1) * block
                    ]
            base += block * half_pieces
        if small:
            packet = parcels[0][0]
            at = packet.left + packet.extra_at
            total = sum(
                jnp.concatenate([ref[at + 16 * i : at + 16 * i + 16] for i in range(4)], 1).astype(F32)
                for ref in operands[1:3]
            )
            width = total.shape[1]
            share = width // GROUPS
            for number in range(GROUPS // 2):
                turned = [
                    pltpu.roll(total, (width - (2 * number + i) * share) % width, 1) for i in (0, 1)
                ]
                part = jnp.where(core == 0, turned[0], turned[1])[:, :SLAB].astype(BF)
                for side in (0, 1):
                    packed[place_of(side, number, orders, core), small_at : small_at + 16] = part
        count = GROUPS // 2
        sent_out[...] = packed[pl.ds((1 - mine) * count, count)]
        kept_out[...] = packed[pl.ds(mine * count, count)]

    arrays = [array for unused, *rest in parcels for array in rest]
    return pl.pallas_call(
        kernel,
        out_shape=[half, half],
        in_specs=[VMEM] * len(arrays),
        out_specs=[VMEM] * 2,
        scratch_shapes=[pltpu.VMEM((GROUPS, height, SLAB), BF)],
        compiler_params=pltpu.CompilerParams(vmem_limit_bytes=16 << 20),
        cost_estimate=lasting(3.5),
    )(*(pinned(item) for item in arrays))


def equal_ids(row_ids, column_ids):
    length = row_ids.shape[1]
    down = jnp.broadcast_to(row_ids.astype(F32), (length, length)).T
    return down == jnp.broadcast_to(column_ids.astype(F32), (length, length))


def scale_out(scale):
    return jnp.broadcast_to(scale, (scale.shape[0], LANES))


def thirds(projected):
    width = projected.shape[1] // 3
    return [projected[:, i * width : (i + 1) * width] for i in range(3)]


def self_part(room, tokens, ids, causal, inward, outward, gain, shift):
    room.projected[...] = matmul(tokens, inward[...]).astype(BF)
    length = tokens.shape[0]
    rows = lax.broadcasted_iota(jnp.int32, (length, length), 0)
    columns = lax.broadcasted_iota(jnp.int32, (length, length), 1)
    reach = jnp.where(causal, 0, length)
    allowed = equal_ids(ids, ids) & (rows + reach >= columns)
    mixed = attend(*thirds(room.projected), allowed, room.chances)
    room.mixed[...] = mixed
    summed = tokens.astype(F32) + matmul(mixed, outward[...])
    first, unit, scale = norm(summed, gain, shift)
    room.unit[...] = unit
    room.scale[...] = scale_out(scale)
    return first


def own_body(room):
    section = room.section
    ids = room.segments[pl.ds(section, 1), pl.ds(section, 1), 0, :][0]
    gain = jnp.where(section == 0, room.encoder_gain[0:1], room.decoder_gain[0:1])
    shift = jnp.where(section == 0, room.encoder_shift[0:1], room.decoder_shift[0:1])
    room.first[...] = self_part(
        room, room.tokens[...], ids, section == 1, room.inward, room.outward, gain, shift
    )


def forward_body(room, packet):
    section = room.section
    source_ids = room.segments[0, pl.ds(section, 1), 0, :]
    target_ids = room.segments[1, pl.ds(section, 1), 0, :]
    ids = jnp.where(section == 0, target_ids, source_ids)
    gain = jnp.where(section == 0, room.decoder_gain[0:1], room.encoder_gain[0:1])
    shift = jnp.where(section == 0, room.decoder_shift[0:1], room.encoder_shift[0:1])
    other = self_part(
        room, room.tokens[...], ids, section == 0, room.inward, room.outward, gain, shift
    )
    own = room.own_first[...]

    first = jnp.where(section == 0, own, other)
    low = first.astype(BF)
    widen_forward(low, room.encoder_widen, room.e_hidden, room.e_slope)
    room.e_low[...] = low
    summed = first + matmul(room.e_hidden[...], room.encoder_narrow[...])
    result, unit, scale = norm(summed, room.encoder_gain[1:2], room.encoder_shift[1:2])
    memory = result.astype(BF)
    room.e_unit1[...] = unit
    room.e_scale1[...] = scale_out(scale)
    room.memory[...] = memory

    first = jnp.where(section == 0, other, own)
    low = first.astype(BF)
    query = matmul(low, room.decoder_cross_query[...]).astype(BF)
    paired = matmul(memory, room.decoder_cross_memory[...]).astype(BF)
    room.d_low[...] = low
    room.c_query[...] = query
    room.c_paired[...] = paired
    width = query.shape[1]
    mixed = attend(
        query,
        room.c_paired[:, :width],
        room.c_paired[:, width:],
        equal_ids(target_ids, source_ids),
        room.c_chances,
    )
    room.c_mixed[...] = mixed
    summed = first + matmul(mixed, room.decoder_cross_outward[...])
    second, unit, scale = norm(summed, room.decoder_gain[1:2], room.decoder_shift[1:2])
    room.d_unit1[...] = unit
    room.d_scale1[...] = scale_out(scale)

    low = second.astype(BF)
    widen_forward(low, room.decoder_widen, room.d_hidden, room.d_slope)
    summed = second + matmul(room.d_hidden[...], room.decoder_narrow[...])
    gain = room.decoder_gain[2:3]
    result, unit, scale = norm(summed, gain, room.decoder_shift[2:3])
    room.output[...] = result.astype(BF)

    grad_sum, grad_gain, grad_shift = norm_back(
        room.cotangent[...].astype(F32), unit, scale, gain
    )
    grad_low = grad_sum.astype(BF)
    grad_before = widen_backward(grad_low, room.decoder_narrow, room.d_slope)
    packet.stash(
        decoder_narrow=(room.d_hidden[...], grad_low), decoder_widen=(low, grad_before)
    )
    room.d_grad[...] = grad_sum + matmul_back(grad_before, room.decoder_widen[...])
    room.d_small2[...] = jnp.concatenate([grad_gain, grad_shift], 0)


def widen_forward(low, widen_ref, hidden_ref, slope_ref):
    step = 512
    for at in range(0, widen_ref.shape[1], step):
        hidden, slope = gelu_both(matmul(low, widen_ref[:, at : at + step]))
        hidden_ref[:, at : at + step] = hidden.astype(BF)
        slope_ref[:, at : at + step] = slope


def widen_backward(grad_low, narrow_ref, slope_ref):
    step = 512
    parts = []
    for at in range(0, narrow_ref.shape[0], step):
        grad_hidden = matmul_back(grad_low, narrow_ref[at : at + step])
        parts.append((grad_hidden * slope_ref[:, at : at + step]).astype(BF))
    return jnp.concatenate(parts, 1)


def cross_back_body(room, packet):
    gain = room.decoder_gain
    grad_sum, gain1, shift1 = norm_back(
        room.d_grad[...], room.d_unit1[...], room.d_scale1[:, :1], gain[1:2]
    )
    grad_low = grad_sum.astype(BF)
    grad_mixed = matmul_back(grad_low, room.decoder_cross_outward[...]).astype(BF)
    paired = room.c_paired
    query = room.c_query[...]
    width = query.shape[1]
    grad_query, grad_keys, grad_values = attend_back(
        query, paired[:, :width], paired[:, width:], room.c_chances, grad_mixed
    )
    grad_paired = jnp.concatenate([grad_keys, grad_values], 1)
    packet.stash(
        decoder_cross_query=(room.d_low[...], grad_query),
        decoder_cross_memory=(room.memory[...], grad_paired),
        decoder_cross_outward=(room.c_mixed[...], grad_low),
    )
    room.grad_memory[...] = matmul_back(grad_paired, room.decoder_cross_memory[...]).astype(BF)
    grad_normed = grad_sum + matmul_back(grad_query, room.decoder_cross_query[...])
    grad_sum, gain0, shift0 = norm_back(
        grad_normed,
        room.either(room.far_unit, room.near_unit),
        room.either(room.far_scale, room.near_scale)[:, :1],
        gain[0:1],
    )
    room.d_grad0[...] = grad_sum
    room.d_small01[...] = jnp.concatenate([gain0, gain1, shift0, shift1], 0)


def self_back(grad_sum, inward, outward, tokens, projected, chances, mixed):
    grad_low = grad_sum.astype(BF)
    grad_mixed = matmul_back(grad_low, outward[...]).astype(BF)
    grad_projected = jnp.concatenate(attend_back(*thirds(projected), chances, grad_mixed), 1)
    pairs = ((tokens, grad_projected), (mixed, grad_low))
    return pairs, grad_sum + matmul_back(grad_projected, inward[...])


def decoder_self_body(room, packet):
    either = room.either
    (inward, outward), grad_inputs = self_back(
        room.d_grad0[...],
        room.decoder_inward,
        room.decoder_outward,
        room.tokens[...],
        either(room.far_projected, room.near_projected),
        either(room.far_chances, room.near_chances),
        either(room.far_mixed, room.near_mixed),
    )
    packet.stash(decoder_inward=inward, decoder_outward=outward)
    room.d_inputs[...] = grad_inputs.astype(BF)


def encoder_back_body(room, packet):
    gain = room.encoder_gain
    grad_sum, gain1, shift1 = norm_back(
        room.grad_memory[...].astype(F32), room.e_unit1[...], room.e_scale1[:, :1], gain[1:2]
    )
    grad_low = grad_sum.astype(BF)
    grad_before = widen_backward(grad_low, room.encoder_narrow, room.e_slope)
    packet.stash(
        encoder_narrow=(room.e_hidden[...], grad_low), encoder_widen=(room.e_low[...], grad_before)
    )
    grad_normed = grad_sum + matmul_back(grad_before, room.encoder_widen[...])
    either = room.either
    grad_sum, gain0, shift0 = norm_back(
        grad_normed,
        either(room.near_unit, room.far_unit),
        either(room.near_scale, room.far_scale)[:, :1],
        gain[0:1],
    )
    inner, outer = room.d_small01[...], room.d_small2[...]
    small = jnp.concatenate(
        [gain0, gain1, shift0, shift1, inner[0:2], outer[0:1], inner[2:4], outer[1:2]]
        + [jnp.zeros((6, inner.shape[1]), F32)],
        0,
    )
    for place, tile in enumerate(tiles_of(small.astype(BF))):
        top = packet.left + packet.extra_at + 16 * place
        packet.send[top : top + 16] = tile
    (inward, outward), grad_inputs = self_back(
        grad_sum,
        room.encoder_inward,
        room.encoder_outward,
        room.tokens[...],
        either(room.near_projected, room.far_projected),
        either(room.near_chances, room.far_chances),
        either(room.near_mixed, room.far_mixed),
    )
    packet.stash(encoder_inward=inward, encoder_outward=outward)
    here, there = grad_inputs.astype(BF), room.d_inputs[...]
    room.sides_mine[0] = either(room.memory, room.output)
    room.sides_mine[1] = jnp.where(room.section == 0, here, there)
    room.sides_theirs[0] = either(room.output, room.memory)
    room.sides_theirs[1] = jnp.where(room.section == 0, there, here)


class Line:
    def __init__(self):
        self.last = None

    def after(self, *values):
        if self.last is None:
            return values
        return lax.optimization_barrier((values, self.last))[0]

    def mark(self, value):
        self.last = value


def pair_swap(value, axis, apart):
    count = lax.axis_size(axis)
    return lax.ppermute(value, axis, [(i, i ^ apart) for i in range(count)])


def halve(kept, came, following):
    count, height = kept.shape[0] // 2, kept.shape[1]
    half = pltpu.VMEM((count, height, SLAB), BF)

    def kernel(kept_ref, came_ref, kept_out, sent_out):
        section, row = lax.axis_index("section"), lax.axis_index("rows")
        bits = [bit_of(step, section, row) for step in following]
        mine = jnp.where(row & 1 == 0, bits[0], bits[1])
        for which, out in ((1 - mine, sent_out), (mine, kept_out)):
            part = pl.ds(which * count, count)
            out[...] = (kept_ref[part].astype(F32) + came_ref[part].astype(F32)).astype(BF)

    return pl.pallas_call(
        kernel,
        out_shape=[half, half],
        in_specs=[VMEM] * 2,
        out_specs=[VMEM] * 2,
        compiler_params=pltpu.CompilerParams(vmem_limit_bytes=4 << 20),
        cost_estimate=lasting(2),
    )(pinned(kept), pinned(came))


class Team:
    def __init__(self, line, orders, small=False, **weights):
        self.line, self.orders, self.small = line, orders, small
        self.shapes = {name: array.shape for name, array in weights.items()}
        self.even = lax.axis_size("rows") == GROUPS
        self.turn = 0
        self.done = {}

    def grads(self, *parcels):
        tied = self.line.after(*(parts for unused, parts in parcels))
        parcels = [(packet, *parts) for (packet, unused), parts in zip(parcels, tied)]
        self.kept, self.sent = weight_grads(
            parcels, list(self.shapes), self.orders, self.even, self.small
        )
        self.line.mark(self.sent)
        if self.even:
            self.go()

    def go(self):
        pieces = lax.axis_size("rows")
        route = []
        for device in range(2 * pieces):
            step = self.orders[device & 1][self.turn]
            route.append((device, device ^ (pieces if step == SIDE else 1 << step)))
        self.came = lax.ppermute(self.sent, ("section", "rows"), route)

    def step(self):
        if not self.even:
            return
        self.turn += 1
        kept, came = self.line.after(self.kept, self.came)
        following = [order[self.turn] for order in self.orders]
        self.kept, self.sent = halve(kept, came, following)
        self.line.mark(self.sent)
        self.go()

    def end(self):
        pieces = lax.axis_size("rows")
        if not self.even:
            return self.end_uneven()
        kept, came = self.line.after(self.kept, self.came)
        shapes = list(self.shapes.values())
        outs = [jax.ShapeDtypeStruct((depth // pieces, width // 2), F32) for depth, width in shapes]
        counts = (2, 2, 3, 3) if self.small else ()
        lanes = 512 // pieces
        outs += [jax.ShapeDtypeStruct((count, lanes), F32) for count in counts]

        def kernel(kept_ref, came_ref, *out_refs):
            top = 0
            for (depth, width), out_ref in zip(shapes, out_refs):
                share = depth // pieces
                for at in range(0, width // 2, SLAB):
                    rows = slice(top, top + share)
                    out_ref[:, at : at + SLAB] = kept_ref[0, rows].astype(F32) + came_ref[
                        0, rows
                    ].astype(F32)
                    top += share
            if counts:
                rows = slice(top, top + 16)
                total = kept_ref[0, rows].astype(F32) + came_ref[0, rows].astype(F32)
                top = 0
                for count, out_ref in zip(counts, out_refs[len(shapes) :]):
                    out_ref[...] = total[top : top + count, :lanes]
                    top += count

        results = pl.pallas_call(
            kernel,
            out_shape=outs,
            in_specs=[VMEM] * 2,
            out_specs=[VMEM] * len(outs),
            compiler_params=pltpu.CompilerParams(vmem_limit_bytes=8 << 20),
            cost_estimate=lasting(1.6),
        )(pinned(kept), pinned(came))
        self.line.mark(results[0])
        self.done = dict(zip(self.shapes, results))
        self.shares = results[len(shapes) :]

    def spread(self, top, count, share):
        core = lax.axis_index("rows") & 1
        both = jnp.stack([self.kept, self.sent])[:, :, top : top + count * share].astype(F32)
        both = both.reshape(2, 2, 2, 2, count, share, SLAB)
        both = both.transpose(0, 3, 2, 1, 5, 4, 6)
        both = both.reshape(2, GROUPS // 2, 1, share, count * SLAB)
        held = jnp.concatenate([both * (core == 0), both * (core == 1)], 2)
        return held.reshape(2, GROUPS, share, count * SLAB)

    def end_uneven(self):
        pieces = lax.axis_size("rows")
        top = 0
        for name, (depth, width) in self.shapes.items():
            share, count = depth // GROUPS, width // (2 * SLAB)
            part = self.spread(top, count, share).reshape(2, depth, width // 2)
            part = lax.psum_scatter(part, "rows", scatter_dimension=1, tiled=True)
            self.done[name] = lax.psum_scatter(part, "section", scatter_dimension=0, tiled=True)[0]
            top += count * share
        if self.small:
            width = 512
            part = self.spread(top, 1, 16)[0, :, :10, : width // GROUPS]
            part = lax.psum(jnp.moveaxis(part, 1, 0).reshape(10, width), ("section", "rows"))
            start = lax.axis_index("rows") * (width // pieces)
            part = lax.dynamic_slice_in_dim(part, start, width // pieces, 1)
            self.shares = (part[0:2], part[2:4], part[4:7], part[7:10])


SIDE = 0
XYZ, YXZ = (SIDE, 1, 2, 3), (1, SIDE, 2, 3)
XZY, YZX = (SIDE, 2, 3, 1), (1, 2, 3, SIDE)
ZXY, ZYX = (2, 3, SIDE, 1), (2, 3, 1, SIDE)
W_ORDERS = (YXZ, ZXY)
Q_ORDERS = (ZYX, YXZ)
E_ORDERS = (XYZ, YXZ)
S_ORDERS = (ZXY, YZX)


def per_device(
    section_input,
    segments,
    cotangent,
    encoder_inward,
    encoder_outward,
    encoder_widen,
    encoder_narrow,
    encoder_gain,
    encoder_shift,
    decoder_inward,
    decoder_outward,
    decoder_cross_query,
    decoder_cross_memory,
    decoder_cross_outward,
    decoder_widen,
    decoder_narrow,
    decoder_gain,
    decoder_shift,
):
    section = lax.axis_index("section")
    own = section_input[0]
    length, width = own.shape[1:]
    wide = encoder_widen.shape[1]

    def low(*shape):
        return jax.ShapeDtypeStruct(shape, BF)

    def full(*shape):
        return jax.ShapeDtypeStruct(shape, F32)

    slabs, units, scales = low(length, width), full(length, width), full(length, LANES)
    chances = full(width // SLAB, PER_SLAB * length, length)
    attended = dict(
        projected=low(length, 3 * width), chances=chances, mixed=slabs, unit=units, scale=scales
    )
    line = Line()

    def run(body, inputs, near, outputs, loads, span, limit, packet=None, extra=None):
        near = dict(near)
        for name in list(near)[:1]:
            (near[name],) = line.after(near[name])
        kept, leaving = call(
            body if packet is None else (lambda room: body(room, packet)),
            inputs,
            near,
            outputs,
            loads,
            span,
            limit,
            packet,
            extra,
        )
        line.mark(list(vars(kept).values())[0])
        if packet is None:
            return kept
        return kept, leaving + (pair_swap(leaving[1], "rows", 1),)

    other = pair_swap(
        lax.dynamic_index_in_dim(own, 1 - section, 0, keepdims=False), "section", 1
    )
    near = run(
        own_body,
        dict(
            segments=segments,
            tokens=Entry(own),
            inward=Either(encoder_inward, decoder_inward),
            encoder_gain=encoder_gain,
            decoder_gain=decoder_gain,
            encoder_shift=encoder_shift,
            decoder_shift=decoder_shift,
            outward=Either(encoder_outward, decoder_outward),
        ),
        {},
        dict(first=units, **attended),
        {},
        4,
        8,
    )

    wide_packet = Packet(decoder_narrow=decoder_narrow, decoder_widen=decoder_widen)
    far, d_wide = run(
        forward_body,
        dict(
            segments=segments,
            tokens=other,
            inward=Either(decoder_inward, encoder_inward),
            decoder_gain=decoder_gain,
            encoder_shift=encoder_shift,
            decoder_shift=decoder_shift,
            outward=Either(decoder_outward, encoder_outward),
            decoder_widen=decoder_widen,
            decoder_narrow=decoder_narrow,
            cotangent=Entry(cotangent),
        ),
        dict(own_first=near.first),
        dict(
            memory=slabs,
            output=slabs,
            **attended,
            e_low=slabs,
            e_hidden=low(length, wide),
            e_slope=full(length, wide),
            e_unit1=units,
            e_scale1=scales,
            d_low=slabs,
            c_query=slabs,
            c_paired=low(length, 2 * width),
            c_chances=chances,
            c_mixed=slabs,
            d_unit1=units,
            d_scale1=scales,
            d_grad=units,
            d_small2=full(2, width),
        ),
        dict(
            encoder_gain=encoder_gain,
            encoder_widen=encoder_widen,
            encoder_narrow=encoder_narrow,
            decoder_cross_query=decoder_cross_query,
            decoder_cross_memory=decoder_cross_memory,
            decoder_cross_outward=decoder_cross_outward,
            decoder_outward=decoder_outward,
            decoder_inward=decoder_inward,
            encoder_outward=encoder_outward,
            encoder_inward=encoder_inward,
        ),
        11,
        24,
        wide_packet,
        dict(d_hidden=low(length, wide), d_slope=full(length, wide)),
    )

    cross_packet = Packet(
        decoder_cross_query=decoder_cross_query,
        decoder_cross_memory=decoder_cross_memory,
        decoder_cross_outward=decoder_cross_outward,
    )
    crossed, d_cross = run(
        cross_back_body,
        dict(decoder_gain=decoder_gain),
        dict(
            d_grad=far.d_grad,
            d_unit1=far.d_unit1,
            d_scale1=far.d_scale1,
            c_query=far.c_query,
            c_paired=far.c_paired,
            c_chances=far.c_chances,
            d_low=far.d_low,
            memory=far.memory,
            c_mixed=far.c_mixed,
            decoder_cross_outward=far.decoder_cross_outward,
            decoder_cross_memory=far.decoder_cross_memory,
            decoder_cross_query=far.decoder_cross_query,
            near_unit=near.unit,
            near_scale=near.scale,
            far_unit=far.unit,
            far_scale=far.scale,
        ),
        dict(grad_memory=slabs, d_grad0=units, d_small01=full(4, width)),
        {},
        4.7,
        8,
        cross_packet,
    )

    def d_self_run():
        packet = Packet(decoder_inward=decoder_inward, decoder_outward=decoder_outward)
        return packet, *run(
            decoder_self_body,
            dict(tokens=Either(other, (own, 1))),
            dict(
                d_grad0=crossed.d_grad0,
                decoder_outward=far.decoder_outward,
                decoder_inward=far.decoder_inward,
                near_projected=near.projected,
                near_chances=near.chances,
                near_mixed=near.mixed,
                far_projected=far.projected,
                far_chances=far.chances,
                far_mixed=far.mixed,
            ),
            dict(d_inputs=slabs),
            {},
            5,
            8,
            packet,
        )

    def encoder_run(d_inputs):
        packet = Packet(
            64,
            encoder_narrow=encoder_narrow,
            encoder_widen=encoder_widen,
            encoder_inward=encoder_inward,
            encoder_outward=encoder_outward,
        )
        sides = low(2, length, width)
        return packet, *run(
            encoder_back_body,
            dict(tokens=Either((own, 0), other)),
            dict(
                encoder_gain=far.encoder_gain,
                grad_memory=crossed.grad_memory,
                e_unit1=far.e_unit1,
                e_scale1=far.e_scale1,
                encoder_narrow=far.encoder_narrow,
                e_slope=far.e_slope,
                e_hidden=far.e_hidden,
                e_low=far.e_low,
                encoder_widen=far.encoder_widen,
                d_small01=crossed.d_small01,
                d_small2=far.d_small2,
                encoder_outward=far.encoder_outward,
                encoder_inward=far.encoder_inward,
                near_unit=near.unit,
                near_scale=near.scale,
                near_projected=near.projected,
                near_chances=near.chances,
                near_mixed=near.mixed,
                far_unit=far.unit,
                far_scale=far.scale,
                far_projected=far.projected,
                far_chances=far.chances,
                far_mixed=far.mixed,
                d_inputs=d_inputs,
                memory=far.memory,
                output=far.output,
            ),
            dict(sides_mine=sides, sides_theirs=sides),
            {},
            8,
            12,
            packet,
        )

    team_w = Team(line, W_ORDERS, decoder_narrow=decoder_narrow, decoder_widen=decoder_widen)
    team_q = Team(
        line,
        Q_ORDERS,
        decoder_cross_query=decoder_cross_query,
        decoder_cross_memory=decoder_cross_memory,
        decoder_cross_outward=decoder_cross_outward,
        decoder_inward=decoder_inward,
        decoder_outward=decoder_outward,
    )
    team_e = Team(line, E_ORDERS, encoder_narrow=encoder_narrow, encoder_widen=encoder_widen)
    team_s = Team(
        line, S_ORDERS, True, encoder_inward=encoder_inward, encoder_outward=encoder_outward
    )
    team_w.grads((wide_packet, d_wide))
    self_packet, turned, d_self = d_self_run()
    encoder_packet, ended, e_all = encoder_run(turned.d_inputs)
    team_q.grads((cross_packet, d_cross), (self_packet, d_self))
    (theirs,) = line.after(ended.sides_theirs)
    theirs = pair_swap(theirs, "section", 1)
    team_e.grads((encoder_packet, e_all))
    team_w.step()
    team_q.step()
    team_s.grads((encoder_packet, e_all))
    team_e.step()
    team_w.step()
    team_s.step()
    team_q.step()
    team_e.step()
    team_w.step()
    team_s.step()
    team_q.step()
    team_e.step()
    team_s.step()
    mine, theirs = line.after(ended.sides_mine, theirs)
    results, gradients = (
        jnp.stack(
            [
                jnp.where(section == 0, mine[i], theirs[i]),
                jnp.where(section == 0, theirs[i], mine[i]),
            ]
        )[None]
        for i in (0, 1)
    )
    line.mark(gradients)
    team_w.end()
    team_q.end()
    team_s.end()
    team_e.end()

    done = {}
    for team in (team_w, team_q, team_e, team_s):
        done.update(team.done)
    deltas = SimpleNamespace(**done)
    shares = team_s.shares
    return (
        results,
        gradients,
        deltas.encoder_inward,
        deltas.encoder_outward,
        deltas.encoder_widen,
        deltas.encoder_narrow,
        shares[0],
        shares[1],
        deltas.decoder_inward,
        deltas.decoder_outward,
        deltas.decoder_cross_query,
        deltas.decoder_cross_memory,
        deltas.decoder_cross_outward,
        deltas.decoder_widen,
        deltas.decoder_narrow,
        shares[2],
        shares[3],
    )


def solution(mesh):
    weights = (P(),) * 15
    shares = P("rows", "section")
    small = P(None, "rows")
    sides = P("section", None, "rows", None)
    return jax.shard_map(
        per_device,
        mesh=mesh,
        in_specs=(sides, P(None, None, "rows", None), P(None, "rows", None)) + weights,
        out_specs=(sides, sides)
        + (shares,) * 4
        + (small,) * 2
        + (shares,) * 7
        + (small,) * 2,
        check_vma=False,
    )
```

```python
import math
from types import SimpleNamespace
from types import SimpleNamespace
from types import SimpleNamespace

import jax
import jax.numpy as jnp
from jax import lax
from jax.experimental import pallas as pl
from jax.experimental.pallas import tpu as pltpu
from jax.sharding import PartitionSpec as P

HEADS = 8
HEAD_DIM = 64
NEG = -1e30
EPS = 1e-05
GROUPS = 16
SLAB = 256
LANES = 128
PER_SLAB = SLAB // HEAD_DIM
BF = jnp.bfloat16
F32 = jnp.float32
def lasting(span):
    return pl.CostEstimate(flops=int(span * 8e9), bytes_accessed=1, transcendentals=0)


FACTOR = 1.0 / math.sqrt(HEAD_DIM)
HBM = pl.BlockSpec(memory_space=pltpu.HBM)
VMEM = pl.BlockSpec(memory_space=pltpu.VMEM)


def matmul(left, right):
    return lax.dot_general(left, right, (((1,), (0,)), ((), ())), preferred_element_type=F32)


def matmul_back(grad, weight):
    return lax.dot_general(grad, weight, (((1,), (1,)), ((), ())), preferred_element_type=F32)


def matmul_across(left, grad):
    return lax.dot_general(left, grad, (((0,), (0,)), ((), ())), preferred_element_type=F32)


def norm(summed, gain, shift):
    center = jnp.mean(summed, -1, keepdims=True)
    centered = summed - center
    spread = jnp.mean(centered * centered, -1, keepdims=True)
    scale = lax.rsqrt(spread + EPS)
    unit = centered * scale
    return unit * gain + shift, unit, scale


def norm_back(grad, unit, scale, gain):
    grad_gain = jnp.sum(grad * unit, 0, keepdims=True)
    grad_shift = jnp.sum(grad, 0, keepdims=True)
    inner = grad * gain
    center = jnp.mean(inner, -1, keepdims=True)
    along = jnp.mean(inner * unit, -1, keepdims=True)
    return scale * (inner - center - unit * along), grad_gain, grad_shift


def gelu_both(before):
    root = math.sqrt(2.0 / math.pi)
    square = before * before
    bent = jnp.tanh(root * before * (1.0 + 0.044715 * square))
    half = 0.5 * (1.0 + bent)
    slope = half + 0.5 * before * (1.0 - bent * bent) * (root * (1.0 + 3 * 0.044715 * square))
    return before * half, slope


def head_marks(dtype):
    lane = lax.broadcasted_iota(jnp.int32, (1, SLAB), 1) // HEAD_DIM
    return [(lane == h).astype(F32).astype(dtype) for h in range(PER_SLAB)]


def spread_heads(slab, marks):
    return jnp.concatenate([slab * mark for mark in marks], 0)


def gather_heads(stacked, rows):
    lane = lax.broadcasted_iota(jnp.int32, (1, SLAB), 1) // HEAD_DIM
    total = stacked[:rows]
    for h in range(1, PER_SLAB):
        total = jnp.where(lane == h, stacked[h * rows : (h + 1) * rows], total)
    return total


def attend(query, keys, values, allowed, chances_ref):
    rows = query.shape[0]
    marks = head_marks(BF)
    wide = jnp.concatenate([allowed] * PER_SLAB, 0)
    mixed = []
    for slab in range(query.shape[1] // SLAB):
        at = slice(slab * SLAB, (slab + 1) * SLAB)
        scores = matmul_back(spread_heads(query[:, at], marks), keys[:, at]) * FACTOR
        scores = jnp.where(wide, scores, NEG)
        weights = jnp.exp(scores - jnp.max(scores, -1, keepdims=True))
        chances = weights * (1.0 / jnp.sum(weights, -1, keepdims=True))
        chances_ref[slab] = chances
        mixed.append(gather_heads(matmul(chances.astype(BF), values[:, at]), rows).astype(BF))
    return jnp.concatenate(mixed, 1)


def attend_back(query, keys, values, chances_ref, grad_mixed):
    rows = query.shape[0]
    marks = head_marks(BF)
    grad_query, grad_keys, grad_values = [], [], []
    for slab in range(query.shape[1] // SLAB):
        at = slice(slab * SLAB, (slab + 1) * SLAB)
        chances = chances_ref[slab]
        spread_grad = spread_heads(grad_mixed[:, at], marks)
        grad_chances = matmul_back(spread_grad, values[:, at])
        grad_values.append(matmul_across(chances.astype(BF), spread_grad).astype(BF))
        held = jnp.sum(chances * grad_chances, -1, keepdims=True)
        grad_scores = (chances * (grad_chances - held)).astype(BF)
        grad_query.append((gather_heads(matmul(grad_scores, keys[:, at]), rows) * FACTOR).astype(BF))
        spread_query = spread_heads(query[:, at], marks)
        grad_keys.append((matmul_across(grad_scores, spread_query) * FACTOR).astype(BF))
    return [jnp.concatenate(item, 1) for item in (grad_query, grad_keys, grad_values)]


def tiles_of(array):
    return [array[:, at : at + LANES] for at in range(0, array.shape[1], LANES)]


class Entry:
    def __init__(self, array):
        self.arrays = (array,)
        self.shape, self.dtype = array.shape[1:], array.dtype

    def pieces(self, refs, section):
        return [(None, refs[0].at[section])]


class Either:
    def __init__(self, *pair):
        pair = [item if isinstance(item, tuple) else (item, None) for item in pair]
        self.arrays = tuple(array for array, unused in pair)
        self.entries = [entry for unused, entry in pair]
        first = self.arrays[0]
        self.shape = first.shape if self.entries[0] is None else first.shape[1:]
        self.dtype = first.dtype

    def pieces(self, refs, section):
        return [
            (here, ref if entry is None else ref.at[entry])
            for here, (ref, entry) in enumerate(zip(refs, self.entries))
        ]


class Whole:
    def __init__(self, array):
        self.arrays = (array,)
        self.shape, self.dtype = array.shape, array.dtype

    def pieces(self, refs, section):
        return [(None, refs[0])]


class Room:
    def __init__(self, inputs, sources, held, sems, away):
        self.inputs, self.sources, self.held, self.sems = inputs, sources, held, sems
        self.away, self.left = away, {}
        self.section = lax.axis_index("section")
        self.core = lax.axis_index("rows") & 1
        self.arrived = set()
        for place, name in enumerate(inputs):
            for here, source in inputs[name].pieces(sources[name], self.section):
                copy = pltpu.make_async_copy(source, held[name], sems.at[place])
                if here is None:
                    copy.start()
                else:
                    pl.when(self.section == here)(copy.start)

    def __getattr__(self, name):
        if name in self.inputs and name not in self.arrived:
            self.arrived.add(name)
            place = list(self.inputs).index(name)
            source = self.inputs[name].pieces(self.sources[name], self.section)[0][1]
            pltpu.make_async_copy(source, self.held[name], self.sems.at[place]).wait()
        return self.held[name]

    def leave(self, *names):
        for name, (target, sem) in self.away.items():
            if name in names:
                copy = pltpu.make_async_copy(self.held[name], target, sem)
                copy.start()
                self.left[name] = copy

    def finish(self):
        self.leave(*(name for name in self.away if name not in self.left))
        for name in self.inputs:
            getattr(self, name)
        for copy in self.left.values():
            copy.wait()

    def either(self, here, there):
        return jnp.where(self.section == 0, here[...], there[...])


class Packet:
    def __init__(self, extra=0, **weights):
        self.shapes = {name: array.shape for name, array in weights.items()}
        self.left_at, self.grad_at = {}, {}
        left = grad = 0
        for name, (depth, width) in self.shapes.items():
            self.left_at[name], self.grad_at[name] = left, grad
            left, grad = left + depth // 2, grad + width
        self.left, self.extra_at, self.grad = left, grad, grad + extra

    def leaving(self):
        return [
            pltpu.VMEM((self.left, LANES), BF),
            pltpu.VMEM((self.left + self.grad, LANES), BF),
        ]

    def bind(self, room, refs):
        self.room, (self.keep, self.send) = room, refs

    def stash(self, **operands):
        even = self.room.core == 0
        for name, (left, grad) in operands.items():
            depth, width = self.shapes[name]
            block = depth // GROUPS
            across = left.T
            for group in range(0, GROUPS, 2):
                first = across[group * block : (group + 1) * block]
                second = across[(group + 1) * block : (group + 2) * block]
                top = self.left_at[name] + group // 2 * block
                self.keep[top : top + block] = jnp.where(even, first, second)
                self.send[top : top + block] = jnp.where(even, second, first)
            for place, tile in enumerate(tiles_of(grad)):
                top = self.left + self.grad_at[name] + place * LANES
                self.send[top : top + LANES] = tile


def far_away(array):
    return pltpu.with_memory_space_constraint(array, pltpu.HBM)


def pinned(array):
    return pltpu.with_memory_space_constraint(array, pltpu.VMEM)


def call(body, inputs, near, outputs, loads, span, limit, packet=None, extra=None, away=None, late=None):
    extra, away = extra or {}, away or {}
    inputs = {
        name: item if hasattr(item, "pieces") else Whole(item) for name, item in inputs.items()
    }
    loads = {name: item if hasattr(item, "pieces") else Whole(item) for name, item in loads.items()}
    inputs.update(loads)
    inputs.update({name: item if hasattr(item, "pieces") else Whole(item) for name, item in (late or {}).items()})
    arrays = [array for item in inputs.values() for array in item.arrays]
    outputs = {
        **outputs,
        **{name: jax.ShapeDtypeStruct(item.shape, item.dtype) for name, item in loads.items()},
    }
    shapes_out = [pltpu.VMEM(item.shape, item.dtype) for item in outputs.values()]
    shapes_out += packet.leaving() if packet else []
    shapes_out += [pltpu.HBM(item.shape, item.dtype) for item in away.values()]
    brought = [name for name in inputs if name not in loads]

    def kernel(*refs):
        refs = list(refs)

        def take(count):
            taken = refs[:count]
            del refs[:count]
            return taken

        sources = {name: take(len(item.arrays)) for name, item in inputs.items()}
        held = dict(zip(near, take(len(near))))
        held.update(zip(outputs, take(len(outputs))))
        leaving = take(2) if packet else None
        targets = take(len(away))
        held.update(zip(brought, take(len(brought))))
        held.update(zip(extra, take(len(extra))))
        held.update(zip(away, take(len(away))))
        away_to = {
            name: (target, refs[1].at[place])
            for place, (name, target) in enumerate(zip(away, targets))
        }
        room = Room(inputs, sources, held, refs[0], away_to)
        if packet:
            packet.bind(room, leaving)
        body(room)
        room.finish()

    scratch = [inputs[name] for name in brought] + list(extra.values()) + list(away.values())
    results = pl.pallas_call(
        kernel,
        out_shape=shapes_out,
        in_specs=[HBM] * len(arrays) + [VMEM] * len(near),
        out_specs=[VMEM] * (len(shapes_out) - len(away)) + [HBM] * len(away),
        scratch_shapes=[pltpu.VMEM(item.shape, item.dtype) for item in scratch]
        + [pltpu.SemaphoreType.DMA((max(1, len(inputs)),))]
        + [pltpu.SemaphoreType.DMA((max(1, len(away)),))],
        compiler_params=pltpu.CompilerParams(vmem_limit_bytes=limit << 20),
        cost_estimate=lasting(span),
    )(*(far_away(item) for item in arrays), *(pinned(item) for item in near.values()))
    made = dict(zip(outputs, results))
    made.update(zip(away, results[len(results) - len(away) :]))
    leaving = tuple(results[len(outputs) : len(results) - len(away)])
    return SimpleNamespace(**made), leaving


def place_of(side, block, orders, core):
    spots = []
    for order in orders:
        spot = side * (8 >> order.index(SIDE))
        for bit in range(3):
            spot = spot + (block >> bit & 1) * (8 >> order.index(bit + 1))
        spots.append(spot)
    return jnp.where(core == 0, spots[0], spots[1])


def bit_of(step, section, row):
    return section if step == SIDE else (row >> step) & 1


def weight_grads(parcels, names, orders, even, small=False):
    parts = [
        (packet, which, name)
        for which, (packet, *unused) in enumerate(parcels)
        for name in packet.shapes
        if name in names
    ]
    height = sum(
        packet.shapes[name][0] // GROUPS * packet.shapes[name][1] // (2 * SLAB)
        for packet, unused, name in parts
    )
    small_at = height
    height += 16 if small else 0
    half = pltpu.VMEM((GROUPS // 2, height, SLAB), BF)

    def kernel(*refs):
        *operands, kept_out, sent_out, packed = refs
        row = lax.axis_index("rows")
        core = row & 1
        if even:
            first = [bit_of(order[0], lax.axis_index("section"), row) for order in orders]
            mine = jnp.where(core == 0, first[0], first[1])
        else:
            mine = 0

        base = 0
        for packet, which, name in parts:
            keep_ref, send_ref, came_ref = operands[3 * which : 3 * which + 3]
            depth, width = packet.shapes[name]
            block, half_pieces = depth // GROUPS, width // (2 * SLAB)
            left_at, grad_at = packet.left_at[name], packet.left + packet.grad_at[name]
            left = jnp.concatenate(
                [ref[left_at : left_at + depth // 2] for ref in (keep_ref, came_ref)], 1
            )
            for piece in range(width // SLAB):
                at = grad_at + piece * SLAB
                right = jnp.concatenate(
                    [
                        jnp.concatenate([ref[at : at + LANES], ref[at + LANES : at + 2 * LANES]], 1)
                        for ref in (send_ref, came_ref)
                    ],
                    0,
                )
                tile = matmul(left, right).astype(BF)
                side, offset = divmod(piece, half_pieces)
                top = base + offset * block
                for number in range(GROUPS // 2):
                    packed[place_of(side, number, orders, core), top : top + block] = tile[
                        number * block : (number + 1) * block
                    ]
            base += block * half_pieces
        if small:
            packet = parcels[0][0]
            at = packet.left + packet.extra_at
            total = sum(
                jnp.concatenate([ref[at + 16 * i : at + 16 * i + 16] for i in range(4)], 1).astype(F32)
                for ref in operands[1:3]
            )
            width = total.shape[1]
            share = width // GROUPS
            for number in range(GROUPS // 2):
                turned = [
                    pltpu.roll(total, (width - (2 * number + i) * share) % width, 1) for i in (0, 1)
                ]
                part = jnp.where(core == 0, turned[0], turned[1])[:, :SLAB].astype(BF)
                for side in (0, 1):
                    packed[place_of(side, number, orders, core), small_at : small_at + 16] = part
        count = GROUPS // 2
        sent_out[...] = packed[pl.ds((1 - mine) * count, count)]
        kept_out[...] = packed[pl.ds(mine * count, count)]

    arrays = [array for unused, *rest in parcels for array in rest]
    return pl.pallas_call(
        kernel,
        out_shape=[half, half],
        in_specs=[VMEM] * len(arrays),
        out_specs=[VMEM] * 2,
        scratch_shapes=[pltpu.VMEM((GROUPS, height, SLAB), BF)],
        compiler_params=pltpu.CompilerParams(vmem_limit_bytes=8 << 20),
        cost_estimate=lasting(3.5),
    )(*(pinned(item) for item in arrays))


def equal_ids(row_ids, column_ids):
    length = row_ids.shape[1]
    down = jnp.broadcast_to(row_ids.astype(F32), (length, length)).T
    return down == jnp.broadcast_to(column_ids.astype(F32), (length, length))


def scale_out(scale):
    return jnp.broadcast_to(scale, (scale.shape[0], LANES))


def thirds(projected):
    width = projected.shape[1] // 3
    return [projected[:, i * width : (i + 1) * width] for i in range(3)]


def self_part(room, tokens, ids, causal, inward, outward, gain, shift):
    room.projected[...] = matmul(tokens, inward[...]).astype(BF)
    room.leave("projected")
    length = tokens.shape[0]
    rows = lax.broadcasted_iota(jnp.int32, (length, length), 0)
    columns = lax.broadcasted_iota(jnp.int32, (length, length), 1)
    reach = jnp.where(causal, 0, length)
    allowed = equal_ids(ids, ids) & (rows + reach >= columns)
    mixed = attend(*thirds(room.projected), allowed, room.chances)
    room.mixed[...] = mixed
    room.leave("chances", "mixed")
    summed = tokens.astype(F32) + matmul(mixed, outward[...])
    first, unit, scale = norm(summed, gain, shift)
    room.unit[...] = unit
    room.scale[...] = scale_out(scale)
    return first


def own_body(room):
    section = room.section
    ids = room.segments[pl.ds(section, 1), pl.ds(section, 1), 0, :][0]
    gain = jnp.where(section == 0, room.encoder_gain[0:1], room.decoder_gain[0:1])
    shift = jnp.where(section == 0, room.encoder_shift[0:1], room.decoder_shift[0:1])
    room.first[...] = self_part(
        room, room.tokens[...], ids, section == 1, room.inward, room.outward, gain, shift
    )


def forward_body(room, packet):
    section = room.section
    source_ids = room.segments[0, pl.ds(section, 1), 0, :]
    target_ids = room.segments[1, pl.ds(section, 1), 0, :]
    ids = jnp.where(section == 0, target_ids, source_ids)
    gain = jnp.where(section == 0, room.decoder_gain[0:1], room.encoder_gain[0:1])
    shift = jnp.where(section == 0, room.decoder_shift[0:1], room.encoder_shift[0:1])
    other = self_part(
        room, room.tokens[...], ids, section == 0, room.inward, room.outward, gain, shift
    )
    own = room.own_first[...]

    first = jnp.where(section == 0, own, other)
    low = first.astype(BF)
    widen_forward(low, room.encoder_widen, room.e_hidden, room.e_slope)
    room.e_low[...] = low
    summed = first + matmul(room.e_hidden[...], room.encoder_narrow[...])
    result, unit, scale = norm(summed, room.encoder_gain[1:2], room.encoder_shift[1:2])
    memory = result.astype(BF)
    room.e_unit1[...] = unit
    room.e_scale1[...] = scale_out(scale)
    room.memory[...] = memory

    first = jnp.where(section == 0, other, own)
    low = first.astype(BF)
    query = matmul(low, room.decoder_cross_query[...]).astype(BF)
    paired = matmul(memory, room.decoder_cross_memory[...]).astype(BF)
    room.d_low[...] = low
    room.c_query[...] = query
    room.c_paired[...] = paired
    width = query.shape[1]
    mixed = attend(
        query,
        room.c_paired[:, :width],
        room.c_paired[:, width:],
        equal_ids(target_ids, source_ids),
        room.c_chances,
    )
    room.c_mixed[...] = mixed
    summed = first + matmul(mixed, room.decoder_cross_outward[...])
    second, unit, scale = norm(summed, room.decoder_gain[1:2], room.decoder_shift[1:2])
    room.d_unit1[...] = unit
    room.d_scale1[...] = scale_out(scale)

    low = second.astype(BF)
    widen_forward(low, room.decoder_widen, room.d_hidden, room.d_slope)
    summed = second + matmul(room.d_hidden[...], room.decoder_narrow[...])
    gain = room.decoder_gain[2:3]
    result, unit, scale = norm(summed, gain, room.decoder_shift[2:3])
    room.output[...] = result.astype(BF)

    grad_sum, grad_gain, grad_shift = norm_back(
        room.cotangent[...].astype(F32), unit, scale, gain
    )
    grad_low = grad_sum.astype(BF)
    grad_before = widen_backward(grad_low, room.decoder_narrow, room.d_slope)
    packet.stash(
        decoder_narrow=(room.d_hidden[...], grad_low), decoder_widen=(low, grad_before)
    )
    room.d_grad[...] = grad_sum + matmul_back(grad_before, room.decoder_widen[...])
    room.d_small2[...] = jnp.concatenate([grad_gain, grad_shift], 0)


def widen_forward(low, widen_ref, hidden_ref, slope_ref):
    step = 512
    for at in range(0, widen_ref.shape[1], step):
        hidden, slope = gelu_both(matmul(low, widen_ref[:, at : at + step]))
        hidden_ref[:, at : at + step] = hidden.astype(BF)
        slope_ref[:, at : at + step] = slope


def widen_backward(grad_low, narrow_ref, slope_ref):
    step = 512
    parts = []
    for at in range(0, narrow_ref.shape[0], step):
        grad_hidden = matmul_back(grad_low, narrow_ref[at : at + step])
        parts.append((grad_hidden * slope_ref[:, at : at + step]).astype(BF))
    return jnp.concatenate(parts, 1)


def cross_back_body(room, packet):
    gain = room.decoder_gain
    grad_sum, gain1, shift1 = norm_back(
        room.d_grad[...], room.d_unit1[...], room.d_scale1[:, :1], gain[1:2]
    )
    grad_low = grad_sum.astype(BF)
    grad_mixed = matmul_back(grad_low, room.decoder_cross_outward[...]).astype(BF)
    paired = room.c_paired
    query = room.c_query[...]
    width = query.shape[1]
    grad_query, grad_keys, grad_values = attend_back(
        query, paired[:, :width], paired[:, width:], room.c_chances, grad_mixed
    )
    grad_paired = jnp.concatenate([grad_keys, grad_values], 1)
    packet.stash(
        decoder_cross_query=(room.d_low[...], grad_query),
        decoder_cross_memory=(room.memory[...], grad_paired),
        decoder_cross_outward=(room.c_mixed[...], grad_low),
    )
    room.grad_memory[...] = matmul_back(grad_paired, room.decoder_cross_memory[...]).astype(BF)
    grad_normed = grad_sum + matmul_back(grad_query, room.decoder_cross_query[...])
    grad_sum, gain0, shift0 = norm_back(
        grad_normed,
        room.either(room.far_unit, room.near_unit),
        room.either(room.far_scale, room.near_scale)[:, :1],
        gain[0:1],
    )
    room.d_grad0[...] = grad_sum
    room.d_small01[...] = jnp.concatenate([gain0, gain1, shift0, shift1], 0)


def self_back(grad_sum, inward, outward, tokens, projected, chances, mixed):
    grad_low = grad_sum.astype(BF)
    grad_mixed = matmul_back(grad_low, outward[...]).astype(BF)
    grad_projected = jnp.concatenate(attend_back(*thirds(projected), chances, grad_mixed), 1)
    pairs = ((tokens, grad_projected), (mixed, grad_low))
    return pairs, grad_sum + matmul_back(grad_projected, inward[...])


def decoder_self_body(room, packet):
    either = room.either
    (inward, outward), grad_inputs = self_back(
        room.d_grad0[...],
        room.decoder_inward,
        room.decoder_outward,
        either(room.far_tokens, room.near_tokens),
        either(room.far_projected, room.near_projected),
        either(room.far_chances, room.near_chances),
        either(room.far_mixed, room.near_mixed),
    )
    packet.stash(decoder_inward=inward, decoder_outward=outward)
    room.d_inputs[...] = grad_inputs.astype(BF)


def encoder_back_body(room, packet):
    gain = room.encoder_gain
    grad_sum, gain1, shift1 = norm_back(
        room.grad_memory[...].astype(F32), room.e_unit1[...], room.e_scale1[:, :1], gain[1:2]
    )
    grad_low = grad_sum.astype(BF)
    grad_before = widen_backward(grad_low, room.encoder_narrow, room.e_slope)
    packet.stash(
        encoder_narrow=(room.e_hidden[...], grad_low), encoder_widen=(room.e_low[...], grad_before)
    )
    grad_normed = grad_sum + matmul_back(grad_before, room.encoder_widen[...])
    either = room.either
    grad_sum, gain0, shift0 = norm_back(
        grad_normed,
        either(room.near_unit, room.far_unit),
        either(room.near_scale, room.far_scale)[:, :1],
        gain[0:1],
    )
    inner, outer = room.d_small01[...], room.d_small2[...]
    small = jnp.concatenate(
        [gain0, gain1, shift0, shift1, inner[0:2], outer[0:1], inner[2:4], outer[1:2]]
        + [jnp.zeros((6, inner.shape[1]), F32)],
        0,
    )
    for place, tile in enumerate(tiles_of(small.astype(BF))):
        top = packet.left + packet.extra_at + 16 * place
        packet.send[top : top + 16] = tile
    (inward, outward), grad_inputs = self_back(
        grad_sum,
        room.encoder_inward,
        room.encoder_outward,
        either(room.near_tokens, room.far_tokens),
        either(room.near_projected, room.far_projected),
        either(room.near_chances, room.far_chances),
        either(room.near_mixed, room.far_mixed),
    )
    packet.stash(encoder_inward=inward, encoder_outward=outward)
    here, there = grad_inputs.astype(BF), room.d_inputs[...]
    room.sides_mine[0] = either(room.memory, room.output)
    room.sides_mine[1] = jnp.where(room.section == 0, here, there)
    room.sides_theirs[0] = either(room.output, room.memory)
    room.sides_theirs[1] = jnp.where(room.section == 0, there, here)


class Line:
    def __init__(self):
        self.last = None

    def after(self, *values):
        if self.last is None:
            return values
        return lax.optimization_barrier((values, self.last))[0]

    def mark(self, value):
        self.last = value


def pair_swap(value, axis, apart):
    count = lax.axis_size(axis)
    return lax.ppermute(value, axis, [(i, i ^ apart) for i in range(count)])


def halve(kept, came, following, span):
    count, height = kept.shape[0] // 2, kept.shape[1]
    half = pltpu.VMEM((count, height, SLAB), BF)

    def kernel(kept_ref, came_ref, kept_out, sent_out):
        section, row = lax.axis_index("section"), lax.axis_index("rows")
        bits = [bit_of(step, section, row) for step in following]
        mine = jnp.where(row & 1 == 0, bits[0], bits[1])
        for which, out in ((1 - mine, sent_out), (mine, kept_out)):
            part = pl.ds(which * count, count)
            out[...] = (kept_ref[part].astype(F32) + came_ref[part].astype(F32)).astype(BF)

    return pl.pallas_call(
        kernel,
        out_shape=[half, half],
        in_specs=[VMEM] * 2,
        out_specs=[VMEM] * 2,
        compiler_params=pltpu.CompilerParams(vmem_limit_bytes=2 << 20),
        cost_estimate=lasting(span),
    )(pinned(kept), pinned(came))


class Team:
    def __init__(self, line, orders, small=False, **weights):
        self.line, self.orders, self.small = line, orders, small
        self.shapes = {name: array.shape for name, array in weights.items()}
        self.even = lax.axis_size("rows") == GROUPS
        self.turn = 0
        self.done = {}

    def grads(self, *parcels):
        tied = self.line.after(*(parts for unused, parts in parcels))
        parcels = [(packet, *parts) for (packet, unused), parts in zip(parcels, tied)]
        self.kept, self.sent = weight_grads(
            parcels, list(self.shapes), self.orders, self.even, self.small
        )
        self.line.mark(self.sent)
        if self.even:
            self.go()

    def go(self):
        pieces = lax.axis_size("rows")
        route = []
        for device in range(2 * pieces):
            step = self.orders[device & 1][self.turn]
            route.append((device, device ^ (pieces if step == SIDE else 1 << step)))
        self.came = lax.ppermute(self.sent, ("section", "rows"), route)

    def step(self, span=2):
        if not self.even:
            return
        self.turn += 1
        kept, came = self.line.after(self.kept, self.came)
        following = [order[self.turn] for order in self.orders]
        self.kept, self.sent = halve(kept, came, following, span)
        self.line.mark(self.sent)
        self.go()

    def end(self):
        pieces = lax.axis_size("rows")
        if not self.even:
            return self.end_uneven()
        kept, came = self.line.after(self.kept, self.came)
        shapes = list(self.shapes.values())
        outs = [jax.ShapeDtypeStruct((depth // pieces, width // 2), F32) for depth, width in shapes]
        counts = (2, 2, 3, 3) if self.small else ()
        lanes = 512 // pieces
        outs += [jax.ShapeDtypeStruct((count, lanes), F32) for count in counts]

        def kernel(kept_ref, came_ref, *out_refs):
            top = 0
            for (depth, width), out_ref in zip(shapes, out_refs):
                share = depth // pieces
                for at in range(0, width // 2, SLAB):
                    rows = slice(top, top + share)
                    out_ref[:, at : at + SLAB] = kept_ref[0, rows].astype(F32) + came_ref[
                        0, rows
                    ].astype(F32)
                    top += share
            if counts:
                rows = slice(top, top + 16)
                total = kept_ref[0, rows].astype(F32) + came_ref[0, rows].astype(F32)
                top = 0
                for count, out_ref in zip(counts, out_refs[len(shapes) :]):
                    out_ref[...] = total[top : top + count, :lanes]
                    top += count

        results = pl.pallas_call(
            kernel,
            out_shape=outs,
            in_specs=[VMEM] * 2,
            out_specs=[VMEM] * len(outs),
            compiler_params=pltpu.CompilerParams(vmem_limit_bytes=2 << 20),
            cost_estimate=lasting(1.6),
        )(pinned(kept), pinned(came))
        self.line.mark(results[0])
        self.done = dict(zip(self.shapes, results))
        self.shares = results[len(shapes) :]

    def spread(self, top, count, share):
        core = lax.axis_index("rows") & 1
        both = jnp.stack([self.kept, self.sent])[:, :, top : top + count * share].astype(F32)
        both = both.reshape(2, 2, 2, 2, count, share, SLAB)
        both = both.transpose(0, 3, 2, 1, 5, 4, 6)
        both = both.reshape(2, GROUPS // 2, 1, share, count * SLAB)
        held = jnp.concatenate([both * (core == 0), both * (core == 1)], 2)
        return held.reshape(2, GROUPS, share, count * SLAB)

    def end_uneven(self):
        pieces = lax.axis_size("rows")
        top = 0
        for name, (depth, width) in self.shapes.items():
            share, count = depth // GROUPS, width // (2 * SLAB)
            part = self.spread(top, count, share).reshape(2, depth, width // 2)
            part = lax.psum_scatter(part, "rows", scatter_dimension=1, tiled=True)
            self.done[name] = lax.psum_scatter(part, "section", scatter_dimension=0, tiled=True)[0]
            top += count * share
        if self.small:
            width = 512
            part = self.spread(top, 1, 16)[0, :, :10, : width // GROUPS]
            part = lax.psum(jnp.moveaxis(part, 1, 0).reshape(10, width), ("section", "rows"))
            start = lax.axis_index("rows") * (width // pieces)
            part = lax.dynamic_slice_in_dim(part, start, width // pieces, 1)
            self.shares = (part[0:2], part[2:4], part[4:7], part[7:10])


SIDE = 0
XYZ, YXZ = (SIDE, 1, 2, 3), (1, SIDE, 2, 3)
XZY, YZX = (SIDE, 2, 3, 1), (1, 2, 3, SIDE)
ZXY, ZYX = (2, 3, SIDE, 1), (2, 3, 1, SIDE)


def per_device(
    section_input,
    segments,
    cotangent,
    encoder_inward,
    encoder_outward,
    encoder_widen,
    encoder_narrow,
    encoder_gain,
    encoder_shift,
    decoder_inward,
    decoder_outward,
    decoder_cross_query,
    decoder_cross_memory,
    decoder_cross_outward,
    decoder_widen,
    decoder_narrow,
    decoder_gain,
    decoder_shift,
):
    section = lax.axis_index("section")
    own = section_input[0]
    length, width = own.shape[1:]
    wide = encoder_widen.shape[1]

    def low(*shape):
        return jax.ShapeDtypeStruct(shape, BF)

    def full(*shape):
        return jax.ShapeDtypeStruct(shape, F32)

    slabs, units, scales = low(length, width), full(length, width), full(length, LANES)
    chances = full(width // SLAB, PER_SLAB * length, length)
    attended = dict(
        projected=low(length, 3 * width), chances=chances, mixed=slabs, unit=units, scale=scales
    )
    line = Line()

    def run(body, inputs, near, outputs, loads, span, limit, packet=None, extra=None, away=None, late=None):
        near = dict(near)
        for name in list(near)[:1]:
            (near[name],) = line.after(near[name])
        kept, leaving = call(
            body if packet is None else (lambda room: body(room, packet)),
            inputs,
            near,
            outputs,
            loads,
            span,
            limit,
            packet,
            extra,
            away,
            late,
        )
        line.mark(list(vars(kept).values())[0])
        if packet is None:
            return kept
        return kept, leaving + (pair_swap(leaving[1], "rows", 1),)

    other = pair_swap(
        lax.dynamic_index_in_dim(own, 1 - section, 0, keepdims=False), "section", 1
    )
    near = run(
        own_body,
        dict(
            segments=segments,
            tokens=Entry(own),
            inward=Either(encoder_inward, decoder_inward),
            encoder_gain=encoder_gain,
            encoder_shift=encoder_shift,
            decoder_gain=decoder_gain,
            decoder_shift=decoder_shift,
            outward=Either(encoder_outward, decoder_outward),
        ),
        {},
        {},
        dict(
            other_inward=Either(decoder_inward, encoder_inward),
            other_outward=Either(decoder_outward, encoder_outward),
        ),
        4,
        6,
        away=dict(first=units, **attended),
    )

    wide_packet = Packet(decoder_narrow=decoder_narrow, decoder_widen=decoder_widen)
    far, d_wide = run(
        forward_body,
        dict(
            segments=segments,
            encoder_shift=encoder_shift,
            decoder_shift=decoder_shift,
            own_first=near.first,
        ),
        dict(
            tokens=other,
            inward=near.other_inward,
            outward=near.other_outward,
        ),
        dict(
            memory=slabs,
            output=slabs,
            **attended,
            e_low=slabs,
            e_hidden=low(length, wide),
            e_slope=full(length, wide),
            e_unit1=units,
            e_scale1=scales,
            d_low=slabs,
            c_query=slabs,
            c_paired=low(length, 2 * width),
            c_chances=chances,
            c_mixed=slabs,
            d_unit1=units,
            d_scale1=scales,
            d_grad=units,
            d_small2=full(2, width),
        ),
        dict(
            encoder_gain=encoder_gain,
            decoder_gain=decoder_gain,
            encoder_widen=encoder_widen,
            encoder_narrow=encoder_narrow,
            decoder_cross_query=decoder_cross_query,
            decoder_cross_memory=decoder_cross_memory,
            decoder_cross_outward=decoder_cross_outward,
        ),
        11,
        14,
        wide_packet,
        dict(d_hidden=low(length, wide), d_slope=full(length, wide)),
        late=dict(
            decoder_widen=decoder_widen,
            decoder_narrow=decoder_narrow,
            cotangent=Entry(cotangent),
        ),
    )

    cross_packet = Packet(
        decoder_cross_query=decoder_cross_query,
        decoder_cross_memory=decoder_cross_memory,
        decoder_cross_outward=decoder_cross_outward,
    )
    crossed, d_cross = run(
        cross_back_body,
        dict(near_unit=near.unit, near_scale=near.scale),
        dict(
            d_grad=far.d_grad,
            decoder_gain=far.decoder_gain,
            d_unit1=far.d_unit1,
            d_scale1=far.d_scale1,
            c_query=far.c_query,
            c_paired=far.c_paired,
            c_chances=far.c_chances,
            d_low=far.d_low,
            memory=far.memory,
            c_mixed=far.c_mixed,
            decoder_cross_outward=far.decoder_cross_outward,
            decoder_cross_memory=far.decoder_cross_memory,
            decoder_cross_query=far.decoder_cross_query,
            far_unit=far.unit,
            far_scale=far.scale,
        ),
        dict(grad_memory=slabs, d_grad0=units, d_small01=full(4, width)),
        {},
        4.7,
        5,
        cross_packet,
    )

    def d_self_run():
        packet = Packet(decoder_inward=decoder_inward, decoder_outward=decoder_outward)
        return packet, *run(
            decoder_self_body,
            dict(
                decoder_outward=decoder_outward,
                near_projected=near.projected,
                near_chances=near.chances,
                near_tokens=Entry(own),
                near_mixed=near.mixed,
                decoder_inward=decoder_inward,
            ),
            dict(
                far_tokens=other,
                d_grad0=crossed.d_grad0,
                far_projected=far.projected,
                far_chances=far.chances,
                far_mixed=far.mixed,
            ),
            dict(d_inputs=slabs),
            {},
            5,
            5,
            packet,
        )

    def encoder_run(d_inputs):
        packet = Packet(
            64,
            encoder_narrow=encoder_narrow,
            encoder_widen=encoder_widen,
            encoder_inward=encoder_inward,
            encoder_outward=encoder_outward,
        )
        sides = low(2, length, width)
        return packet, *run(
            encoder_back_body,
            dict(
                near_unit=near.unit,
                near_scale=near.scale,
                near_projected=near.projected,
                near_chances=near.chances,
                near_tokens=Entry(own),
                near_mixed=near.mixed,
                encoder_outward=encoder_outward,
                encoder_inward=encoder_inward,
            ),
            dict(
                far_tokens=other,
                encoder_gain=far.encoder_gain,
                grad_memory=crossed.grad_memory,
                e_unit1=far.e_unit1,
                e_scale1=far.e_scale1,
                encoder_narrow=far.encoder_narrow,
                e_slope=far.e_slope,
                e_hidden=far.e_hidden,
                e_low=far.e_low,
                encoder_widen=far.encoder_widen,
                d_small01=crossed.d_small01,
                d_small2=far.d_small2,
                far_unit=far.unit,
                far_scale=far.scale,
                far_projected=far.projected,
                far_chances=far.chances,
                far_mixed=far.mixed,
                d_inputs=d_inputs,
                memory=far.memory,
                output=far.output,
            ),
            dict(sides_mine=sides, sides_theirs=sides),
            {},
            8,
            8,
            packet,
        )

    team_w = Team(
        line,
        (YZX, ZXY),
        False,
        decoder_narrow=decoder_narrow,
        decoder_widen=decoder_widen,
    )
    team_q = Team(
        line,
        (XYZ, XYZ),
        False,
        decoder_cross_query=decoder_cross_query,
        decoder_cross_memory=decoder_cross_memory,
        decoder_cross_outward=decoder_cross_outward,
    )
    team_r = Team(
        line,
        (XZY, YZX),
        False,
        decoder_inward=decoder_inward,
        decoder_outward=decoder_outward,
    )
    team_e = Team(
        line,
        (XYZ, YXZ),
        False,
        encoder_narrow=encoder_narrow,
        encoder_widen=encoder_widen,
    )
    team_s = Team(
        line,
        (YXZ, XZY),
        True,
        encoder_inward=encoder_inward,
        encoder_outward=encoder_outward,
    )
    team_w.grads((wide_packet, d_wide))
    team_q.grads((cross_packet, d_cross))
    self_packet, turned, d_self = d_self_run()
    encoder_packet, ended, e_all = encoder_run(turned.d_inputs)
    team_r.grads((self_packet, d_self))
    team_s.grads((encoder_packet, e_all))
    team_w.step()
    team_e.grads((encoder_packet, e_all))
    team_q.step()
    team_r.step()
    team_w.step()
    team_s.step()
    team_q.step()
    team_r.step()
    team_e.step()
    team_q.step()
    team_s.step()
    (theirs,) = line.after(ended.sides_theirs)
    theirs = pair_swap(theirs, "section", 1)
    team_w.step()
    team_e.step()
    team_q.end()
    team_s.step()
    team_r.step()
    team_e.step()
    team_w.end()
    mine, theirs = line.after(ended.sides_mine, theirs)
    results, gradients = (
        jnp.stack(
            [
                jnp.where(section == 0, mine[i], theirs[i]),
                jnp.where(section == 0, theirs[i], mine[i]),
            ]
        )[None]
        for i in (0, 1)
    )
    line.mark(gradients)
    team_s.end()
    team_r.end()
    team_e.end()

    done = {}
    for team in (team_w, team_q, team_r, team_e, team_s):
        done.update(team.done)
    deltas = SimpleNamespace(**done)
    shares = team_s.shares
    return (
        results,
        gradients,
        deltas.encoder_inward,
        deltas.encoder_outward,
        deltas.encoder_widen,
        deltas.encoder_narrow,
        shares[0],
        shares[1],
        deltas.decoder_inward,
        deltas.decoder_outward,
        deltas.decoder_cross_query,
        deltas.decoder_cross_memory,
        deltas.decoder_cross_outward,
        deltas.decoder_widen,
        deltas.decoder_narrow,
        shares[2],
        shares[3],
    )


def solution(mesh):
    weights = (P(),) * 15
    shares = P("rows", "section")
    small = P(None, "rows")
    sides = P("section", None, "rows", None)
    return jax.shard_map(
        per_device,
        mesh=mesh,
        in_specs=(sides, P(None, None, "rows", None), P(None, "rows", None)) + weights,
        out_specs=(sides, sides)
        + (shares,) * 4
        + (small,) * 2
        + (shares,) * 7
        + (small,) * 2,
        check_vma=False,
    )
```

```python
import math
from types import SimpleNamespace
from types import SimpleNamespace
from types import SimpleNamespace

import jax
import jax.numpy as jnp
from jax import lax
from jax.experimental import pallas as pl
from jax.experimental.pallas import tpu as pltpu
from jax.sharding import PartitionSpec as P

HEADS = 8
HEAD_DIM = 64
NEG = -1e30
EPS = 1e-05
GROUPS = 16
SLAB = 256
LANES = 128
BF = jnp.bfloat16
F32 = jnp.float32
def lasting(span):
    return pl.CostEstimate(flops=int(span * 5.5e9), bytes_accessed=1, transcendentals=0)


FACTOR = 1.0 / math.sqrt(HEAD_DIM)
HBM = pl.BlockSpec(memory_space=pltpu.HBM)
VMEM = pl.BlockSpec(memory_space=pltpu.VMEM)


def matmul(left, right):
    return lax.dot_general(left, right, (((1,), (0,)), ((), ())), preferred_element_type=F32)


def matmul_back(grad, weight):
    return lax.dot_general(grad, weight, (((1,), (1,)), ((), ())), preferred_element_type=F32)


def matmul_across(left, grad):
    return lax.dot_general(left, grad, (((0,), (0,)), ((), ())), preferred_element_type=F32)


def norm(summed, gain, shift):
    center = jnp.mean(summed, -1, keepdims=True)
    centered = summed - center
    spread = jnp.mean(centered * centered, -1, keepdims=True)
    scale = lax.rsqrt(spread + EPS)
    unit = centered * scale
    return unit * gain + shift, unit, scale


def norm_back(grad, unit, scale, gain):
    grad_gain = jnp.sum(grad * unit, 0, keepdims=True)
    grad_shift = jnp.sum(grad, 0, keepdims=True)
    inner = grad * gain
    center = jnp.mean(inner, -1, keepdims=True)
    along = jnp.mean(inner * unit, -1, keepdims=True)
    return scale * (inner - center - unit * along), grad_gain, grad_shift


def gelu_both(before):
    root = math.sqrt(2.0 / math.pi)
    square = before * before
    half = 0.5 + 0.5 * jnp.tanh(before * (root + root * 0.044715 * square))
    steep = 2 * root + 6 * root * 0.044715 * square
    return before * half, half * (1.0 + before * (1.0 - half) * steep)


def pair_marks():
    lane = lax.broadcasted_iota(jnp.int32, (1, LANES), 1) // HEAD_DIM
    return [(lane == h).astype(F32).astype(BF) for h in (0, 1)]


def join_pairs(parts):
    lane = lax.broadcasted_iota(jnp.int32, (1, LANES), 1) // HEAD_DIM
    pairs = zip(parts[0::2], parts[1::2])
    return jnp.concatenate([jnp.where(lane == 0, one, two) for one, two in pairs], 1)


def attend(query, keys, values, allowed, chances_ref):
    marks = pair_marks()
    query_down, values_down = query.T, values.T
    scores = []
    for head in range(HEADS):
        at = slice(head // 2 * LANES, (head // 2 + 1) * LANES)
        scores.append(matmul(keys[:, at] * marks[head % 2], query_down[at]))
    scores = [jnp.where(allowed, item * FACTOR, NEG) for item in scores]
    weights = [jnp.exp(item - jnp.max(item, 0, keepdims=True)) for item in scores]
    chances = [item * (1.0 / jnp.sum(item, 0, keepdims=True)) for item in weights]
    mixed = []
    for head, item in enumerate(chances):
        chances_ref[head] = item
        at = slice(head * HEAD_DIM, (head + 1) * HEAD_DIM)
        mixed.append(matmul(values_down[at], item.astype(BF)).astype(BF))
    return jnp.concatenate(mixed, 0).T


def attend_back(query, keys, values, chances_ref, grad_mixed):
    marks = pair_marks()
    grad_down, keys_down = grad_mixed.T, keys.T
    pairs = [slice(head // 2 * LANES, (head // 2 + 1) * LANES) for head in range(HEADS)]
    chances = [chances_ref[head] for head in range(HEADS)]
    grad_chances = [
        matmul(values[:, at] * marks[head % 2], grad_down[at]) for head, at in enumerate(pairs)
    ]
    grad_values = [matmul(item.astype(BF), grad_mixed[:, at]) for item, at in zip(chances, pairs)]
    held = [jnp.sum(one * two, 0, keepdims=True) for one, two in zip(chances, grad_chances)]
    grad_scores = [
        (one * (two - total)).astype(BF) for one, two, total in zip(chances, grad_chances, held)
    ]
    grad_keys = [matmul(item, query[:, at]) for item, at in zip(grad_scores, pairs)]
    grad_query = [
        matmul(keys_down[head * HEAD_DIM : (head + 1) * HEAD_DIM], item)
        for head, item in enumerate(grad_scores)
    ]
    turned = (jnp.concatenate(grad_query, 0) * FACTOR).astype(BF).T
    return [
        turned,
        (join_pairs(grad_keys) * FACTOR).astype(BF),
        join_pairs(grad_values).astype(BF),
    ]


def tiles_of(array):
    return [array[:, at : at + LANES] for at in range(0, array.shape[1], LANES)]


class Entry:
    def __init__(self, array):
        self.arrays = (array,)
        self.shape, self.dtype = array.shape[1:], array.dtype

    def pieces(self, refs, section):
        return [(None, refs[0].at[section])]


class Either:
    def __init__(self, *pair):
        pair = [item if isinstance(item, tuple) else (item, None) for item in pair]
        self.arrays = tuple(array for array, unused in pair)
        self.entries = [entry for unused, entry in pair]
        first = self.arrays[0]
        self.shape = first.shape if self.entries[0] is None else first.shape[1:]
        self.dtype = first.dtype

    def pieces(self, refs, section):
        return [
            (here, ref if entry is None else ref.at[entry])
            for here, (ref, entry) in enumerate(zip(refs, self.entries))
        ]


class Whole:
    def __init__(self, array):
        self.arrays = (array,)
        self.shape, self.dtype = array.shape, array.dtype

    def pieces(self, refs, section):
        return [(None, refs[0])]


class Room:
    def __init__(self, inputs, sources, held, sems, away):
        self.inputs, self.sources, self.held, self.sems = inputs, sources, held, sems
        self.away, self.left = away, {}
        self.section = lax.axis_index("section")
        self.core = lax.axis_index("rows") & 1
        self.arrived = set()
        for place, name in enumerate(inputs):
            for here, source in inputs[name].pieces(sources[name], self.section):
                copy = pltpu.make_async_copy(source, held[name], sems.at[place])
                if here is None:
                    copy.start()
                else:
                    pl.when(self.section == here)(copy.start)

    def __getattr__(self, name):
        if name in self.inputs and name not in self.arrived:
            self.arrived.add(name)
            place = list(self.inputs).index(name)
            source = self.inputs[name].pieces(self.sources[name], self.section)[0][1]
            pltpu.make_async_copy(source, self.held[name], self.sems.at[place]).wait()
        return self.held[name]

    def leave(self, *names):
        for name, (target, sem) in self.away.items():
            if name in names:
                copy = pltpu.make_async_copy(self.held[name], target, sem)
                copy.start()
                self.left[name] = copy

    def finish(self):
        self.leave(*(name for name in self.away if name not in self.left))
        for name in self.inputs:
            getattr(self, name)
        for copy in self.left.values():
            copy.wait()

    def either(self, here, there):
        return jnp.where(self.section == 0, here[...], there[...])


class Packet:
    def __init__(self, extra=0, **weights):
        self.shapes = {name: array.shape for name, array in weights.items()}
        self.left_at, self.grad_at = {}, {}
        left = grad = 0
        for name, (depth, width) in self.shapes.items():
            self.left_at[name], self.grad_at[name] = left, grad
            left, grad = left + depth // 2, grad + width
        self.left, self.extra_at, self.grad = left, grad, grad + extra

    def leaving(self):
        return [
            pltpu.VMEM((self.left, LANES), BF),
            pltpu.VMEM((self.left + self.grad, LANES), BF),
        ]

    def bind(self, room, refs):
        self.room, (self.keep, self.send) = room, refs

    def stash(self, **operands):
        even = self.room.core == 0
        for name, (left, grad) in operands.items():
            depth, width = self.shapes[name]
            block = depth // GROUPS
            across = left.T
            for group in range(0, GROUPS, 2):
                first = across[group * block : (group + 1) * block]
                second = across[(group + 1) * block : (group + 2) * block]
                top = self.left_at[name] + group // 2 * block
                self.keep[top : top + block] = jnp.where(even, first, second)
                self.send[top : top + block] = jnp.where(even, second, first)
            for place, tile in enumerate(tiles_of(grad)):
                top = self.left + self.grad_at[name] + place * LANES
                self.send[top : top + LANES] = tile


def far_away(array):
    return pltpu.with_memory_space_constraint(array, pltpu.HBM)


def pinned(array):
    return pltpu.with_memory_space_constraint(array, pltpu.VMEM)


def call(body, inputs, near, outputs, loads, span, limit, packet=None, extra=None, away=None, late=None):
    extra, away = extra or {}, away or {}
    inputs = {
        name: item if hasattr(item, "pieces") else Whole(item) for name, item in inputs.items()
    }
    loads = {name: item if hasattr(item, "pieces") else Whole(item) for name, item in loads.items()}
    inputs.update(loads)
    inputs.update({name: item if hasattr(item, "pieces") else Whole(item) for name, item in (late or {}).items()})
    arrays = [array for item in inputs.values() for array in item.arrays]
    outputs = {
        **outputs,
        **{name: jax.ShapeDtypeStruct(item.shape, item.dtype) for name, item in loads.items()},
    }
    shapes_out = [pltpu.VMEM(item.shape, item.dtype) for item in outputs.values()]
    shapes_out += packet.leaving() if packet else []
    shapes_out += [pltpu.HBM(item.shape, item.dtype) for item in away.values()]
    brought = [name for name in inputs if name not in loads]

    def kernel(*refs):
        refs = list(refs)

        def take(count):
            taken = refs[:count]
            del refs[:count]
            return taken

        sources = {name: take(len(item.arrays)) for name, item in inputs.items()}
        held = dict(zip(near, take(len(near))))
        held.update(zip(outputs, take(len(outputs))))
        leaving = take(2) if packet else None
        targets = take(len(away))
        held.update(zip(brought, take(len(brought))))
        held.update(zip(extra, take(len(extra))))
        held.update(zip(away, take(len(away))))
        away_to = {
            name: (target, refs[1].at[place])
            for place, (name, target) in enumerate(zip(away, targets))
        }
        room = Room(inputs, sources, held, refs[0], away_to)
        if packet:
            packet.bind(room, leaving)
        body(room)
        room.finish()

    scratch = [inputs[name] for name in brought] + list(extra.values()) + list(away.values())
    results = pl.pallas_call(
        kernel,
        out_shape=shapes_out,
        in_specs=[HBM] * len(arrays) + [VMEM] * len(near),
        out_specs=[VMEM] * (len(shapes_out) - len(away)) + [HBM] * len(away),
        scratch_shapes=[pltpu.VMEM(item.shape, item.dtype) for item in scratch]
        + [pltpu.SemaphoreType.DMA((max(1, len(inputs)),))]
        + [pltpu.SemaphoreType.DMA((max(1, len(away)),))],
        compiler_params=pltpu.CompilerParams(vmem_limit_bytes=limit << 20),
        cost_estimate=lasting(span),
    )(*(far_away(item) for item in arrays), *(pinned(item) for item in near.values()))
    made = dict(zip(outputs, results))
    made.update(zip(away, results[len(results) - len(away) :]))
    leaving = tuple(results[len(outputs) : len(results) - len(away)])
    return SimpleNamespace(**made), leaving


def place_of(side, block, orders, core):
    spots = []
    for order in orders:
        spot = side * (8 >> order.index(SIDE))
        for bit in range(3):
            spot = spot + (block >> bit & 1) * (8 >> order.index(bit + 1))
        spots.append(spot)
    return jnp.where(core == 0, spots[0], spots[1])


def bit_of(step, section, row):
    return section if step == SIDE else (row >> step) & 1


def weight_grads(parcels, names, orders, even, small=False):
    parts = [
        (packet, which, name)
        for which, (packet, *unused) in enumerate(parcels)
        for name in packet.shapes
        if name in names
    ]
    height = sum(
        packet.shapes[name][0] // GROUPS * packet.shapes[name][1] // (2 * SLAB)
        for packet, unused, name in parts
    )
    small_at = height
    height += 16 if small else 0
    half = pltpu.VMEM((GROUPS // 2, height, SLAB), BF)

    def kernel(*refs):
        *operands, kept_out, sent_out, packed = refs
        row = lax.axis_index("rows")
        core = row & 1
        if even:
            first = [bit_of(order[0], lax.axis_index("section"), row) for order in orders]
            mine = jnp.where(core == 0, first[0], first[1])
        else:
            mine = 0

        base = 0
        for packet, which, name in parts:
            keep_ref, send_ref, came_ref = operands[3 * which : 3 * which + 3]
            depth, width = packet.shapes[name]
            block, half_pieces = depth // GROUPS, width // (2 * SLAB)
            left_at, grad_at = packet.left_at[name], packet.left + packet.grad_at[name]
            left = jnp.concatenate(
                [ref[left_at : left_at + depth // 2] for ref in (keep_ref, came_ref)], 1
            )
            for piece in range(width // SLAB):
                at = grad_at + piece * SLAB
                right = jnp.concatenate(
                    [
                        jnp.concatenate([ref[at : at + LANES], ref[at + LANES : at + 2 * LANES]], 1)
                        for ref in (send_ref, came_ref)
                    ],
                    0,
                )
                tile = matmul(left, right).astype(BF)
                side, offset = divmod(piece, half_pieces)
                top = base + offset * block
                for number in range(GROUPS // 2):
                    packed[place_of(side, number, orders, core), top : top + block] = tile[
                        number * block : (number + 1) * block
                    ]
            base += block * half_pieces
        if small:
            packet = parcels[0][0]
            at = packet.left + packet.extra_at
            total = sum(
                jnp.concatenate([ref[at + 16 * i : at + 16 * i + 16] for i in range(4)], 1).astype(F32)
                for ref in operands[1:3]
            )
            width = total.shape[1]
            share = width // GROUPS
            for number in range(GROUPS // 2):
                turned = [
                    pltpu.roll(total, (width - (2 * number + i) * share) % width, 1) for i in (0, 1)
                ]
                part = jnp.where(core == 0, turned[0], turned[1])[:, :SLAB].astype(BF)
                for side in (0, 1):
                    packed[place_of(side, number, orders, core), small_at : small_at + 16] = part
        count = GROUPS // 2
        sent_out[...] = packed[pl.ds((1 - mine) * count, count)]
        kept_out[...] = packed[pl.ds(mine * count, count)]

    arrays = [array for unused, *rest in parcels for array in rest]
    return pl.pallas_call(
        kernel,
        out_shape=[half, half],
        in_specs=[VMEM] * len(arrays),
        out_specs=[VMEM] * 2,
        scratch_shapes=[pltpu.VMEM((GROUPS, height, SLAB), BF)],
        compiler_params=pltpu.CompilerParams(vmem_limit_bytes=8 << 20),
        cost_estimate=lasting(3.5),
    )(*(pinned(item) for item in arrays))


def equal_ids(row_ids, column_ids):
    length = row_ids.shape[1]
    down = jnp.broadcast_to(row_ids.astype(F32), (length, length)).T
    return down == jnp.broadcast_to(column_ids.astype(F32), (length, length))


def scale_out(scale):
    return jnp.broadcast_to(scale, (scale.shape[0], LANES))


def thirds(projected):
    width = projected.shape[1] // 3
    return [projected[:, i * width : (i + 1) * width] for i in range(3)]


def self_part(room, tokens, ids, causal, inward, outward, gain, shift):
    room.projected[...] = matmul(tokens, inward[...]).astype(BF)
    room.leave("projected")
    length = tokens.shape[0]
    rows = lax.broadcasted_iota(jnp.int32, (length, length), 0)
    columns = lax.broadcasted_iota(jnp.int32, (length, length), 1)
    reach = jnp.where(causal, 0, length)
    allowed = equal_ids(ids, ids) & (columns + reach >= rows)
    mixed = attend(*thirds(room.projected), allowed, room.chances)
    room.mixed[...] = mixed
    room.leave("chances", "mixed")
    summed = tokens.astype(F32) + matmul(mixed, outward[...])
    first, unit, scale = norm(summed, gain, shift)
    room.unit[...] = unit
    room.scale[...] = scale_out(scale)
    return first


def own_body(room):
    section = room.section
    ids = room.segments[pl.ds(section, 1), pl.ds(section, 1), 0, :][0]
    gain = jnp.where(section == 0, room.encoder_gain[0:1], room.decoder_gain[0:1])
    shift = jnp.where(section == 0, room.encoder_shift[0:1], room.decoder_shift[0:1])
    room.first[...] = self_part(
        room, room.tokens[...], ids, section == 1, room.inward, room.outward, gain, shift
    )


def forward_body(room, packet):
    section = room.section
    source_ids = room.segments[0, pl.ds(section, 1), 0, :]
    target_ids = room.segments[1, pl.ds(section, 1), 0, :]
    ids = jnp.where(section == 0, target_ids, source_ids)
    gain = jnp.where(section == 0, room.decoder_gain[0:1], room.encoder_gain[0:1])
    shift = jnp.where(section == 0, room.decoder_shift[0:1], room.encoder_shift[0:1])
    other = self_part(
        room, room.tokens[...], ids, section == 0, room.inward, room.outward, gain, shift
    )
    own = room.own_first[...]

    first = jnp.where(section == 0, own, other)
    low = first.astype(BF)
    widen_forward(low, room.encoder_widen, room.e_hidden, room.e_slope)
    room.e_low[...] = low
    summed = first + matmul(room.e_hidden[...], room.encoder_narrow[...])
    result, unit, scale = norm(summed, room.encoder_gain[1:2], room.encoder_shift[1:2])
    memory = result.astype(BF)
    room.e_unit1[...] = unit
    room.e_scale1[...] = scale_out(scale)
    room.memory[...] = memory

    first = jnp.where(section == 0, other, own)
    low = first.astype(BF)
    query = matmul(low, room.decoder_cross_query[...]).astype(BF)
    paired = matmul(memory, room.decoder_cross_memory[...]).astype(BF)
    room.d_low[...] = low
    room.c_query[...] = query
    room.c_paired[...] = paired
    width = query.shape[1]
    mixed = attend(
        query,
        room.c_paired[:, :width],
        room.c_paired[:, width:],
        equal_ids(source_ids, target_ids),
        room.c_chances,
    )
    room.c_mixed[...] = mixed
    summed = first + matmul(mixed, room.decoder_cross_outward[...])
    second, unit, scale = norm(summed, room.decoder_gain[1:2], room.decoder_shift[1:2])
    room.d_unit1[...] = unit
    room.d_scale1[...] = scale_out(scale)

    low = second.astype(BF)
    widen_forward(low, room.decoder_widen, room.d_hidden, room.d_slope)
    summed = second + matmul(room.d_hidden[...], room.decoder_narrow[...])
    gain = room.decoder_gain[2:3]
    result, unit, scale = norm(summed, gain, room.decoder_shift[2:3])
    room.output[...] = result.astype(BF)

    grad_sum, grad_gain, grad_shift = norm_back(
        room.cotangent[...].astype(F32), unit, scale, gain
    )
    grad_low = grad_sum.astype(BF)
    grad_before = widen_backward(grad_low, room.decoder_narrow, room.d_slope)
    packet.stash(
        decoder_narrow=(room.d_hidden[...], grad_low), decoder_widen=(low, grad_before)
    )
    room.d_grad[...] = grad_sum + matmul_back(grad_before, room.decoder_widen[...])
    room.d_small2[...] = jnp.concatenate([grad_gain, grad_shift], 0)


def widen_forward(low, widen_ref, hidden_ref, slope_ref):
    step = 512
    for at in range(0, widen_ref.shape[1], step):
        hidden, slope = gelu_both(matmul(low, widen_ref[:, at : at + step]))
        hidden_ref[:, at : at + step] = hidden.astype(BF)
        slope_ref[:, at : at + step] = slope


def widen_backward(grad_low, narrow_ref, slope_ref):
    step = 512
    parts = []
    for at in range(0, narrow_ref.shape[0], step):
        grad_hidden = matmul_back(grad_low, narrow_ref[at : at + step])
        parts.append((grad_hidden * slope_ref[:, at : at + step]).astype(BF))
    return jnp.concatenate(parts, 1)


def cross_back_body(room, packet):
    gain = room.decoder_gain
    grad_sum, gain1, shift1 = norm_back(
        room.d_grad[...], room.d_unit1[...], room.d_scale1[:, :1], gain[1:2]
    )
    grad_low = grad_sum.astype(BF)
    grad_mixed = matmul_back(grad_low, room.decoder_cross_outward[...]).astype(BF)
    paired = room.c_paired
    query = room.c_query[...]
    width = query.shape[1]
    grad_query, grad_keys, grad_values = attend_back(
        query, paired[:, :width], paired[:, width:], room.c_chances, grad_mixed
    )
    grad_paired = jnp.concatenate([grad_keys, grad_values], 1)
    packet.stash(
        decoder_cross_query=(room.d_low[...], grad_query),
        decoder_cross_memory=(room.memory[...], grad_paired),
        decoder_cross_outward=(room.c_mixed[...], grad_low),
    )
    room.grad_memory[...] = matmul_back(grad_paired, room.decoder_cross_memory[...]).astype(BF)
    grad_normed = grad_sum + matmul_back(grad_query, room.decoder_cross_query[...])
    grad_sum, gain0, shift0 = norm_back(
        grad_normed,
        room.either(room.far_unit, room.near_unit),
        room.either(room.far_scale, room.near_scale)[:, :1],
        gain[0:1],
    )
    room.d_grad0[...] = grad_sum
    room.d_small01[...] = jnp.concatenate([gain0, gain1, shift0, shift1], 0)


def self_back(grad_sum, inward, outward, tokens, projected, chances, mixed):
    grad_low = grad_sum.astype(BF)
    grad_mixed = matmul_back(grad_low, outward[...]).astype(BF)
    grad_projected = jnp.concatenate(attend_back(*thirds(projected), chances, grad_mixed), 1)
    pairs = ((tokens, grad_projected), (mixed, grad_low))
    return pairs, grad_sum + matmul_back(grad_projected, inward[...])


def decoder_self_body(room, packet):
    either = room.either
    (inward, outward), grad_inputs = self_back(
        room.d_grad0[...],
        room.decoder_inward,
        room.decoder_outward,
        either(room.far_tokens, room.near_tokens),
        either(room.far_projected, room.near_projected),
        either(room.far_chances, room.near_chances),
        either(room.far_mixed, room.near_mixed),
    )
    packet.stash(decoder_inward=inward, decoder_outward=outward)
    room.d_inputs[...] = grad_inputs.astype(BF)


def encoder_back_body(room, packet):
    gain = room.encoder_gain
    grad_sum, gain1, shift1 = norm_back(
        room.grad_memory[...].astype(F32), room.e_unit1[...], room.e_scale1[:, :1], gain[1:2]
    )
    grad_low = grad_sum.astype(BF)
    grad_before = widen_backward(grad_low, room.encoder_narrow, room.e_slope)
    packet.stash(
        encoder_narrow=(room.e_hidden[...], grad_low), encoder_widen=(room.e_low[...], grad_before)
    )
    grad_normed = grad_sum + matmul_back(grad_before, room.encoder_widen[...])
    either = room.either
    grad_sum, gain0, shift0 = norm_back(
        grad_normed,
        either(room.near_unit, room.far_unit),
        either(room.near_scale, room.far_scale)[:, :1],
        gain[0:1],
    )
    inner, outer = room.d_small01[...], room.d_small2[...]
    small = jnp.concatenate(
        [gain0, gain1, shift0, shift1, inner[0:2], outer[0:1], inner[2:4], outer[1:2]]
        + [jnp.zeros((6, inner.shape[1]), F32)],
        0,
    )
    for place, tile in enumerate(tiles_of(small.astype(BF))):
        top = packet.left + packet.extra_at + 16 * place
        packet.send[top : top + 16] = tile
    (inward, outward), grad_inputs = self_back(
        grad_sum,
        room.encoder_inward,
        room.encoder_outward,
        either(room.near_tokens, room.far_tokens),
        either(room.near_projected, room.far_projected),
        either(room.near_chances, room.far_chances),
        either(room.near_mixed, room.far_mixed),
    )
    packet.stash(encoder_inward=inward, encoder_outward=outward)
    here, there = grad_inputs.astype(BF), room.d_inputs[...]
    room.sides_mine[0] = either(room.memory, room.output)
    room.sides_mine[1] = jnp.where(room.section == 0, here, there)
    room.sides_theirs[0] = either(room.output, room.memory)
    room.sides_theirs[1] = jnp.where(room.section == 0, there, here)


class Line:
    def __init__(self):
        self.last = None

    def after(self, *values):
        if self.last is None:
            return values
        return lax.optimization_barrier((values, self.last))[0]

    def mark(self, value):
        self.last = value


def pair_swap(value, axis, apart):
    count = lax.axis_size(axis)
    return lax.ppermute(value, axis, [(i, i ^ apart) for i in range(count)])


def halve(kept, came, following, span):
    count, height = kept.shape[0] // 2, kept.shape[1]
    half = pltpu.VMEM((count, height, SLAB), BF)

    def kernel(kept_ref, came_ref, kept_out, sent_out):
        section, row = lax.axis_index("section"), lax.axis_index("rows")
        bits = [bit_of(step, section, row) for step in following]
        mine = jnp.where(row & 1 == 0, bits[0], bits[1])
        for which, out in ((1 - mine, sent_out), (mine, kept_out)):
            part = pl.ds(which * count, count)
            out[...] = (kept_ref[part].astype(F32) + came_ref[part].astype(F32)).astype(BF)

    return pl.pallas_call(
        kernel,
        out_shape=[half, half],
        in_specs=[VMEM] * 2,
        out_specs=[VMEM] * 2,
        compiler_params=pltpu.CompilerParams(vmem_limit_bytes=2 << 20),
        cost_estimate=lasting(span),
    )(pinned(kept), pinned(came))


class Team:
    def __init__(self, line, orders, small=False, **weights):
        self.line, self.orders, self.small = line, orders, small
        self.shapes = {name: array.shape for name, array in weights.items()}
        self.even = lax.axis_size("rows") == GROUPS
        self.turn = 0
        self.done = {}

    def grads(self, *parcels):
        tied = self.line.after(*(parts for unused, parts in parcels))
        parcels = [(packet, *parts) for (packet, unused), parts in zip(parcels, tied)]
        self.kept, self.sent = weight_grads(
            parcels, list(self.shapes), self.orders, self.even, self.small
        )
        self.line.mark(self.sent)
        if self.even:
            self.go()

    def go(self):
        pieces = lax.axis_size("rows")
        route = []
        for device in range(2 * pieces):
            step = self.orders[device & 1][self.turn]
            route.append((device, device ^ (pieces if step == SIDE else 1 << step)))
        self.came = lax.ppermute(self.sent, ("section", "rows"), route)

    def step(self, span=2):
        if not self.even:
            return
        self.turn += 1
        kept, came = self.line.after(self.kept, self.came)
        following = [order[self.turn] for order in self.orders]
        self.kept, self.sent = halve(kept, came, following, span)
        self.line.mark(self.sent)
        self.go()

    def end(self):
        pieces = lax.axis_size("rows")
        if not self.even:
            return self.end_uneven()
        kept, came = self.line.after(self.kept, self.came)
        shapes = list(self.shapes.values())
        outs = [jax.ShapeDtypeStruct((depth // pieces, width // 2), F32) for depth, width in shapes]
        counts = (2, 2, 3, 3) if self.small else ()
        lanes = 512 // pieces
        outs += [jax.ShapeDtypeStruct((count, lanes), F32) for count in counts]

        def kernel(kept_ref, came_ref, *out_refs):
            top = 0
            for (depth, width), out_ref in zip(shapes, out_refs):
                share = depth // pieces
                for at in range(0, width // 2, SLAB):
                    rows = slice(top, top + share)
                    out_ref[:, at : at + SLAB] = kept_ref[0, rows].astype(F32) + came_ref[
                        0, rows
                    ].astype(F32)
                    top += share
            if counts:
                rows = slice(top, top + 16)
                total = kept_ref[0, rows].astype(F32) + came_ref[0, rows].astype(F32)
                top = 0
                for count, out_ref in zip(counts, out_refs[len(shapes) :]):
                    out_ref[...] = total[top : top + count, :lanes]
                    top += count

        results = pl.pallas_call(
            kernel,
            out_shape=outs,
            in_specs=[VMEM] * 2,
            out_specs=[VMEM] * len(outs),
            compiler_params=pltpu.CompilerParams(vmem_limit_bytes=2 << 20),
            cost_estimate=lasting(1.6),
        )(pinned(kept), pinned(came))
        self.line.mark(results[0])
        self.done = dict(zip(self.shapes, results))
        self.shares = results[len(shapes) :]

    def spread(self, top, count, share):
        core = lax.axis_index("rows") & 1
        both = jnp.stack([self.kept, self.sent])[:, :, top : top + count * share].astype(F32)
        both = both.reshape(2, 2, 2, 2, count, share, SLAB)
        both = both.transpose(0, 3, 2, 1, 5, 4, 6)
        both = both.reshape(2, GROUPS // 2, 1, share, count * SLAB)
        held = jnp.concatenate([both * (core == 0), both * (core == 1)], 2)
        return held.reshape(2, GROUPS, share, count * SLAB)

    def end_uneven(self):
        pieces = lax.axis_size("rows")
        top = 0
        for name, (depth, width) in self.shapes.items():
            share, count = depth // GROUPS, width // (2 * SLAB)
            part = self.spread(top, count, share).reshape(2, depth, width // 2)
            part = lax.psum_scatter(part, "rows", scatter_dimension=1, tiled=True)
            self.done[name] = lax.psum_scatter(part, "section", scatter_dimension=0, tiled=True)[0]
            top += count * share
        if self.small:
            width = 512
            part = self.spread(top, 1, 16)[0, :, :10, : width // GROUPS]
            part = lax.psum(jnp.moveaxis(part, 1, 0).reshape(10, width), ("section", "rows"))
            start = lax.axis_index("rows") * (width // pieces)
            part = lax.dynamic_slice_in_dim(part, start, width // pieces, 1)
            self.shares = (part[0:2], part[2:4], part[4:7], part[7:10])


SIDE = 0
XYZ, YXZ = (SIDE, 1, 2, 3), (1, SIDE, 2, 3)
XZY, YZX = (SIDE, 2, 3, 1), (1, 2, 3, SIDE)
ZXY, ZYX = (2, 3, SIDE, 1), (2, 3, 1, SIDE)


def per_device(
    section_input,
    segments,
    cotangent,
    encoder_inward,
    encoder_outward,
    encoder_widen,
    encoder_narrow,
    encoder_gain,
    encoder_shift,
    decoder_inward,
    decoder_outward,
    decoder_cross_query,
    decoder_cross_memory,
    decoder_cross_outward,
    decoder_widen,
    decoder_narrow,
    decoder_gain,
    decoder_shift,
):
    section = lax.axis_index("section")
    own = section_input[0]
    length, width = own.shape[1:]
    wide = encoder_widen.shape[1]

    def low(*shape):
        return jax.ShapeDtypeStruct(shape, BF)

    def full(*shape):
        return jax.ShapeDtypeStruct(shape, F32)

    slabs, units, scales = low(length, width), full(length, width), full(length, LANES)
    chances = full(HEADS, length, length)
    attended = dict(
        projected=low(length, 3 * width), chances=chances, mixed=slabs, unit=units, scale=scales
    )
    line = Line()

    def run(body, inputs, near, outputs, loads, span, limit, packet=None, extra=None, away=None, late=None):
        near = dict(near)
        for name in list(near)[:1]:
            (near[name],) = line.after(near[name])
        kept, leaving = call(
            body if packet is None else (lambda room: body(room, packet)),
            inputs,
            near,
            outputs,
            loads,
            span,
            limit,
            packet,
            extra,
            away,
            late,
        )
        line.mark(list(vars(kept).values())[0])
        if packet is None:
            return kept
        return kept, leaving + (pair_swap(leaving[1], "rows", 1),)

    other = pair_swap(
        lax.dynamic_index_in_dim(own, 1 - section, 0, keepdims=False), "section", 1
    )
    near = run(
        own_body,
        dict(
            segments=segments,
            tokens=Entry(own),
            inward=Either(encoder_inward, decoder_inward),
            encoder_gain=encoder_gain,
            encoder_shift=encoder_shift,
            decoder_gain=decoder_gain,
            decoder_shift=decoder_shift,
            outward=Either(encoder_outward, decoder_outward),
        ),
        {},
        {},
        dict(
            other_inward=Either(decoder_inward, encoder_inward),
            other_outward=Either(decoder_outward, encoder_outward),
        ),
        4,
        6,
        away=dict(first=units, **attended),
    )

    wide_packet = Packet(decoder_narrow=decoder_narrow, decoder_widen=decoder_widen)
    far, d_wide = run(
        forward_body,
        dict(
            segments=segments,
            encoder_shift=encoder_shift,
            decoder_shift=decoder_shift,
            own_first=near.first,
        ),
        dict(
            tokens=other,
            inward=near.other_inward,
            outward=near.other_outward,
        ),
        dict(
            memory=slabs,
            output=slabs,
            **attended,
            e_low=slabs,
            e_hidden=low(length, wide),
            e_slope=full(length, wide),
            e_unit1=units,
            e_scale1=scales,
            d_low=slabs,
            c_query=slabs,
            c_paired=low(length, 2 * width),
            c_chances=chances,
            c_mixed=slabs,
            d_unit1=units,
            d_scale1=scales,
            d_grad=units,
            d_small2=full(2, width),
        ),
        dict(
            encoder_gain=encoder_gain,
            decoder_gain=decoder_gain,
            encoder_widen=encoder_widen,
            encoder_narrow=encoder_narrow,
            decoder_cross_query=decoder_cross_query,
            decoder_cross_memory=decoder_cross_memory,
            decoder_cross_outward=decoder_cross_outward,
        ),
        11,
        14,
        wide_packet,
        dict(d_hidden=low(length, wide), d_slope=full(length, wide)),
        late=dict(
            decoder_widen=decoder_widen,
            decoder_narrow=decoder_narrow,
            cotangent=Entry(cotangent),
        ),
    )

    cross_packet = Packet(
        decoder_cross_query=decoder_cross_query,
        decoder_cross_memory=decoder_cross_memory,
        decoder_cross_outward=decoder_cross_outward,
    )
    crossed, d_cross = run(
        cross_back_body,
        dict(near_unit=near.unit, near_scale=near.scale),
        dict(
            d_grad=far.d_grad,
            decoder_gain=far.decoder_gain,
            d_unit1=far.d_unit1,
            d_scale1=far.d_scale1,
            c_query=far.c_query,
            c_paired=far.c_paired,
            c_chances=far.c_chances,
            d_low=far.d_low,
            memory=far.memory,
            c_mixed=far.c_mixed,
            decoder_cross_outward=far.decoder_cross_outward,
            decoder_cross_memory=far.decoder_cross_memory,
            decoder_cross_query=far.decoder_cross_query,
            far_unit=far.unit,
            far_scale=far.scale,
        ),
        dict(grad_memory=slabs, d_grad0=units, d_small01=full(4, width)),
        {},
        4.7,
        5,
        cross_packet,
    )

    def d_self_run():
        packet = Packet(decoder_inward=decoder_inward, decoder_outward=decoder_outward)
        return packet, *run(
            decoder_self_body,
            dict(
                decoder_outward=decoder_outward,
                near_projected=near.projected,
                near_chances=near.chances,
                near_tokens=Entry(own),
                near_mixed=near.mixed,
                decoder_inward=decoder_inward,
            ),
            dict(
                far_tokens=other,
                d_grad0=crossed.d_grad0,
                far_projected=far.projected,
                far_chances=far.chances,
                far_mixed=far.mixed,
            ),
            dict(d_inputs=slabs),
            {},
            5,
            5,
            packet,
        )

    def encoder_run(d_inputs):
        packet = Packet(
            64,
            encoder_narrow=encoder_narrow,
            encoder_widen=encoder_widen,
            encoder_inward=encoder_inward,
            encoder_outward=encoder_outward,
        )
        sides = low(2, length, width)
        return packet, *run(
            encoder_back_body,
            dict(
                near_unit=near.unit,
                near_scale=near.scale,
                near_projected=near.projected,
                near_chances=near.chances,
                near_tokens=Entry(own),
                near_mixed=near.mixed,
                encoder_outward=encoder_outward,
                encoder_inward=encoder_inward,
            ),
            dict(
                far_tokens=other,
                encoder_gain=far.encoder_gain,
                grad_memory=crossed.grad_memory,
                e_unit1=far.e_unit1,
                e_scale1=far.e_scale1,
                encoder_narrow=far.encoder_narrow,
                e_slope=far.e_slope,
                e_hidden=far.e_hidden,
                e_low=far.e_low,
                encoder_widen=far.encoder_widen,
                d_small01=crossed.d_small01,
                d_small2=far.d_small2,
                far_unit=far.unit,
                far_scale=far.scale,
                far_projected=far.projected,
                far_chances=far.chances,
                far_mixed=far.mixed,
                d_inputs=d_inputs,
                memory=far.memory,
                output=far.output,
            ),
            dict(sides_mine=sides, sides_theirs=sides),
            {},
            8,
            8,
            packet,
        )

    team_w = Team(
        line,
        (XYZ, YZX),
        False,
        decoder_narrow=decoder_narrow,
        decoder_widen=decoder_widen,
    )
    team_q = Team(
        line,
        (ZYX, ZYX),
        False,
        decoder_cross_query=decoder_cross_query,
        decoder_cross_memory=decoder_cross_memory,
        decoder_cross_outward=decoder_cross_outward,
    )
    team_r = Team(
        line,
        (XZY, YZX),
        False,
        decoder_inward=decoder_inward,
        decoder_outward=decoder_outward,
    )
    team_e = Team(
        line,
        (XYZ, YXZ),
        False,
        encoder_narrow=encoder_narrow,
    )
    team_f = Team(
        line,
        (XZY, XYZ),
        False,
        encoder_widen=encoder_widen,
    )
    team_s = Team(
        line,
        (XYZ, YXZ),
        True,
        encoder_inward=encoder_inward,
        encoder_outward=encoder_outward,
    )
    team_w.grads((wide_packet, d_wide))
    team_q.grads((cross_packet, d_cross))
    self_packet, turned, d_self = d_self_run()
    encoder_packet, ended, e_all = encoder_run(turned.d_inputs)
    team_r.grads((self_packet, d_self))
    team_w.step()
    team_e.grads((encoder_packet, e_all))
    team_q.step()
    team_r.step()
    team_f.grads((encoder_packet, e_all))
    team_w.step()
    team_s.grads((encoder_packet, e_all))
    team_q.step()
    team_e.step()
    team_r.step()
    team_f.step()
    team_q.step()
    team_w.step()
    team_e.step()
    team_r.step()
    team_s.step()
    team_f.step()
    team_w.end()
    (theirs,) = line.after(ended.sides_theirs)
    theirs = pair_swap(theirs, "section", 1)
    team_r.end()
    team_s.step()
    team_e.step()
    team_f.step()
    team_s.step()
    mine, theirs = line.after(ended.sides_mine, theirs)
    results, gradients = (
        jnp.stack(
            [
                jnp.where(section == 0, mine[i], theirs[i]),
                jnp.where(section == 0, theirs[i], mine[i]),
            ]
        )[None]
        for i in (0, 1)
    )
    line.mark(gradients)
    team_q.end()
    team_f.end()
    team_e.end()
    team_s.end()

    done = {}
    for team in (team_w, team_q, team_r, team_e, team_f, team_s):
        done.update(team.done)
    deltas = SimpleNamespace(**done)
    shares = team_s.shares
    return (
        results,
        gradients,
        deltas.encoder_inward,
        deltas.encoder_outward,
        deltas.encoder_widen,
        deltas.encoder_narrow,
        shares[0],
        shares[1],
        deltas.decoder_inward,
        deltas.decoder_outward,
        deltas.decoder_cross_query,
        deltas.decoder_cross_memory,
        deltas.decoder_cross_outward,
        deltas.decoder_widen,
        deltas.decoder_narrow,
        shares[2],
        shares[3],
    )


def solution(mesh):
    weights = (P(),) * 15
    shares = P("rows", "section")
    small = P(None, "rows")
    sides = P("section", None, "rows", None)
    return jax.shard_map(
        per_device,
        mesh=mesh,
        in_specs=(sides, P(None, None, "rows", None), P(None, "rows", None)) + weights,
        out_specs=(sides, sides)
        + (shares,) * 4
        + (small,) * 2
        + (shares,) * 7
        + (small,) * 2,
        check_vma=False,
    )
```

```python
import math
from types import SimpleNamespace
from types import SimpleNamespace
from types import SimpleNamespace

import jax
import jax.numpy as jnp
from jax import lax
from jax.experimental import pallas as pl
from jax.experimental.pallas import tpu as pltpu
from jax.sharding import PartitionSpec as P

HEADS = 8
HEAD_DIM = 64
NEG = -1e30
EPS = 1e-05
GROUPS = 16
SLAB = 256
LANES = 128
BF = jnp.bfloat16
F32 = jnp.float32
def lasting(span):
    return pl.CostEstimate(flops=int(span * 5.5e9), bytes_accessed=1, transcendentals=0)


FACTOR = 1.0 / math.sqrt(HEAD_DIM)
HBM = pl.BlockSpec(memory_space=pltpu.HBM)
VMEM = pl.BlockSpec(memory_space=pltpu.VMEM)


def matmul(left, right):
    return lax.dot_general(left, right, (((1,), (0,)), ((), ())), preferred_element_type=F32)


def matmul_back(grad, weight):
    return lax.dot_general(grad, weight, (((1,), (1,)), ((), ())), preferred_element_type=F32)


def matmul_across(left, grad):
    return lax.dot_general(left, grad, (((0,), (0,)), ((), ())), preferred_element_type=F32)


def norm(summed, gain, shift):
    center = jnp.mean(summed, -1, keepdims=True)
    centered = summed - center
    spread = jnp.mean(centered * centered, -1, keepdims=True)
    scale = lax.rsqrt(spread + EPS)
    unit = centered * scale
    return unit * gain + shift, unit, scale


def norm_back(grad, unit, scale, gain):
    grad_gain = jnp.sum(grad * unit, 0, keepdims=True)
    grad_shift = jnp.sum(grad, 0, keepdims=True)
    inner = grad * gain
    center = jnp.mean(inner, -1, keepdims=True)
    along = jnp.mean(inner * unit, -1, keepdims=True)
    return scale * (inner - center - unit * along), grad_gain, grad_shift


def gelu_both(before):
    root = math.sqrt(2.0 / math.pi)
    square = before * before
    half = 0.5 + 0.5 * jnp.tanh(before * (root + root * 0.044715 * square))
    steep = 2 * root + 6 * root * 0.044715 * square
    return before * half, half * (1.0 + before * (1.0 - half) * steep)


def pair_marks():
    lane = lax.broadcasted_iota(jnp.int32, (1, LANES), 1) // HEAD_DIM
    return [(lane == h).astype(F32).astype(BF) for h in (0, 1)]


def join_pairs(parts):
    lane = lax.broadcasted_iota(jnp.int32, (1, LANES), 1) // HEAD_DIM
    pairs = zip(parts[0::2], parts[1::2])
    return jnp.concatenate([jnp.where(lane == 0, one, two) for one, two in pairs], 1)


def attend(query, keys, values, allowed, chances_ref):
    marks = pair_marks()
    query_down, values_down = query.T, values.T
    scores = []
    for head in range(HEADS):
        at = slice(head // 2 * LANES, (head // 2 + 1) * LANES)
        scores.append(matmul(keys[:, at] * marks[head % 2], query_down[at]))
    scores = [jnp.where(allowed, item * FACTOR, NEG) for item in scores]
    weights = [jnp.exp(item - jnp.max(item, 0, keepdims=True)) for item in scores]
    chances = [item * (1.0 / jnp.sum(item, 0, keepdims=True)) for item in weights]
    mixed = []
    for head, item in enumerate(chances):
        chances_ref[head] = item
        at = slice(head * HEAD_DIM, (head + 1) * HEAD_DIM)
        mixed.append(matmul(values_down[at], item.astype(BF)).astype(BF))
    return jnp.concatenate(mixed, 0).T


def attend_back(query, keys, values, chances_ref, grad_mixed):
    marks = pair_marks()
    grad_down, keys_down = grad_mixed.T, keys.T
    pairs = [slice(head // 2 * LANES, (head // 2 + 1) * LANES) for head in range(HEADS)]
    chances = [chances_ref[head] for head in range(HEADS)]
    grad_chances = [
        matmul(values[:, at] * marks[head % 2], grad_down[at]) for head, at in enumerate(pairs)
    ]
    grad_values = [matmul(item.astype(BF), grad_mixed[:, at]) for item, at in zip(chances, pairs)]
    held = [jnp.sum(one * two, 0, keepdims=True) for one, two in zip(chances, grad_chances)]
    grad_scores = [
        (one * (two - total)).astype(BF) for one, two, total in zip(chances, grad_chances, held)
    ]
    grad_keys = [matmul(item, query[:, at]) for item, at in zip(grad_scores, pairs)]
    grad_query = [
        matmul(keys_down[head * HEAD_DIM : (head + 1) * HEAD_DIM], item)
        for head, item in enumerate(grad_scores)
    ]
    turned = (jnp.concatenate(grad_query, 0) * FACTOR).astype(BF).T
    return [
        turned,
        (join_pairs(grad_keys) * FACTOR).astype(BF),
        join_pairs(grad_values).astype(BF),
    ]


def tiles_of(array):
    return [array[:, at : at + LANES] for at in range(0, array.shape[1], LANES)]


class Entry:
    def __init__(self, array):
        self.arrays = (array,)
        self.shape, self.dtype = array.shape[1:], array.dtype

    def pieces(self, refs, section):
        return [(None, refs[0].at[section])]


class Either:
    def __init__(self, *pair):
        pair = [item if isinstance(item, tuple) else (item, None) for item in pair]
        self.arrays = tuple(array for array, unused in pair)
        self.entries = [entry for unused, entry in pair]
        first = self.arrays[0]
        self.shape = first.shape if self.entries[0] is None else first.shape[1:]
        self.dtype = first.dtype

    def pieces(self, refs, section):
        return [
            (here, ref if entry is None else ref.at[entry])
            for here, (ref, entry) in enumerate(zip(refs, self.entries))
        ]


class Whole:
    def __init__(self, array):
        self.arrays = (array,)
        self.shape, self.dtype = array.shape, array.dtype

    def pieces(self, refs, section):
        return [(None, refs[0])]


class Room:
    def __init__(self, inputs, sources, held, sems, away):
        self.inputs, self.sources, self.held, self.sems = inputs, sources, held, sems
        self.away, self.left = away, {}
        self.section = lax.axis_index("section")
        self.core = lax.axis_index("rows") & 1
        self.arrived = set()
        for place, name in enumerate(inputs):
            for here, source in inputs[name].pieces(sources[name], self.section):
                copy = pltpu.make_async_copy(source, held[name], sems.at[place])
                if here is None:
                    copy.start()
                else:
                    pl.when(self.section == here)(copy.start)

    def __getattr__(self, name):
        if name in self.inputs and name not in self.arrived:
            self.arrived.add(name)
            place = list(self.inputs).index(name)
            source = self.inputs[name].pieces(self.sources[name], self.section)[0][1]
            pltpu.make_async_copy(source, self.held[name], self.sems.at[place]).wait()
        return self.held[name]

    def leave(self, *names):
        for name, (target, sem) in self.away.items():
            if name in names:
                copy = pltpu.make_async_copy(self.held[name], target, sem)
                copy.start()
                self.left[name] = copy

    def finish(self):
        self.leave(*(name for name in self.away if name not in self.left))
        for name in self.inputs:
            getattr(self, name)
        for copy in self.left.values():
            copy.wait()

    def either(self, here, there):
        return jnp.where(self.section == 0, here[...], there[...])


class Packet:
    def __init__(self, extra=0, **weights):
        self.shapes = {name: array.shape for name, array in weights.items()}
        self.left_at, self.grad_at = {}, {}
        left = grad = 0
        for name, (depth, width) in self.shapes.items():
            self.left_at[name], self.grad_at[name] = left, grad
            left, grad = left + depth // 2, grad + width
        self.left, self.extra_at, self.grad = left, grad, grad + extra

    def leaving(self):
        return [
            pltpu.VMEM((self.left, LANES), BF),
            pltpu.VMEM((self.left + self.grad, LANES), BF),
        ]

    def bind(self, room, refs):
        self.room, (self.keep, self.send) = room, refs

    def stash(self, **operands):
        even = self.room.core == 0
        for name, (left, grad) in operands.items():
            depth, width = self.shapes[name]
            block = depth // GROUPS
            across = left.T
            for group in range(0, GROUPS, 2):
                first = across[group * block : (group + 1) * block]
                second = across[(group + 1) * block : (group + 2) * block]
                top = self.left_at[name] + group // 2 * block
                self.keep[top : top + block] = jnp.where(even, first, second)
                self.send[top : top + block] = jnp.where(even, second, first)
            for place, tile in enumerate(tiles_of(grad)):
                top = self.left + self.grad_at[name] + place * LANES
                self.send[top : top + LANES] = tile


def far_away(array):
    return pltpu.with_memory_space_constraint(array, pltpu.HBM)


def pinned(array):
    return pltpu.with_memory_space_constraint(array, pltpu.VMEM)


def call(body, inputs, near, outputs, loads, span, limit, packet=None, extra=None, away=None, late=None):
    extra, away = extra or {}, away or {}
    inputs = {
        name: item if hasattr(item, "pieces") else Whole(item) for name, item in inputs.items()
    }
    loads = {name: item if hasattr(item, "pieces") else Whole(item) for name, item in loads.items()}
    inputs.update(loads)
    inputs.update({name: item if hasattr(item, "pieces") else Whole(item) for name, item in (late or {}).items()})
    arrays = [array for item in inputs.values() for array in item.arrays]
    outputs = {
        **outputs,
        **{name: jax.ShapeDtypeStruct(item.shape, item.dtype) for name, item in loads.items()},
    }
    shapes_out = [pltpu.VMEM(item.shape, item.dtype) for item in outputs.values()]
    shapes_out += packet.leaving() if packet else []
    shapes_out += [pltpu.HBM(item.shape, item.dtype) for item in away.values()]
    brought = [name for name in inputs if name not in loads]

    def kernel(*refs):
        refs = list(refs)

        def take(count):
            taken = refs[:count]
            del refs[:count]
            return taken

        sources = {name: take(len(item.arrays)) for name, item in inputs.items()}
        held = dict(zip(near, take(len(near))))
        held.update(zip(outputs, take(len(outputs))))
        leaving = take(2) if packet else None
        targets = take(len(away))
        held.update(zip(brought, take(len(brought))))
        held.update(zip(extra, take(len(extra))))
        held.update(zip(away, take(len(away))))
        away_to = {
            name: (target, refs[1].at[place])
            for place, (name, target) in enumerate(zip(away, targets))
        }
        room = Room(inputs, sources, held, refs[0], away_to)
        if packet:
            packet.bind(room, leaving)
        body(room)
        room.finish()

    scratch = [inputs[name] for name in brought] + list(extra.values()) + list(away.values())
    results = pl.pallas_call(
        kernel,
        out_shape=shapes_out,
        in_specs=[HBM] * len(arrays) + [VMEM] * len(near),
        out_specs=[VMEM] * (len(shapes_out) - len(away)) + [HBM] * len(away),
        scratch_shapes=[pltpu.VMEM(item.shape, item.dtype) for item in scratch]
        + [pltpu.SemaphoreType.DMA((max(1, len(inputs)),))]
        + [pltpu.SemaphoreType.DMA((max(1, len(away)),))],
        compiler_params=pltpu.CompilerParams(vmem_limit_bytes=limit << 20),
        cost_estimate=lasting(span),
    )(*(far_away(item) for item in arrays), *(pinned(item) for item in near.values()))
    made = dict(zip(outputs, results))
    made.update(zip(away, results[len(results) - len(away) :]))
    leaving = tuple(results[len(outputs) : len(results) - len(away)])
    return SimpleNamespace(**made), leaving


def place_of(side, block, orders, core):
    spots = []
    for order in orders:
        spot = side * (8 >> order.index(SIDE))
        for bit in range(3):
            spot = spot + (block >> bit & 1) * (8 >> order.index(bit + 1))
        spots.append(spot)
    return jnp.where(core == 0, spots[0], spots[1])


def bit_of(step, section, row):
    return section if step == SIDE else (row >> step) & 1


def weight_grads(parcels, names, orders, even, small=False):
    parts = [
        (packet, which, name)
        for which, (packet, *unused) in enumerate(parcels)
        for name in packet.shapes
        if name in names
    ]
    height = sum(
        packet.shapes[name][0] // GROUPS * packet.shapes[name][1] // (2 * SLAB)
        for packet, unused, name in parts
    )
    small_at = height
    height += 16 if small else 0
    half = pltpu.VMEM((GROUPS // 2, height, SLAB), BF)

    def kernel(*refs):
        *operands, kept_out, sent_out, packed = refs
        row = lax.axis_index("rows")
        core = row & 1
        if even:
            first = [bit_of(order[0], lax.axis_index("section"), row) for order in orders]
            mine = jnp.where(core == 0, first[0], first[1])
        else:
            mine = 0

        base = 0
        for packet, which, name in parts:
            keep_ref, send_ref, came_ref = operands[3 * which : 3 * which + 3]
            depth, width = packet.shapes[name]
            block, half_pieces = depth // GROUPS, width // (2 * SLAB)
            left_at, grad_at = packet.left_at[name], packet.left + packet.grad_at[name]
            left = jnp.concatenate(
                [ref[left_at : left_at + depth // 2] for ref in (keep_ref, came_ref)], 1
            )
            for piece in range(width // SLAB):
                at = grad_at + piece * SLAB
                right = jnp.concatenate(
                    [
                        jnp.concatenate([ref[at : at + LANES], ref[at + LANES : at + 2 * LANES]], 1)
                        for ref in (send_ref, came_ref)
                    ],
                    0,
                )
                tile = matmul(left, right).astype(BF)
                side, offset = divmod(piece, half_pieces)
                top = base + offset * block
                for number in range(GROUPS // 2):
                    packed[place_of(side, number, orders, core), top : top + block] = tile[
                        number * block : (number + 1) * block
                    ]
            base += block * half_pieces
        if small:
            packet = parcels[0][0]
            at = packet.left + packet.extra_at
            total = sum(
                jnp.concatenate([ref[at + 16 * i : at + 16 * i + 16] for i in range(4)], 1).astype(F32)
                for ref in operands[1:3]
            )
            width = total.shape[1]
            share = width // GROUPS
            for number in range(GROUPS // 2):
                turned = [
                    pltpu.roll(total, (width - (2 * number + i) * share) % width, 1) for i in (0, 1)
                ]
                part = jnp.where(core == 0, turned[0], turned[1])[:, :SLAB].astype(BF)
                for side in (0, 1):
                    packed[place_of(side, number, orders, core), small_at : small_at + 16] = part
        count = GROUPS // 2
        sent_out[...] = packed[pl.ds((1 - mine) * count, count)]
        kept_out[...] = packed[pl.ds(mine * count, count)]

    arrays = [array for unused, *rest in parcels for array in rest]
    return pl.pallas_call(
        kernel,
        out_shape=[half, half],
        in_specs=[VMEM] * len(arrays),
        out_specs=[VMEM] * 2,
        scratch_shapes=[pltpu.VMEM((GROUPS, height, SLAB), BF)],
        compiler_params=pltpu.CompilerParams(vmem_limit_bytes=8 << 20),
        cost_estimate=lasting(3.5),
    )(*(pinned(item) for item in arrays))


def equal_ids(row_ids, column_ids):
    length = row_ids.shape[1]
    down = jnp.broadcast_to(row_ids.astype(F32), (length, length)).T
    return down == jnp.broadcast_to(column_ids.astype(F32), (length, length))


def scale_out(scale):
    return jnp.broadcast_to(scale, (scale.shape[0], LANES))


def thirds(projected):
    width = projected.shape[1] // 3
    return [projected[:, i * width : (i + 1) * width] for i in range(3)]


def self_part(room, tokens, ids, causal, inward, outward, gain, shift):
    room.projected[...] = matmul(tokens, inward[...]).astype(BF)
    room.leave("projected")
    length = tokens.shape[0]
    rows = lax.broadcasted_iota(jnp.int32, (length, length), 0)
    columns = lax.broadcasted_iota(jnp.int32, (length, length), 1)
    reach = jnp.where(causal, 0, length)
    allowed = equal_ids(ids, ids) & (columns + reach >= rows)
    mixed = attend(*thirds(room.projected), allowed, room.chances)
    room.mixed[...] = mixed
    room.leave("chances", "mixed")
    summed = tokens.astype(F32) + matmul(mixed, outward[...])
    first, unit, scale = norm(summed, gain, shift)
    room.unit[...] = unit
    room.scale[...] = scale_out(scale)
    return first


def own_body(room):
    section = room.section
    ids = room.segments[pl.ds(section, 1), pl.ds(section, 1), 0, :][0]
    gain = jnp.where(section == 0, room.encoder_gain[0:1], room.decoder_gain[0:1])
    shift = jnp.where(section == 0, room.encoder_shift[0:1], room.decoder_shift[0:1])
    room.first[...] = self_part(
        room, room.tokens[...], ids, section == 1, room.inward, room.outward, gain, shift
    )


def forward_body(room, packet):
    section = room.section
    source_ids = room.segments[0, pl.ds(section, 1), 0, :]
    target_ids = room.segments[1, pl.ds(section, 1), 0, :]
    ids = jnp.where(section == 0, target_ids, source_ids)
    gain = jnp.where(section == 0, room.decoder_gain[0:1], room.encoder_gain[0:1])
    shift = jnp.where(section == 0, room.decoder_shift[0:1], room.encoder_shift[0:1])
    other = self_part(
        room, room.tokens[...], ids, section == 0, room.inward, room.outward, gain, shift
    )
    own = room.own_first[...]

    first = jnp.where(section == 0, own, other)
    low = first.astype(BF)
    widen_forward(low, room.encoder_widen, room.e_hidden, room.e_slope)
    room.e_low[...] = low
    summed = first + matmul(room.e_hidden[...], room.encoder_narrow[...])
    result, unit, scale = norm(summed, room.encoder_gain[1:2], room.encoder_shift[1:2])
    memory = result.astype(BF)
    room.e_unit1[...] = unit
    room.e_scale1[...] = scale_out(scale)
    room.memory[...] = memory

    first = jnp.where(section == 0, other, own)
    low = first.astype(BF)
    query = matmul(low, room.decoder_cross_query[...]).astype(BF)
    paired = matmul(memory, room.decoder_cross_memory[...]).astype(BF)
    room.d_low[...] = low
    room.c_query[...] = query
    room.c_paired[...] = paired
    width = query.shape[1]
    mixed = attend(
        query,
        room.c_paired[:, :width],
        room.c_paired[:, width:],
        equal_ids(source_ids, target_ids),
        room.c_chances,
    )
    room.c_mixed[...] = mixed
    summed = first + matmul(mixed, room.decoder_cross_outward[...])
    second, unit, scale = norm(summed, room.decoder_gain[1:2], room.decoder_shift[1:2])
    room.d_unit1[...] = unit
    room.d_scale1[...] = scale_out(scale)

    low = second.astype(BF)
    widen_forward(low, room.decoder_widen, room.d_hidden, room.d_slope)
    summed = second + matmul(room.d_hidden[...], room.decoder_narrow[...])
    gain = room.decoder_gain[2:3]
    result, unit, scale = norm(summed, gain, room.decoder_shift[2:3])
    room.output[...] = result.astype(BF)

    grad_sum, grad_gain, grad_shift = norm_back(
        room.cotangent[...].astype(F32), unit, scale, gain
    )
    grad_low = grad_sum.astype(BF)
    grad_before = widen_backward(grad_low, room.decoder_narrow, room.d_slope)
    packet.stash(
        decoder_narrow=(room.d_hidden[...], grad_low), decoder_widen=(low, grad_before)
    )
    room.d_sum[...] = grad_sum
    room.d_before[...] = grad_before
    room.d_small2[...] = jnp.concatenate([grad_gain, grad_shift], 0)


def widen_forward(low, widen_ref, hidden_ref, slope_ref):
    step = 512
    for at in range(0, widen_ref.shape[1], step):
        hidden, slope = gelu_both(matmul(low, widen_ref[:, at : at + step]))
        hidden_ref[:, at : at + step] = hidden.astype(BF)
        slope_ref[:, at : at + step] = slope


def widen_backward(grad_low, narrow_ref, slope_ref):
    step = 512
    parts = []
    for at in range(0, narrow_ref.shape[0], step):
        grad_hidden = matmul_back(grad_low, narrow_ref[at : at + step])
        parts.append((grad_hidden * slope_ref[:, at : at + step]).astype(BF))
    return jnp.concatenate(parts, 1)


def cross_back_body(room, packet):
    grad_normed = room.d_sum[...] + matmul_back(room.d_before[...], room.decoder_widen[...])
    grad_sum, gain1, shift1 = norm_back(
        grad_normed, room.d_unit1[...], room.d_scale1[:, :1], room.decoder_gain[1:2]
    )
    grad_low = grad_sum.astype(BF)
    grad_mixed = matmul_back(grad_low, room.decoder_cross_outward[...]).astype(BF)
    paired = room.c_paired
    query = room.c_query[...]
    width = query.shape[1]
    grad_query, grad_keys, grad_values = attend_back(
        query, paired[:, :width], paired[:, width:], room.c_chances, grad_mixed
    )
    grad_paired = jnp.concatenate([grad_keys, grad_values], 1)
    packet.stash(
        decoder_cross_query=(room.d_low[...], grad_query),
        decoder_cross_memory=(room.memory[...], grad_paired),
        decoder_cross_outward=(room.c_mixed[...], grad_low),
    )
    room.d_sum1[...] = grad_sum
    room.c_grad_query[...] = grad_query
    room.c_grad_paired[...] = grad_paired
    room.d_small1[...] = jnp.concatenate([gain1, shift1], 0)


def self_back(grad_sum, inward, outward, tokens, projected, chances, mixed):
    grad_low = grad_sum.astype(BF)
    grad_mixed = matmul_back(grad_low, outward[...]).astype(BF)
    grad_projected = jnp.concatenate(attend_back(*thirds(projected), chances, grad_mixed), 1)
    pairs = ((tokens, grad_projected), (mixed, grad_low))
    return pairs, grad_sum + matmul_back(grad_projected, inward[...])


def decoder_self_body(room, packet):
    either = room.either
    grad_query, grad_paired = room.c_grad_query[...], room.c_grad_paired[...]
    room.grad_memory[...] = matmul_back(grad_paired, room.decoder_cross_memory[...]).astype(BF)
    grad_normed = room.d_sum1[...] + matmul_back(grad_query, room.decoder_cross_query[...])
    grad_sum, gain0, shift0 = norm_back(
        grad_normed,
        either(room.far_unit, room.near_unit),
        either(room.far_scale, room.near_scale)[:, :1],
        room.decoder_gain[0:1],
    )
    room.d_small0[...] = jnp.concatenate([gain0, shift0], 0)
    (inward, outward), grad_inputs = self_back(
        grad_sum,
        room.decoder_inward,
        room.decoder_outward,
        either(room.far_tokens, room.near_tokens),
        either(room.far_projected, room.near_projected),
        either(room.far_chances, room.near_chances),
        either(room.far_mixed, room.near_mixed),
    )
    packet.stash(decoder_inward=inward, decoder_outward=outward)
    room.d_inputs[...] = grad_inputs.astype(BF)


def encoder_back_body(room, packet):
    gain = room.encoder_gain
    grad_sum, gain1, shift1 = norm_back(
        room.grad_memory[...].astype(F32), room.e_unit1[...], room.e_scale1[:, :1], gain[1:2]
    )
    grad_low = grad_sum.astype(BF)
    grad_before = widen_backward(grad_low, room.encoder_narrow, room.e_slope)
    packet.stash(
        encoder_narrow=(room.e_hidden[...], grad_low), encoder_widen=(room.e_low[...], grad_before)
    )
    grad_normed = grad_sum + matmul_back(grad_before, room.encoder_widen[...])
    either = room.either
    grad_sum, gain0, shift0 = norm_back(
        grad_normed,
        either(room.near_unit, room.far_unit),
        either(room.near_scale, room.far_scale)[:, :1],
        gain[0:1],
    )
    smalls = [room.d_small0[...], room.d_small1[...], room.d_small2[...]]
    small = jnp.concatenate(
        [gain0, gain1, shift0, shift1]
        + [item[0:1] for item in smalls]
        + [item[1:2] for item in smalls]
        + [jnp.zeros((6, gain0.shape[1]), F32)],
        0,
    )
    for place, tile in enumerate(tiles_of(small.astype(BF))):
        top = packet.left + packet.extra_at + 16 * place
        packet.send[top : top + 16] = tile
    (inward, outward), grad_inputs = self_back(
        grad_sum,
        room.encoder_inward,
        room.encoder_outward,
        either(room.near_tokens, room.far_tokens),
        either(room.near_projected, room.far_projected),
        either(room.near_chances, room.far_chances),
        either(room.near_mixed, room.far_mixed),
    )
    packet.stash(encoder_inward=inward, encoder_outward=outward)
    here, there = grad_inputs.astype(BF), room.d_inputs[...]
    room.sides_mine[0] = either(room.memory, room.output)
    room.sides_mine[1] = jnp.where(room.section == 0, here, there)
    room.sides_theirs[0] = either(room.output, room.memory)
    room.sides_theirs[1] = jnp.where(room.section == 0, there, here)


class Line:
    def __init__(self):
        self.last = None

    def after(self, *values):
        if self.last is None:
            return values
        return lax.optimization_barrier((values, self.last))[0]

    def mark(self, value):
        self.last = value


def pair_swap(value, axis, apart):
    count = lax.axis_size(axis)
    return lax.ppermute(value, axis, [(i, i ^ apart) for i in range(count)])


def halve(kept, came, following, span):
    count, height = kept.shape[0] // 2, kept.shape[1]
    half = pltpu.VMEM((count, height, SLAB), BF)

    def kernel(kept_ref, came_ref, kept_out, sent_out):
        section, row = lax.axis_index("section"), lax.axis_index("rows")
        bits = [bit_of(step, section, row) for step in following]
        mine = jnp.where(row & 1 == 0, bits[0], bits[1])
        for which, out in ((1 - mine, sent_out), (mine, kept_out)):
            part = pl.ds(which * count, count)
            out[...] = (kept_ref[part].astype(F32) + came_ref[part].astype(F32)).astype(BF)

    return pl.pallas_call(
        kernel,
        out_shape=[half, half],
        in_specs=[VMEM] * 2,
        out_specs=[VMEM] * 2,
        compiler_params=pltpu.CompilerParams(vmem_limit_bytes=2 << 20),
        cost_estimate=lasting(span),
    )(pinned(kept), pinned(came))


class Team:
    def __init__(self, line, orders, small=False, **weights):
        self.line, self.orders, self.small = line, orders, small
        self.shapes = {name: array.shape for name, array in weights.items()}
        self.even = lax.axis_size("rows") == GROUPS
        self.turn = 0
        self.done = {}

    def grads(self, *parcels):
        tied = self.line.after(*(parts for unused, parts in parcels))
        parcels = [(packet, *parts) for (packet, unused), parts in zip(parcels, tied)]
        self.kept, self.sent = weight_grads(
            parcels, list(self.shapes), self.orders, self.even, self.small
        )
        self.line.mark(self.sent)
        if self.even:
            self.go()

    def go(self):
        pieces = lax.axis_size("rows")
        route = []
        for device in range(2 * pieces):
            step = self.orders[device & 1][self.turn]
            route.append((device, device ^ (pieces if step == SIDE else 1 << step)))
        self.came = lax.ppermute(self.sent, ("section", "rows"), route)

    def step(self, span=2):
        if not self.even:
            return
        self.turn += 1
        kept, came = self.line.after(self.kept, self.came)
        following = [order[self.turn] for order in self.orders]
        self.kept, self.sent = halve(kept, came, following, span)
        self.line.mark(self.sent)
        self.go()

    def end(self):
        pieces = lax.axis_size("rows")
        if not self.even:
            return self.end_uneven()
        kept, came = self.line.after(self.kept, self.came)
        shapes = list(self.shapes.values())
        outs = [jax.ShapeDtypeStruct((depth // pieces, width // 2), F32) for depth, width in shapes]
        counts = (2, 2, 3, 3) if self.small else ()
        lanes = 512 // pieces
        outs += [jax.ShapeDtypeStruct((count, lanes), F32) for count in counts]

        def kernel(kept_ref, came_ref, *out_refs):
            top = 0
            for (depth, width), out_ref in zip(shapes, out_refs):
                share = depth // pieces
                for at in range(0, width // 2, SLAB):
                    rows = slice(top, top + share)
                    out_ref[:, at : at + SLAB] = kept_ref[0, rows].astype(F32) + came_ref[
                        0, rows
                    ].astype(F32)
                    top += share
            if counts:
                rows = slice(top, top + 16)
                total = kept_ref[0, rows].astype(F32) + came_ref[0, rows].astype(F32)
                top = 0
                for count, out_ref in zip(counts, out_refs[len(shapes) :]):
                    out_ref[...] = total[top : top + count, :lanes]
                    top += count

        results = pl.pallas_call(
            kernel,
            out_shape=outs,
            in_specs=[VMEM] * 2,
            out_specs=[VMEM] * len(outs),
            compiler_params=pltpu.CompilerParams(vmem_limit_bytes=2 << 20),
            cost_estimate=lasting(1.6),
        )(pinned(kept), pinned(came))
        self.line.mark(results[0])
        self.done = dict(zip(self.shapes, results))
        self.shares = results[len(shapes) :]

    def spread(self, top, count, share):
        core = lax.axis_index("rows") & 1
        both = jnp.stack([self.kept, self.sent])[:, :, top : top + count * share].astype(F32)
        both = both.reshape(2, 2, 2, 2, count, share, SLAB)
        both = both.transpose(0, 3, 2, 1, 5, 4, 6)
        both = both.reshape(2, GROUPS // 2, 1, share, count * SLAB)
        held = jnp.concatenate([both * (core == 0), both * (core == 1)], 2)
        return held.reshape(2, GROUPS, share, count * SLAB)

    def end_uneven(self):
        pieces = lax.axis_size("rows")
        top = 0
        for name, (depth, width) in self.shapes.items():
            share, count = depth // GROUPS, width // (2 * SLAB)
            part = self.spread(top, count, share).reshape(2, depth, width // 2)
            part = lax.psum_scatter(part, "rows", scatter_dimension=1, tiled=True)
            self.done[name] = lax.psum_scatter(part, "section", scatter_dimension=0, tiled=True)[0]
            top += count * share
        if self.small:
            width = 512
            part = self.spread(top, 1, 16)[0, :, :10, : width // GROUPS]
            part = lax.psum(jnp.moveaxis(part, 1, 0).reshape(10, width), ("section", "rows"))
            start = lax.axis_index("rows") * (width // pieces)
            part = lax.dynamic_slice_in_dim(part, start, width // pieces, 1)
            self.shares = (part[0:2], part[2:4], part[4:7], part[7:10])


SIDE = 0
XYZ, YXZ = (SIDE, 1, 2, 3), (1, SIDE, 2, 3)
XZY, YZX = (SIDE, 2, 3, 1), (1, 2, 3, SIDE)
ZXY, ZYX = (2, 3, SIDE, 1), (2, 3, 1, SIDE)


def per_device(
    section_input,
    segments,
    cotangent,
    encoder_inward,
    encoder_outward,
    encoder_widen,
    encoder_narrow,
    encoder_gain,
    encoder_shift,
    decoder_inward,
    decoder_outward,
    decoder_cross_query,
    decoder_cross_memory,
    decoder_cross_outward,
    decoder_widen,
    decoder_narrow,
    decoder_gain,
    decoder_shift,
):
    section = lax.axis_index("section")
    own = section_input[0]
    length, width = own.shape[1:]
    wide = encoder_widen.shape[1]

    def low(*shape):
        return jax.ShapeDtypeStruct(shape, BF)

    def full(*shape):
        return jax.ShapeDtypeStruct(shape, F32)

    slabs, units, scales = low(length, width), full(length, width), full(length, LANES)
    chances = full(HEADS, length, length)
    attended = dict(
        projected=low(length, 3 * width), chances=chances, mixed=slabs, unit=units, scale=scales
    )
    line = Line()

    def run(body, inputs, near, outputs, loads, span, limit, packet=None, extra=None, away=None, late=None):
        near = dict(near)
        for name in list(near)[:1]:
            (near[name],) = line.after(near[name])
        kept, leaving = call(
            body if packet is None else (lambda room: body(room, packet)),
            inputs,
            near,
            outputs,
            loads,
            span,
            limit,
            packet,
            extra,
            away,
            late,
        )
        line.mark(list(vars(kept).values())[0])
        if packet is None:
            return kept
        return kept, leaving + (pair_swap(leaving[1], "rows", 1),)

    other = pair_swap(
        lax.dynamic_index_in_dim(own, 1 - section, 0, keepdims=False), "section", 1
    )
    near = run(
        own_body,
        dict(
            segments=segments,
            tokens=Entry(own),
            inward=Either(encoder_inward, decoder_inward),
            encoder_gain=encoder_gain,
            encoder_shift=encoder_shift,
            decoder_gain=decoder_gain,
            decoder_shift=decoder_shift,
            outward=Either(encoder_outward, decoder_outward),
        ),
        {},
        {},
        dict(
            other_inward=Either(decoder_inward, encoder_inward),
            other_outward=Either(decoder_outward, encoder_outward),
        ),
        4,
        6,
        away=dict(first=units, **attended),
    )

    wide_packet = Packet(decoder_narrow=decoder_narrow, decoder_widen=decoder_widen)
    far, d_wide = run(
        forward_body,
        dict(
            segments=segments,
            encoder_shift=encoder_shift,
            decoder_shift=decoder_shift,
            own_first=near.first,
        ),
        dict(
            tokens=other,
            inward=near.other_inward,
            outward=near.other_outward,
        ),
        dict(
            memory=slabs,
            output=slabs,
            **attended,
            e_low=slabs,
            e_hidden=low(length, wide),
            e_slope=full(length, wide),
            e_unit1=units,
            e_scale1=scales,
            d_low=slabs,
            c_query=slabs,
            c_paired=low(length, 2 * width),
            c_chances=chances,
            c_mixed=slabs,
            d_unit1=units,
            d_scale1=scales,
            d_sum=units,
            d_before=low(length, wide),
            d_small2=full(2, width),
        ),
        dict(
            encoder_gain=encoder_gain,
            decoder_gain=decoder_gain,
            encoder_widen=encoder_widen,
            encoder_narrow=encoder_narrow,
            decoder_cross_query=decoder_cross_query,
            decoder_cross_memory=decoder_cross_memory,
            decoder_cross_outward=decoder_cross_outward,
            decoder_widen=decoder_widen,
        ),
        11,
        14,
        wide_packet,
        dict(d_hidden=low(length, wide), d_slope=full(length, wide)),
        late=dict(decoder_narrow=decoder_narrow, cotangent=Entry(cotangent)),
    )

    cross_packet = Packet(
        decoder_cross_query=decoder_cross_query,
        decoder_cross_memory=decoder_cross_memory,
        decoder_cross_outward=decoder_cross_outward,
    )
    crossed, d_cross = run(
        cross_back_body,
        {},
        dict(
            d_sum=far.d_sum,
            d_before=far.d_before,
            decoder_widen=far.decoder_widen,
            decoder_gain=far.decoder_gain,
            d_unit1=far.d_unit1,
            d_scale1=far.d_scale1,
            c_query=far.c_query,
            c_paired=far.c_paired,
            c_chances=far.c_chances,
            d_low=far.d_low,
            memory=far.memory,
            c_mixed=far.c_mixed,
            decoder_cross_outward=far.decoder_cross_outward,
        ),
        dict(
            d_sum1=units,
            c_grad_query=slabs,
            c_grad_paired=low(length, 2 * width),
            d_small1=full(2, width),
        ),
        {},
        4.7,
        5,
        cross_packet,
    )

    def d_self_run():
        packet = Packet(decoder_inward=decoder_inward, decoder_outward=decoder_outward)
        return packet, *run(
            decoder_self_body,
            dict(
                near_unit=near.unit,
                near_scale=near.scale,
                decoder_outward=decoder_outward,
                near_projected=near.projected,
                near_chances=near.chances,
                near_tokens=Entry(own),
                near_mixed=near.mixed,
                decoder_inward=decoder_inward,
            ),
            dict(
                far_tokens=other,
                c_grad_query=crossed.c_grad_query,
                c_grad_paired=crossed.c_grad_paired,
                d_sum1=crossed.d_sum1,
                decoder_cross_memory=far.decoder_cross_memory,
                decoder_cross_query=far.decoder_cross_query,
                decoder_gain=far.decoder_gain,
                far_unit=far.unit,
                far_scale=far.scale,
                far_projected=far.projected,
                far_chances=far.chances,
                far_mixed=far.mixed,
            ),
            dict(d_inputs=slabs, grad_memory=slabs, d_small0=full(2, width)),
            {},
            5,
            5,
            packet,
        )

    def encoder_run(turned):
        packet = Packet(
            64,
            encoder_narrow=encoder_narrow,
            encoder_widen=encoder_widen,
            encoder_inward=encoder_inward,
            encoder_outward=encoder_outward,
        )
        sides = low(2, length, width)
        return packet, *run(
            encoder_back_body,
            dict(
                near_unit=near.unit,
                near_scale=near.scale,
                near_projected=near.projected,
                near_chances=near.chances,
                near_tokens=Entry(own),
                near_mixed=near.mixed,
                encoder_outward=encoder_outward,
                encoder_inward=encoder_inward,
            ),
            dict(
                far_tokens=other,
                encoder_gain=far.encoder_gain,
                grad_memory=turned.grad_memory,
                e_unit1=far.e_unit1,
                e_scale1=far.e_scale1,
                encoder_narrow=far.encoder_narrow,
                e_slope=far.e_slope,
                e_hidden=far.e_hidden,
                e_low=far.e_low,
                encoder_widen=far.encoder_widen,
                d_small0=turned.d_small0,
                d_small1=crossed.d_small1,
                d_small2=far.d_small2,
                far_unit=far.unit,
                far_scale=far.scale,
                far_projected=far.projected,
                far_chances=far.chances,
                far_mixed=far.mixed,
                d_inputs=turned.d_inputs,
                memory=far.memory,
                output=far.output,
            ),
            dict(sides_mine=sides, sides_theirs=sides),
            {},
            8,
            8,
            packet,
        )

    team_w = Team(
        line,
        (XYZ, YZX),
        False,
        decoder_narrow=decoder_narrow,
        decoder_widen=decoder_widen,
    )
    team_q = Team(
        line,
        (ZYX, ZYX),
        False,
        decoder_cross_query=decoder_cross_query,
        decoder_cross_memory=decoder_cross_memory,
        decoder_cross_outward=decoder_cross_outward,
    )
    team_r = Team(
        line,
        (XZY, YZX),
        False,
        decoder_inward=decoder_inward,
        decoder_outward=decoder_outward,
    )
    team_e = Team(
        line,
        (YZX, XYZ),
        False,
        encoder_narrow=encoder_narrow,
    )
    team_f = Team(
        line,
        (XZY, XYZ),
        False,
        encoder_widen=encoder_widen,
    )
    team_s = Team(
        line,
        (XYZ, YXZ),
        True,
        encoder_inward=encoder_inward,
        encoder_outward=encoder_outward,
    )
    team_w.grads((wide_packet, d_wide))
    team_q.grads((cross_packet, d_cross))
    self_packet, turned, d_self = d_self_run()
    encoder_packet, ended, e_all = encoder_run(turned)
    team_r.grads((self_packet, d_self))
    team_w.step()
    team_q.step()
    team_e.grads((encoder_packet, e_all))
    team_f.grads((encoder_packet, e_all))
    team_r.step()
    team_w.step()
    team_s.grads((encoder_packet, e_all))
    team_q.step()
    team_e.step()
    team_r.step()
    team_f.step()
    team_q.step()
    team_w.step()
    team_e.step()
    team_r.step()
    team_s.step()
    team_f.step()
    team_w.end()
    (theirs,) = line.after(ended.sides_theirs)
    theirs = pair_swap(theirs, "section", 1)
    team_r.end()
    team_s.step()
    team_e.step()
    team_f.step()
    team_s.step()
    mine, theirs = line.after(ended.sides_mine, theirs)
    results, gradients = (
        jnp.stack(
            [
                jnp.where(section == 0, mine[i], theirs[i]),
                jnp.where(section == 0, theirs[i], mine[i]),
            ]
        )[None]
        for i in (0, 1)
    )
    line.mark(gradients)
    team_q.end()
    team_f.end()
    team_e.end()
    team_s.end()

    done = {}
    for team in (team_w, team_q, team_r, team_e, team_f, team_s):
        done.update(team.done)
    deltas = SimpleNamespace(**done)
    shares = team_s.shares
    return (
        results,
        gradients,
        deltas.encoder_inward,
        deltas.encoder_outward,
        deltas.encoder_widen,
        deltas.encoder_narrow,
        shares[0],
        shares[1],
        deltas.decoder_inward,
        deltas.decoder_outward,
        deltas.decoder_cross_query,
        deltas.decoder_cross_memory,
        deltas.decoder_cross_outward,
        deltas.decoder_widen,
        deltas.decoder_narrow,
        shares[2],
        shares[3],
    )


def solution(mesh):
    weights = (P(),) * 15
    shares = P("rows", "section")
    small = P(None, "rows")
    sides = P("section", None, "rows", None)
    return jax.shard_map(
        per_device,
        mesh=mesh,
        in_specs=(sides, P(None, None, "rows", None), P(None, "rows", None)) + weights,
        out_specs=(sides, sides)
        + (shares,) * 4
        + (small,) * 2
        + (shares,) * 7
        + (small,) * 2,
        check_vma=False,
    )
```

```python
import math
from types import SimpleNamespace
from types import SimpleNamespace
from types import SimpleNamespace

import jax
import jax.numpy as jnp
from jax import lax
from jax.experimental import pallas as pl
from jax.experimental.pallas import tpu as pltpu
from jax.sharding import PartitionSpec as P

HEADS = 8
HEAD_DIM = 64
NEG = -1e30
EPS = 1e-05
GROUPS = 16
SLAB = 256
LANES = 128
BF = jnp.bfloat16
F32 = jnp.float32
def lasting(span):
    return pl.CostEstimate(flops=int(span * 5.5e9), bytes_accessed=1, transcendentals=0)


FACTOR = 1.0 / math.sqrt(HEAD_DIM)
HBM = pl.BlockSpec(memory_space=pltpu.HBM)
VMEM = pl.BlockSpec(memory_space=pltpu.VMEM)


def matmul(left, right):
    return lax.dot_general(left, right, (((1,), (0,)), ((), ())), preferred_element_type=F32)


def matmul_back(grad, weight):
    return lax.dot_general(grad, weight, (((1,), (1,)), ((), ())), preferred_element_type=F32)


def matmul_across(left, grad):
    return lax.dot_general(left, grad, (((0,), (0,)), ((), ())), preferred_element_type=F32)


def norm(summed, gain, shift):
    center = jnp.mean(summed, -1, keepdims=True)
    centered = summed - center
    spread = jnp.mean(centered * centered, -1, keepdims=True)
    scale = lax.rsqrt(spread + EPS)
    unit = centered * scale
    return unit * gain + shift, unit, scale


def norm_back(grad, unit, scale, gain):
    grad_gain = jnp.sum(grad * unit, 0, keepdims=True)
    grad_shift = jnp.sum(grad, 0, keepdims=True)
    inner = grad * gain
    center = jnp.mean(inner, -1, keepdims=True)
    along = jnp.mean(inner * unit, -1, keepdims=True)
    return scale * (inner - center - unit * along), grad_gain, grad_shift


def gelu_both(before):
    root = math.sqrt(2.0 / math.pi)
    square = before * before
    half = 0.5 + 0.5 * jnp.tanh(before * (root + root * 0.044715 * square))
    steep = 2 * root + 6 * root * 0.044715 * square
    return before * half, half * (1.0 + before * (1.0 - half) * steep)


def pair_marks():
    lane = lax.broadcasted_iota(jnp.int32, (1, LANES), 1) // HEAD_DIM
    return [(lane == h).astype(F32).astype(BF) for h in (0, 1)]


def join_pairs(parts):
    lane = lax.broadcasted_iota(jnp.int32, (1, LANES), 1) // HEAD_DIM
    pairs = zip(parts[0::2], parts[1::2])
    return jnp.concatenate([jnp.where(lane == 0, one, two) for one, two in pairs], 1)


def attend(query, keys, values, allowed, chances_ref):
    marks = pair_marks()
    query_down, values_down = query.T, values.T
    scores = []
    for head in range(HEADS):
        at = slice(head // 2 * LANES, (head // 2 + 1) * LANES)
        scores.append(matmul(keys[:, at] * marks[head % 2], query_down[at]))
    scores = [jnp.where(allowed, item * FACTOR, NEG) for item in scores]
    weights = [jnp.exp(item - jnp.max(item, 0, keepdims=True)) for item in scores]
    chances = [item * (1.0 / jnp.sum(item, 0, keepdims=True)) for item in weights]
    mixed = []
    for head, item in enumerate(chances):
        chances_ref[head] = item
        at = slice(head * HEAD_DIM, (head + 1) * HEAD_DIM)
        mixed.append(matmul(values_down[at], item.astype(BF)).astype(BF))
    return jnp.concatenate(mixed, 0).T


def attend_back(query, keys, values, chances_ref, grad_mixed):
    marks = pair_marks()
    grad_down, keys_down = grad_mixed.T, keys.T
    pairs = [slice(head // 2 * LANES, (head // 2 + 1) * LANES) for head in range(HEADS)]
    chances = [chances_ref[head] for head in range(HEADS)]
    grad_chances = [
        matmul(values[:, at] * marks[head % 2], grad_down[at]) for head, at in enumerate(pairs)
    ]
    grad_values = [matmul(item.astype(BF), grad_mixed[:, at]) for item, at in zip(chances, pairs)]
    held = [jnp.sum(one * two, 0, keepdims=True) for one, two in zip(chances, grad_chances)]
    grad_scores = [
        (one * (two - total)).astype(BF) for one, two, total in zip(chances, grad_chances, held)
    ]
    grad_keys = [matmul(item, query[:, at]) for item, at in zip(grad_scores, pairs)]
    grad_query = [
        matmul(keys_down[head * HEAD_DIM : (head + 1) * HEAD_DIM], item)
        for head, item in enumerate(grad_scores)
    ]
    turned = (jnp.concatenate(grad_query, 0) * FACTOR).astype(BF).T
    return [
        turned,
        (join_pairs(grad_keys) * FACTOR).astype(BF),
        join_pairs(grad_values).astype(BF),
    ]


def tiles_of(array):
    return [array[:, at : at + LANES] for at in range(0, array.shape[1], LANES)]


class Entry:
    def __init__(self, array):
        self.arrays = (array,)
        self.shape, self.dtype = array.shape[1:], array.dtype

    def pieces(self, refs, section):
        return [(None, refs[0].at[section])]


class Either:
    def __init__(self, *pair):
        pair = [item if isinstance(item, tuple) else (item, None) for item in pair]
        self.arrays = tuple(array for array, unused in pair)
        self.entries = [entry for unused, entry in pair]
        first = self.arrays[0]
        self.shape = first.shape if self.entries[0] is None else first.shape[1:]
        self.dtype = first.dtype

    def pieces(self, refs, section):
        return [
            (here, ref if entry is None else ref.at[entry])
            for here, (ref, entry) in enumerate(zip(refs, self.entries))
        ]


class Whole:
    def __init__(self, array):
        self.arrays = (array,)
        self.shape, self.dtype = array.shape, array.dtype

    def pieces(self, refs, section):
        return [(None, refs[0])]


class Room:
    def __init__(self, inputs, sources, held, sems, away):
        self.inputs, self.sources, self.held, self.sems = inputs, sources, held, sems
        self.away, self.left = away, {}
        self.section = lax.axis_index("section")
        self.core = lax.axis_index("rows") & 1
        self.arrived = set()
        for place, name in enumerate(inputs):
            for here, source in inputs[name].pieces(sources[name], self.section):
                copy = pltpu.make_async_copy(source, held[name], sems.at[place])
                if here is None:
                    copy.start()
                else:
                    pl.when(self.section == here)(copy.start)

    def __getattr__(self, name):
        if name in self.inputs and name not in self.arrived:
            self.arrived.add(name)
            place = list(self.inputs).index(name)
            source = self.inputs[name].pieces(self.sources[name], self.section)[0][1]
            pltpu.make_async_copy(source, self.held[name], self.sems.at[place]).wait()
        return self.held[name]

    def leave(self, *names):
        for name, (target, sem) in self.away.items():
            if name in names:
                copy = pltpu.make_async_copy(self.held[name], target, sem)
                copy.start()
                self.left[name] = copy

    def finish(self):
        self.leave(*(name for name in self.away if name not in self.left))
        for name in self.inputs:
            getattr(self, name)
        for copy in self.left.values():
            copy.wait()

    def either(self, here, there):
        return jnp.where(self.section == 0, here[...], there[...])


class Packet:
    def __init__(self, extra=0, **weights):
        self.shapes = {name: array.shape for name, array in weights.items()}
        self.left_at, self.grad_at = {}, {}
        left = grad = 0
        for name, (depth, width) in self.shapes.items():
            self.left_at[name], self.grad_at[name] = left, grad
            left, grad = left + depth // 2, grad + width
        self.left, self.extra_at, self.grad = left, grad, grad + extra

    def leaving(self):
        return [
            pltpu.VMEM((self.left, LANES), BF),
            pltpu.VMEM((self.left + self.grad, LANES), BF),
        ]

    def bind(self, room, refs):
        self.room, (self.keep, self.send) = room, refs

    def stash(self, **operands):
        even = self.room.core == 0
        for name, (left, grad) in operands.items():
            depth, width = self.shapes[name]
            block = depth // GROUPS
            across = left.T
            for group in range(0, GROUPS, 2):
                first = across[group * block : (group + 1) * block]
                second = across[(group + 1) * block : (group + 2) * block]
                top = self.left_at[name] + group // 2 * block
                self.keep[top : top + block] = jnp.where(even, first, second)
                self.send[top : top + block] = jnp.where(even, second, first)
            for place, tile in enumerate(tiles_of(grad)):
                top = self.left + self.grad_at[name] + place * LANES
                self.send[top : top + LANES] = tile


def far_away(array):
    return pltpu.with_memory_space_constraint(array, pltpu.HBM)


def pinned(array):
    return pltpu.with_memory_space_constraint(array, pltpu.VMEM)


def call(body, inputs, near, outputs, loads, span, limit, packet=None, extra=None, away=None, late=None):
    extra, away = extra or {}, away or {}
    inputs = {
        name: item if hasattr(item, "pieces") else Whole(item) for name, item in inputs.items()
    }
    loads = {name: item if hasattr(item, "pieces") else Whole(item) for name, item in loads.items()}
    inputs.update(loads)
    inputs.update({name: item if hasattr(item, "pieces") else Whole(item) for name, item in (late or {}).items()})
    arrays = [array for item in inputs.values() for array in item.arrays]
    outputs = {
        **outputs,
        **{name: jax.ShapeDtypeStruct(item.shape, item.dtype) for name, item in loads.items()},
    }
    shapes_out = [pltpu.VMEM(item.shape, item.dtype) for item in outputs.values()]
    shapes_out += packet.leaving() if packet else []
    shapes_out += [pltpu.HBM(item.shape, item.dtype) for item in away.values()]
    brought = [name for name in inputs if name not in loads]

    def kernel(*refs):
        refs = list(refs)

        def take(count):
            taken = refs[:count]
            del refs[:count]
            return taken

        sources = {name: take(len(item.arrays)) for name, item in inputs.items()}
        held = dict(zip(near, take(len(near))))
        held.update(zip(outputs, take(len(outputs))))
        leaving = take(2) if packet else None
        targets = take(len(away))
        held.update(zip(brought, take(len(brought))))
        held.update(zip(extra, take(len(extra))))
        held.update(zip(away, take(len(away))))
        away_to = {
            name: (target, refs[1].at[place])
            for place, (name, target) in enumerate(zip(away, targets))
        }
        room = Room(inputs, sources, held, refs[0], away_to)
        if packet:
            packet.bind(room, leaving)
        body(room)
        room.finish()

    scratch = [inputs[name] for name in brought] + list(extra.values()) + list(away.values())
    results = pl.pallas_call(
        kernel,
        out_shape=shapes_out,
        in_specs=[HBM] * len(arrays) + [VMEM] * len(near),
        out_specs=[VMEM] * (len(shapes_out) - len(away)) + [HBM] * len(away),
        scratch_shapes=[pltpu.VMEM(item.shape, item.dtype) for item in scratch]
        + [pltpu.SemaphoreType.DMA((max(1, len(inputs)),))]
        + [pltpu.SemaphoreType.DMA((max(1, len(away)),))],
        compiler_params=pltpu.CompilerParams(vmem_limit_bytes=limit << 20),
        cost_estimate=lasting(span),
    )(*(far_away(item) for item in arrays), *(pinned(item) for item in near.values()))
    made = dict(zip(outputs, results))
    made.update(zip(away, results[len(results) - len(away) :]))
    leaving = tuple(results[len(outputs) : len(results) - len(away)])
    return SimpleNamespace(**made), leaving


def place_of(side, block, orders, core):
    spots = []
    for order in orders:
        spot = side * (8 >> order.index(SIDE))
        for bit in range(3):
            spot = spot + (block >> bit & 1) * (8 >> order.index(bit + 1))
        spots.append(spot)
    return jnp.where(core == 0, spots[0], spots[1])


def bit_of(step, section, row):
    return section if step == SIDE else (row >> step) & 1


def weight_grads(parcels, names, orders, even, small=False):
    parts = [
        (packet, which, name)
        for which, (packet, *unused) in enumerate(parcels)
        for name in packet.shapes
        if name in names
    ]
    height = sum(
        packet.shapes[name][0] // GROUPS * packet.shapes[name][1] // (2 * SLAB)
        for packet, unused, name in parts
    )
    small_at = height
    height += 16 if small else 0
    half = pltpu.VMEM((GROUPS // 2, height, SLAB), BF)

    def kernel(*refs):
        *operands, kept_out, sent_out, packed = refs
        row = lax.axis_index("rows")
        core = row & 1
        if even:
            first = [bit_of(order[0], lax.axis_index("section"), row) for order in orders]
            mine = jnp.where(core == 0, first[0], first[1])
        else:
            mine = 0

        base = 0
        for packet, which, name in parts:
            keep_ref, send_ref, came_ref = operands[3 * which : 3 * which + 3]
            depth, width = packet.shapes[name]
            block, half_pieces = depth // GROUPS, width // (2 * SLAB)
            left_at, grad_at = packet.left_at[name], packet.left + packet.grad_at[name]
            left = jnp.concatenate(
                [ref[left_at : left_at + depth // 2] for ref in (keep_ref, came_ref)], 1
            )
            for piece in range(width // SLAB):
                at = grad_at + piece * SLAB
                right = jnp.concatenate(
                    [
                        jnp.concatenate([ref[at : at + LANES], ref[at + LANES : at + 2 * LANES]], 1)
                        for ref in (send_ref, came_ref)
                    ],
                    0,
                )
                tile = matmul(left, right).astype(BF)
                side, offset = divmod(piece, half_pieces)
                top = base + offset * block
                for number in range(GROUPS // 2):
                    packed[place_of(side, number, orders, core), top : top + block] = tile[
                        number * block : (number + 1) * block
                    ]
            base += block * half_pieces
        if small:
            packet = parcels[0][0]
            at = packet.left + packet.extra_at
            total = sum(
                jnp.concatenate([ref[at + 16 * i : at + 16 * i + 16] for i in range(4)], 1).astype(F32)
                for ref in operands[1:3]
            )
            width = total.shape[1]
            share = width // GROUPS
            for number in range(GROUPS // 2):
                turned = [
                    pltpu.roll(total, (width - (2 * number + i) * share) % width, 1) for i in (0, 1)
                ]
                part = jnp.where(core == 0, turned[0], turned[1])[:, :SLAB].astype(BF)
                for side in (0, 1):
                    packed[place_of(side, number, orders, core), small_at : small_at + 16] = part
        count = GROUPS // 2
        sent_out[...] = packed[pl.ds((1 - mine) * count, count)]
        kept_out[...] = packed[pl.ds(mine * count, count)]

    arrays = [array for unused, *rest in parcels for array in rest]
    return pl.pallas_call(
        kernel,
        out_shape=[half, half],
        in_specs=[VMEM] * len(arrays),
        out_specs=[VMEM] * 2,
        scratch_shapes=[pltpu.VMEM((GROUPS, height, SLAB), BF)],
        compiler_params=pltpu.CompilerParams(vmem_limit_bytes=8 << 20),
        cost_estimate=lasting(3.5),
    )(*(pinned(item) for item in arrays))


def equal_ids(row_ids, column_ids):
    length = row_ids.shape[1]
    down = jnp.broadcast_to(row_ids.astype(F32), (length, length)).T
    return down == jnp.broadcast_to(column_ids.astype(F32), (length, length))


def scale_out(scale):
    return jnp.broadcast_to(scale, (scale.shape[0], LANES))


def thirds(projected):
    width = projected.shape[1] // 3
    return [projected[:, i * width : (i + 1) * width] for i in range(3)]


def self_part(room, tokens, ids, causal, inward, outward, gain, shift):
    room.projected[...] = matmul(tokens, inward[...]).astype(BF)
    room.leave("projected")
    length = tokens.shape[0]
    rows = lax.broadcasted_iota(jnp.int32, (length, length), 0)
    columns = lax.broadcasted_iota(jnp.int32, (length, length), 1)
    reach = jnp.where(causal, 0, length)
    allowed = equal_ids(ids, ids) & (columns + reach >= rows)
    mixed = attend(*thirds(room.projected), allowed, room.chances)
    room.mixed[...] = mixed
    room.leave("chances", "mixed")
    summed = tokens.astype(F32) + matmul(mixed, outward[...])
    first, unit, scale = norm(summed, gain, shift)
    room.unit[...] = unit
    room.scale[...] = scale_out(scale)
    return first


def own_body(room):
    section = room.section
    ids = room.segments[pl.ds(section, 1), pl.ds(section, 1), 0, :][0]
    gain = jnp.where(section == 0, room.encoder_gain[0:1], room.decoder_gain[0:1])
    shift = jnp.where(section == 0, room.encoder_shift[0:1], room.decoder_shift[0:1])
    room.first[...] = self_part(
        room, room.tokens[...], ids, section == 1, room.inward, room.outward, gain, shift
    )


def forward_body(room, packet):
    section = room.section
    source_ids = room.segments[0, pl.ds(section, 1), 0, :]
    target_ids = room.segments[1, pl.ds(section, 1), 0, :]
    ids = jnp.where(section == 0, target_ids, source_ids)
    gain = jnp.where(section == 0, room.decoder_gain[0:1], room.encoder_gain[0:1])
    shift = jnp.where(section == 0, room.decoder_shift[0:1], room.encoder_shift[0:1])
    other = self_part(
        room, room.tokens[...], ids, section == 0, room.inward, room.outward, gain, shift
    )
    own = room.own_first[...]

    first = jnp.where(section == 0, own, other)
    low = first.astype(BF)
    widen_forward(low, room.encoder_widen, room.e_hidden, room.e_slope)
    room.e_low[...] = low
    summed = first + matmul(room.e_hidden[...], room.encoder_narrow[...])
    result, unit, scale = norm(summed, room.encoder_gain[1:2], room.encoder_shift[1:2])
    memory = result.astype(BF)
    room.e_unit1[...] = unit
    room.e_scale1[...] = scale_out(scale)
    room.memory[...] = memory

    first = jnp.where(section == 0, other, own)
    low = first.astype(BF)
    query = matmul(low, room.decoder_cross_query[...]).astype(BF)
    paired = matmul(memory, room.decoder_cross_memory[...]).astype(BF)
    room.d_low[...] = low
    room.c_query[...] = query
    room.c_paired[...] = paired
    width = query.shape[1]
    mixed = attend(
        query,
        room.c_paired[:, :width],
        room.c_paired[:, width:],
        equal_ids(source_ids, target_ids),
        room.c_chances,
    )
    room.c_mixed[...] = mixed
    summed = first + matmul(mixed, room.decoder_cross_outward[...])
    second, unit, scale = norm(summed, room.decoder_gain[1:2], room.decoder_shift[1:2])
    room.d_unit1[...] = unit
    room.d_scale1[...] = scale_out(scale)

    low = second.astype(BF)
    widen_forward(low, room.decoder_widen, room.d_hidden, room.d_slope)
    summed = second + matmul(room.d_hidden[...], room.decoder_narrow[...])
    gain = room.decoder_gain[2:3]
    result, unit, scale = norm(summed, gain, room.decoder_shift[2:3])
    room.output[...] = result.astype(BF)

    grad_sum, grad_gain, grad_shift = norm_back(
        room.cotangent[...].astype(F32), unit, scale, gain
    )
    grad_low = grad_sum.astype(BF)
    grad_before = widen_backward(grad_low, room.decoder_narrow, room.d_slope)
    packet.stash(
        decoder_narrow=(room.d_hidden[...], grad_low), decoder_widen=(low, grad_before)
    )
    room.d_sum[...] = grad_sum
    room.d_before[...] = grad_before
    room.d_small2[...] = jnp.concatenate([grad_gain, grad_shift], 0)


def widen_forward(low, widen_ref, hidden_ref, slope_ref):
    step = 512
    for at in range(0, widen_ref.shape[1], step):
        hidden, slope = gelu_both(matmul(low, widen_ref[:, at : at + step]))
        hidden_ref[:, at : at + step] = hidden.astype(BF)
        slope_ref[:, at : at + step] = slope


def widen_backward(grad_low, narrow_ref, slope_ref):
    step = 512
    parts = []
    for at in range(0, narrow_ref.shape[0], step):
        grad_hidden = matmul_back(grad_low, narrow_ref[at : at + step])
        parts.append((grad_hidden * slope_ref[:, at : at + step]).astype(BF))
    return jnp.concatenate(parts, 1)


def cross_back_body(room, packet):
    grad_normed = room.d_sum[...] + matmul_back(room.d_before[...], room.decoder_widen[...])
    grad_sum, gain1, shift1 = norm_back(
        grad_normed, room.d_unit1[...], room.d_scale1[:, :1], room.decoder_gain[1:2]
    )
    grad_low = grad_sum.astype(BF)
    grad_mixed = matmul_back(grad_low, room.decoder_cross_outward[...]).astype(BF)
    paired = room.c_paired
    query = room.c_query[...]
    width = query.shape[1]
    grad_query, grad_keys, grad_values = attend_back(
        query, paired[:, :width], paired[:, width:], room.c_chances, grad_mixed
    )
    grad_paired = jnp.concatenate([grad_keys, grad_values], 1)
    packet.stash(
        decoder_cross_query=(room.d_low[...], grad_query),
        decoder_cross_memory=(room.memory[...], grad_paired),
        decoder_cross_outward=(room.c_mixed[...], grad_low),
    )
    room.d_sum1[...] = grad_sum
    room.c_grad_query[...] = grad_query
    room.c_grad_paired[...] = grad_paired
    room.d_small1[...] = jnp.concatenate([gain1, shift1], 0)


def self_back(grad_sum, inward, outward, tokens, projected, chances, mixed):
    grad_low = grad_sum.astype(BF)
    grad_mixed = matmul_back(grad_low, outward[...]).astype(BF)
    grad_projected = jnp.concatenate(attend_back(*thirds(projected), chances, grad_mixed), 1)
    pairs = ((tokens, grad_projected), (mixed, grad_low))
    return pairs, grad_sum + matmul_back(grad_projected, inward[...])


def decoder_self_body(room, packet):
    either = room.either
    grad_query, grad_paired = room.c_grad_query[...], room.c_grad_paired[...]
    room.grad_memory[...] = matmul_back(grad_paired, room.decoder_cross_memory[...]).astype(BF)
    grad_normed = room.d_sum1[...] + matmul_back(grad_query, room.decoder_cross_query[...])
    grad_sum, gain0, shift0 = norm_back(
        grad_normed,
        either(room.far_unit, room.near_unit),
        either(room.far_scale, room.near_scale)[:, :1],
        room.decoder_gain[0:1],
    )
    room.d_small0[...] = jnp.concatenate([gain0, shift0], 0)
    (inward, outward), grad_inputs = self_back(
        grad_sum,
        room.decoder_inward,
        room.decoder_outward,
        either(room.far_tokens, room.near_tokens),
        either(room.far_projected, room.near_projected),
        either(room.far_chances, room.near_chances),
        either(room.far_mixed, room.near_mixed),
    )
    packet.stash(decoder_inward=inward, decoder_outward=outward)
    room.d_inputs[...] = grad_inputs.astype(BF)


def encoder_back_body(room, packet):
    gain = room.encoder_gain
    grad_sum, gain1, shift1 = norm_back(
        room.grad_memory[...].astype(F32), room.e_unit1[...], room.e_scale1[:, :1], gain[1:2]
    )
    grad_low = grad_sum.astype(BF)
    grad_before = widen_backward(grad_low, room.encoder_narrow, room.e_slope)
    packet.stash(
        encoder_narrow=(room.e_hidden[...], grad_low), encoder_widen=(room.e_low[...], grad_before)
    )
    grad_normed = grad_sum + matmul_back(grad_before, room.encoder_widen[...])
    either = room.either
    grad_sum, gain0, shift0 = norm_back(
        grad_normed,
        either(room.near_unit, room.far_unit),
        either(room.near_scale, room.far_scale)[:, :1],
        gain[0:1],
    )
    smalls = [room.d_small0[...], room.d_small1[...], room.d_small2[...]]
    small = jnp.concatenate(
        [gain0, gain1, shift0, shift1]
        + [item[0:1] for item in smalls]
        + [item[1:2] for item in smalls]
        + [jnp.zeros((6, gain0.shape[1]), F32)],
        0,
    )
    for place, tile in enumerate(tiles_of(small.astype(BF))):
        top = packet.left + packet.extra_at + 16 * place
        packet.send[top : top + 16] = tile
    (inward, outward), grad_inputs = self_back(
        grad_sum,
        room.encoder_inward,
        room.encoder_outward,
        either(room.near_tokens, room.far_tokens),
        either(room.near_projected, room.far_projected),
        either(room.near_chances, room.far_chances),
        either(room.near_mixed, room.far_mixed),
    )
    packet.stash(encoder_inward=inward, encoder_outward=outward)
    here, there = grad_inputs.astype(BF), room.d_inputs[...]
    room.sides_mine[0] = either(room.memory, room.output)
    room.sides_mine[1] = jnp.where(room.section == 0, here, there)
    room.sides_theirs[0] = either(room.output, room.memory)
    room.sides_theirs[1] = jnp.where(room.section == 0, there, here)


class Line:
    def __init__(self):
        self.last = None

    def after(self, *values):
        if self.last is None:
            return values
        return lax.optimization_barrier((values, self.last))[0]

    def mark(self, value):
        self.last = value


def pair_swap(value, axis, apart):
    count = lax.axis_size(axis)
    return lax.ppermute(value, axis, [(i, i ^ apart) for i in range(count)])


def halve(kept, came, following, span):
    count, height = kept.shape[0] // 2, kept.shape[1]
    half = pltpu.VMEM((count, height, SLAB), BF)

    def kernel(kept_ref, came_ref, kept_out, sent_out):
        section, row = lax.axis_index("section"), lax.axis_index("rows")
        bits = [bit_of(step, section, row) for step in following]
        mine = jnp.where(row & 1 == 0, bits[0], bits[1])
        for which, out in ((1 - mine, sent_out), (mine, kept_out)):
            part = pl.ds(which * count, count)
            out[...] = (kept_ref[part].astype(F32) + came_ref[part].astype(F32)).astype(BF)

    return pl.pallas_call(
        kernel,
        out_shape=[half, half],
        in_specs=[VMEM] * 2,
        out_specs=[VMEM] * 2,
        compiler_params=pltpu.CompilerParams(vmem_limit_bytes=2 << 20),
        cost_estimate=lasting(span),
    )(pinned(kept), pinned(came))


class Team:
    def __init__(self, line, orders, small=False, **weights):
        self.line, self.small = line, small
        self.shapes = {name: array.shape for name, array in weights.items()}
        self.even = lax.axis_size("rows") == GROUPS
        self.orders = orders if self.even else (XYZ, XYZ)
        self.turn = 0
        self.done = {}

    def grads(self, *parcels):
        tied = self.line.after(*(parts for unused, parts in parcels))
        parcels = [(packet, *parts) for (packet, unused), parts in zip(parcels, tied)]
        self.kept, self.sent = weight_grads(
            parcels, list(self.shapes), self.orders, self.even, self.small
        )
        self.line.mark(self.sent)
        if self.even:
            self.go()

    def go(self):
        pieces = lax.axis_size("rows")
        route = []
        for device in range(2 * pieces):
            step = self.orders[device & 1][self.turn]
            route.append((device, device ^ (pieces if step == SIDE else 1 << step)))
        self.came = lax.ppermute(self.sent, ("section", "rows"), route)

    def step(self, span=2):
        if not self.even:
            return
        self.turn += 1
        kept, came = self.line.after(self.kept, self.came)
        following = [order[self.turn] for order in self.orders]
        self.kept, self.sent = halve(kept, came, following, span)
        self.line.mark(self.sent)
        self.go()

    def end(self):
        pieces = lax.axis_size("rows")
        if not self.even:
            return self.end_uneven()
        kept, came = self.line.after(self.kept, self.came)
        shapes = list(self.shapes.values())
        outs = [jax.ShapeDtypeStruct((depth // pieces, width // 2), F32) for depth, width in shapes]
        counts = (2, 2, 3, 3) if self.small else ()
        lanes = 512 // pieces
        outs += [jax.ShapeDtypeStruct((count, lanes), F32) for count in counts]

        def kernel(kept_ref, came_ref, *out_refs):
            top = 0
            for (depth, width), out_ref in zip(shapes, out_refs):
                share = depth // pieces
                for at in range(0, width // 2, SLAB):
                    rows = slice(top, top + share)
                    out_ref[:, at : at + SLAB] = kept_ref[0, rows].astype(F32) + came_ref[
                        0, rows
                    ].astype(F32)
                    top += share
            if counts:
                rows = slice(top, top + 16)
                total = kept_ref[0, rows].astype(F32) + came_ref[0, rows].astype(F32)
                top = 0
                for count, out_ref in zip(counts, out_refs[len(shapes) :]):
                    out_ref[...] = total[top : top + count, :lanes]
                    top += count

        results = pl.pallas_call(
            kernel,
            out_shape=outs,
            in_specs=[VMEM] * 2,
            out_specs=[VMEM] * len(outs),
            compiler_params=pltpu.CompilerParams(vmem_limit_bytes=2 << 20),
            cost_estimate=lasting(1.6),
        )(pinned(kept), pinned(came))
        self.line.mark(results[0])
        self.done = dict(zip(self.shapes, results))
        self.shares = results[len(shapes) :]

    def spread(self, top, count, share):
        core = lax.axis_index("rows") & 1
        both = jnp.stack([self.kept, self.sent])[:, :, top : top + count * share].astype(F32)
        both = both.reshape(2, 2, 2, 2, count, share, SLAB)
        both = both.transpose(0, 3, 2, 1, 5, 4, 6)
        both = both.reshape(2, GROUPS // 2, 1, share, count * SLAB)
        held = jnp.concatenate([both * (core == 0), both * (core == 1)], 2)
        return held.reshape(2, GROUPS, share, count * SLAB)

    def end_uneven(self):
        pieces = lax.axis_size("rows")
        top = 0
        for name, (depth, width) in self.shapes.items():
            share, count = depth // GROUPS, width // (2 * SLAB)
            part = self.spread(top, count, share).reshape(2, depth, width // 2)
            part = lax.psum_scatter(part, "rows", scatter_dimension=1, tiled=True)
            self.done[name] = lax.psum_scatter(part, "section", scatter_dimension=0, tiled=True)[0]
            top += count * share
        if self.small:
            width = 512
            part = self.spread(top, 1, 16)[0, :, :10, : width // GROUPS]
            part = lax.psum(jnp.moveaxis(part, 1, 0).reshape(10, width), ("section", "rows"))
            start = lax.axis_index("rows") * (width // pieces)
            part = lax.dynamic_slice_in_dim(part, start, width // pieces, 1)
            self.shares = (part[0:2], part[2:4], part[4:7], part[7:10])


SIDE = 0
XYZ, YXZ = (SIDE, 1, 2, 3), (1, SIDE, 2, 3)
XZY, YZX = (SIDE, 2, 3, 1), (1, 2, 3, SIDE)
ZXY, ZYX = (2, 3, SIDE, 1), (2, 3, 1, SIDE)


def per_device(
    section_input,
    segments,
    cotangent,
    encoder_inward,
    encoder_outward,
    encoder_widen,
    encoder_narrow,
    encoder_gain,
    encoder_shift,
    decoder_inward,
    decoder_outward,
    decoder_cross_query,
    decoder_cross_memory,
    decoder_cross_outward,
    decoder_widen,
    decoder_narrow,
    decoder_gain,
    decoder_shift,
):
    section = lax.axis_index("section")
    own = section_input[0]
    length, width = own.shape[1:]
    wide = encoder_widen.shape[1]

    def low(*shape):
        return jax.ShapeDtypeStruct(shape, BF)

    def full(*shape):
        return jax.ShapeDtypeStruct(shape, F32)

    slabs, units, scales = low(length, width), full(length, width), full(length, LANES)
    chances = full(HEADS, length, length)
    attended = dict(
        projected=low(length, 3 * width), chances=chances, mixed=slabs, unit=units, scale=scales
    )
    line = Line()

    def run(body, inputs, near, outputs, loads, span, limit, packet=None, extra=None, away=None, late=None):
        near = dict(near)
        for name in list(near)[:1]:
            (near[name],) = line.after(near[name])
        kept, leaving = call(
            body if packet is None else (lambda room: body(room, packet)),
            inputs,
            near,
            outputs,
            loads,
            span,
            limit,
            packet,
            extra,
            away,
            late,
        )
        line.mark(list(vars(kept).values())[0])
        if packet is None:
            return kept
        return kept, leaving + (pair_swap(leaving[1], "rows", 1),)

    other = pair_swap(
        lax.dynamic_index_in_dim(own, 1 - section, 0, keepdims=False), "section", 1
    )
    near = run(
        own_body,
        dict(
            segments=segments,
            tokens=Entry(own),
            inward=Either(encoder_inward, decoder_inward),
            encoder_gain=encoder_gain,
            encoder_shift=encoder_shift,
            decoder_gain=decoder_gain,
            decoder_shift=decoder_shift,
            outward=Either(encoder_outward, decoder_outward),
        ),
        {},
        {},
        dict(
            other_inward=Either(decoder_inward, encoder_inward),
            other_outward=Either(decoder_outward, encoder_outward),
        ),
        4,
        6,
        away=dict(first=units, **attended),
    )

    wide_packet = Packet(decoder_narrow=decoder_narrow, decoder_widen=decoder_widen)
    far, d_wide = run(
        forward_body,
        dict(
            segments=segments,
            encoder_shift=encoder_shift,
            decoder_shift=decoder_shift,
            own_first=near.first,
        ),
        dict(
            tokens=other,
            inward=near.other_inward,
            outward=near.other_outward,
        ),
        dict(
            memory=slabs,
            output=slabs,
            **attended,
            e_low=slabs,
            e_hidden=low(length, wide),
            e_slope=full(length, wide),
            e_unit1=units,
            e_scale1=scales,
            d_low=slabs,
            c_query=slabs,
            c_paired=low(length, 2 * width),
            c_chances=chances,
            c_mixed=slabs,
            d_unit1=units,
            d_scale1=scales,
            d_sum=units,
            d_before=low(length, wide),
            d_small2=full(2, width),
        ),
        dict(
            encoder_gain=encoder_gain,
            decoder_gain=decoder_gain,
            encoder_widen=encoder_widen,
            encoder_narrow=encoder_narrow,
            decoder_cross_query=decoder_cross_query,
            decoder_cross_memory=decoder_cross_memory,
            decoder_cross_outward=decoder_cross_outward,
            decoder_widen=decoder_widen,
        ),
        11,
        14,
        wide_packet,
        dict(d_hidden=low(length, wide), d_slope=full(length, wide)),
        late=dict(decoder_narrow=decoder_narrow, cotangent=Entry(cotangent)),
    )

    cross_packet = Packet(
        decoder_cross_query=decoder_cross_query,
        decoder_cross_memory=decoder_cross_memory,
        decoder_cross_outward=decoder_cross_outward,
    )
    crossed, d_cross = run(
        cross_back_body,
        {},
        dict(
            d_sum=far.d_sum,
            d_before=far.d_before,
            decoder_widen=far.decoder_widen,
            decoder_gain=far.decoder_gain,
            d_unit1=far.d_unit1,
            d_scale1=far.d_scale1,
            c_query=far.c_query,
            c_paired=far.c_paired,
            c_chances=far.c_chances,
            d_low=far.d_low,
            memory=far.memory,
            c_mixed=far.c_mixed,
            decoder_cross_outward=far.decoder_cross_outward,
        ),
        dict(
            d_sum1=units,
            c_grad_query=slabs,
            c_grad_paired=low(length, 2 * width),
            d_small1=full(2, width),
        ),
        {},
        4.7,
        5,
        cross_packet,
    )

    def d_self_run():
        packet = Packet(decoder_inward=decoder_inward, decoder_outward=decoder_outward)
        return packet, *run(
            decoder_self_body,
            dict(
                near_unit=near.unit,
                near_scale=near.scale,
                decoder_outward=decoder_outward,
                near_projected=near.projected,
                near_chances=near.chances,
                near_tokens=Entry(own),
                near_mixed=near.mixed,
                decoder_inward=decoder_inward,
            ),
            dict(
                far_tokens=other,
                c_grad_query=crossed.c_grad_query,
                c_grad_paired=crossed.c_grad_paired,
                d_sum1=crossed.d_sum1,
                decoder_cross_memory=far.decoder_cross_memory,
                decoder_cross_query=far.decoder_cross_query,
                decoder_gain=far.decoder_gain,
                far_unit=far.unit,
                far_scale=far.scale,
                far_projected=far.projected,
                far_chances=far.chances,
                far_mixed=far.mixed,
            ),
            dict(d_inputs=slabs, grad_memory=slabs, d_small0=full(2, width)),
            {},
            5,
            5,
            packet,
        )

    def encoder_run(turned):
        packet = Packet(
            64,
            encoder_narrow=encoder_narrow,
            encoder_widen=encoder_widen,
            encoder_inward=encoder_inward,
            encoder_outward=encoder_outward,
        )
        sides = low(2, length, width)
        return packet, *run(
            encoder_back_body,
            dict(
                near_unit=near.unit,
                near_scale=near.scale,
                near_projected=near.projected,
                near_chances=near.chances,
                near_tokens=Entry(own),
                near_mixed=near.mixed,
                encoder_outward=encoder_outward,
                encoder_inward=encoder_inward,
            ),
            dict(
                far_tokens=other,
                encoder_gain=far.encoder_gain,
                grad_memory=turned.grad_memory,
                e_unit1=far.e_unit1,
                e_scale1=far.e_scale1,
                encoder_narrow=far.encoder_narrow,
                e_slope=far.e_slope,
                e_hidden=far.e_hidden,
                e_low=far.e_low,
                encoder_widen=far.encoder_widen,
                d_small0=turned.d_small0,
                d_small1=crossed.d_small1,
                d_small2=far.d_small2,
                far_unit=far.unit,
                far_scale=far.scale,
                far_projected=far.projected,
                far_chances=far.chances,
                far_mixed=far.mixed,
                d_inputs=turned.d_inputs,
                memory=far.memory,
                output=far.output,
            ),
            dict(sides_mine=sides, sides_theirs=sides),
            {},
            8,
            8,
            packet,
        )

    team_w = Team(
        line,
        (XYZ, YZX),
        False,
        decoder_narrow=decoder_narrow,
        decoder_widen=decoder_widen,
    )
    team_q = Team(
        line,
        (ZYX, ZYX),
        False,
        decoder_cross_query=decoder_cross_query,
        decoder_cross_memory=decoder_cross_memory,
        decoder_cross_outward=decoder_cross_outward,
    )
    team_r = Team(
        line,
        (XZY, YZX),
        False,
        decoder_inward=decoder_inward,
        decoder_outward=decoder_outward,
    )
    team_e = Team(
        line,
        (YZX, XYZ),
        False,
        encoder_narrow=encoder_narrow,
    )
    team_f = Team(
        line,
        (XZY, XYZ),
        False,
        encoder_widen=encoder_widen,
    )
    team_s = Team(
        line,
        (XYZ, YXZ),
        True,
        encoder_inward=encoder_inward,
        encoder_outward=encoder_outward,
    )
    team_w.grads((wide_packet, d_wide))
    team_q.grads((cross_packet, d_cross))
    self_packet, turned, d_self = d_self_run()
    encoder_packet, ended, e_all = encoder_run(turned)
    team_r.grads((self_packet, d_self))
    team_w.step()
    team_q.step()
    team_e.grads((encoder_packet, e_all))
    team_f.grads((encoder_packet, e_all))
    team_r.step()
    team_w.step()
    team_s.grads((encoder_packet, e_all))
    team_q.step()
    team_e.step()
    team_r.step()
    team_f.step()
    team_q.step()
    team_w.step()
    team_e.step()
    team_r.step()
    team_s.step()
    team_f.step()
    team_w.end()
    (theirs,) = line.after(ended.sides_theirs)
    theirs = pair_swap(theirs, "section", 1)
    team_r.end()
    team_s.step()
    team_e.step()
    team_f.step()
    team_s.step()
    mine, theirs = line.after(ended.sides_mine, theirs)
    results, gradients = (
        jnp.stack(
            [
                jnp.where(section == 0, mine[i], theirs[i]),
                jnp.where(section == 0, theirs[i], mine[i]),
            ]
        )[None]
        for i in (0, 1)
    )
    line.mark(gradients)
    team_q.end()
    team_f.end()
    team_e.end()
    team_s.end()

    done = {}
    for team in (team_w, team_q, team_r, team_e, team_f, team_s):
        done.update(team.done)
    deltas = SimpleNamespace(**done)
    shares = team_s.shares
    return (
        results,
        gradients,
        deltas.encoder_inward,
        deltas.encoder_outward,
        deltas.encoder_widen,
        deltas.encoder_narrow,
        shares[0],
        shares[1],
        deltas.decoder_inward,
        deltas.decoder_outward,
        deltas.decoder_cross_query,
        deltas.decoder_cross_memory,
        deltas.decoder_cross_outward,
        deltas.decoder_widen,
        deltas.decoder_narrow,
        shares[2],
        shares[3],
    )


def solution(mesh):
    weights = (P(),) * 15
    shares = P("rows", "section")
    small = P(None, "rows")
    sides = P("section", None, "rows", None)
    return jax.shard_map(
        per_device,
        mesh=mesh,
        in_specs=(sides, P(None, None, "rows", None), P(None, "rows", None)) + weights,
        out_specs=(sides, sides)
        + (shares,) * 4
        + (small,) * 2
        + (shares,) * 7
        + (small,) * 2,
        check_vma=False,
    )
```
